32 devices in a mesh: groups: 2 (over y), atoms: 4 (over z), states: 2 (over x), sub: 2 (over core).
Axes of the slice: x: 2, y: 2, z: 4, core: 2. Of those that a mesh axis runs over, the one named last changes fastest.
Arguments:
- coeffs: float32 [16384, 2048], P(('groups', 'atoms', 'sub'), 'states'), parts along dimension 0, may hold values from -0.15 to 0.15
- occup: float32 [4096], P(('groups', 'states')), parts along dimension 0, may hold values from 0.1 to 2
- energies: float32 [4096], P(('groups', 'states')), parts along dimension 0, may hold values from -1.5 to 0.5
- nbr: int32 [16, 4096], P(None, ('groups', 'atoms', 'sub')), parts along dimension 1, may hold values from -1 to 2047, as said below
- dham: float32 [48, 16, 4096], P(None, None, ('groups', 'atoms', 'sub')), parts along dimension 2, may hold values from -6 to 6
- dovl: float32 [48, 16, 4096], P(None, None, ('groups', 'atoms', 'sub')), parts along dimension 2, may hold values from -6 to 6
Outputs:
- forces: float32 [3, 4096], P(None, ('groups', 'atoms', 'sub')), parts along dimension 1
The draws below stay inside these ranges and needn't reach their ends.
There are 2 independent parts, one for each index of `groups`. The reference program is written for one: setup_inputs(seed, part) draws one part's arguments, and reference() takes and returns one part's arrays. A program takes and returns all parts, laid end to end along the dimension named above; each array names one. Nothing has to cross between parts.
Inputs may be any that keep to these rules, and one draw needn't show every extreme that they name: Each live nbr[n, i] lies in i+1 .. i+128, and the live entries of an atom are distinct. Each atom has from half of 16 to 16 live slots, which come first; near the end of the slab a target past the last atom is dropped to -1 in whatever slot it stands, which can leave -1 between live slots. Atom 0 has all 16 slots live and its neighbour i+128.
All inputs are finite; a program needn't handle non-finite values.
Results may differ from the reference program's by a relative error of at most 0.0001.
Values sent between devices are 32-bit elements; how exact they have to be, the bound alone decides.
No kernel may reach another device: no remote copies, remote signals or barrier semaphores. Data moves between devices by JAX's collectives and lax.ppermute only.
A program may use at most 64 MiB of HBM per device.

```python
import jax
import jax.numpy as jnp
from jax import lax

NS = 2048
NB = 16
AT_DEV = 256
HALO = 128
ATOMS = 2048
ORBS = 8192


def draw_nbr(key, part):
    key = jax.random.fold_in(key, 11)
    key_order, key_count = jax.random.split(key)
    scores = jax.random.randint(key_order, (ATOMS, HALO), 0, 1 << 20)
    scores = scores * HALO + jnp.arange(HALO, dtype=jnp.int32)[None, :]
    unused, chosen = lax.top_k(scores, NB)
    offsets = chosen.astype(jnp.int32) + 1
    offsets = offsets.at[0].set(HALO - jnp.arange(NB, dtype=jnp.int32))
    counts = jax.random.randint(key_count, (ATOMS,), NB // 2, NB + 1)
    counts = counts.at[0].set(NB)
    slots = jnp.arange(NB, dtype=jnp.int32)
    targets = jnp.arange(ATOMS, dtype=jnp.int32)[:, None] + offsets
    alive = (slots[None, :] < counts[:, None]) & (targets < ATOMS)
    return jnp.where(alive, targets, -1).astype(jnp.int32).T


def block_scale(own_key, extent, pieces, smallest, high):
    factor_of, own = 1.0, jax.random.fold_in(own_key, 6)
    for axis_at, parts in pieces:
        steps = jnp.exp(jax.random.uniform(jax.random.fold_in(own, axis_at), (parts,), jnp.float32, smallest / len(pieces), high / len(pieces)))
        factor_of = factor_of * jnp.repeat(steps, extent[axis_at] // parts).reshape([-1 if axis == axis_at else 1 for axis in range(len(extent))])
    return factor_of


def bell_draw(own_key, extent, scale, most, cuts=(), kind=jnp.bfloat16):
    gain = block_scale(own_key, extent, cuts, -0.22, 0.18) if cuts else 1.0
    entries = jax.random.normal(own_key, extent, jnp.float32) * scale * gain
    return jnp.minimum(jnp.maximum(entries, -most), most).astype(kind)


def setup_inputs(seed: int = 0, part: int = 0) -> dict:
    key_of = jax.random.split(jax.random.key(seed), 7)
    own_keys = jax.random.split(jax.random.fold_in(key_of[6], part), 7)
    return {
        "coeffs": bell_draw(own_keys[0], (ORBS, NS), 0.025, 0.15, ((0, 8), (1, 2)), jnp.float32),
        "occup": jnp.clip(0.1 + 1.9 * jax.random.uniform(own_keys[1], (NS,), jnp.float32) ** block_scale(own_keys[1], (NS,), ((0, 2),), -0.2, 0.2), 0.1, 2.0),
        "energies": jnp.clip(-1.5 + 2.0 * jax.random.uniform(own_keys[2], (NS,), jnp.float32) ** block_scale(own_keys[2], (NS,), ((0, 2),), -0.2, 0.2), -1.5, 0.5),
        "nbr": draw_nbr(jax.random.fold_in(jax.random.fold_in(key_of[6], part), 71), part),
        "dham": bell_draw(own_keys[4], (48, NB, ATOMS), 1.0, 6.0, ((2, 8),), jnp.float32),
        "dovl": bell_draw(own_keys[5], (48, NB, ATOMS), 1.0, 6.0, ((2, 8),), jnp.float32),
    }


def pair_forces(window, weights, deriv_h, deriv_s, neighbours, window_start, atom_count, block_atoms, halo_atoms):
    states_local = window.shape[1]
    accum = jnp.zeros((3, atom_count + halo_atoms), jnp.float32)
    span = block_atoms + halo_atoms

    def step(block_index, accum):
        first_atom = block_index * block_atoms
        own_rows = lax.dynamic_slice_in_dim(window, first_atom * 4, block_atoms * 4, 0)
        near_rows = lax.dynamic_slice_in_dim(window, first_atom * 4, span * 4, 0)
        near_rows = near_rows.reshape(span, 4, states_local).transpose(1, 0, 2).reshape(4 * span, states_local)
        scaled = own_rows[None] * weights[:, None, :]
        gram_blocks = jnp.einsum('xrs,cs->xrc', scaled, near_rows, precision=lax.Precision.HIGHEST)
        gram_blocks = gram_blocks.reshape(2, block_atoms, 4, 4, span)
        listed = lax.dynamic_slice_in_dim(neighbours, first_atom, block_atoms, 1)
        alive = listed >= 0
        relative = jnp.where(alive, listed - window_start - first_atom, 0).astype(jnp.int32)
        onehot = ((relative[:, :, None] == jnp.arange(span, dtype=jnp.int32)[None, None, :]) & alive[:, :, None]).astype(jnp.float32)
        picked = jnp.einsum('xiabj,nij->xabni', gram_blocks, onehot, precision=lax.Precision.HIGHEST)
        block_h = lax.dynamic_slice_in_dim(deriv_h, first_atom, block_atoms, 4)
        block_s = lax.dynamic_slice_in_dim(deriv_s, first_atom, block_atoms, 4)
        pair_terms = jnp.einsum('abni,kabni->kni', picked[0], block_h, precision=lax.Precision.HIGHEST)
        pair_terms = pair_terms - jnp.einsum('abni,kabni->kni', picked[1], block_s, precision=lax.Precision.HIGHEST)
        pair_terms = jnp.where(alive[None], pair_terms, 0.0)
        self_part = -2.0 * jnp.sum(pair_terms, axis=1)
        spread_terms = 2.0 * jnp.einsum('kni,nij->kj', pair_terms, onehot, precision=lax.Precision.HIGHEST)
        window_part = lax.dynamic_slice_in_dim(accum, first_atom, span, 1) + spread_terms
        window_part = window_part.at[:, :block_atoms].add(self_part)
        return lax.dynamic_update_slice_in_dim(accum, window_part, first_atom, 1)

    return lax.fori_loop(0, atom_count // block_atoms, step, accum)


def reference(coeffs, occup, energies, nbr, dham, dovl):
    weights = jnp.stack([occup, occup * energies])
    window = jnp.pad(coeffs, ((0, 4 * HALO), (0, 0)))
    deriv_h = dham.reshape(3, 4, 4, NB, ATOMS)
    deriv_s = dovl.reshape(3, 4, 4, NB, ATOMS)
    accum = pair_forces(window, weights, deriv_h, deriv_s, nbr, 0, ATOMS, min(AT_DEV, 128), HALO)
    return accum[:, :ATOMS]
```

```python
import functools

import jax
import jax.numpy as jnp
from jax import lax
from jax.experimental import pallas as pl
from jax.experimental.pallas import tpu as pltpu
from jax.sharding import PartitionSpec as P

LANES = 128
CHUNK = 64
SHARD = ("atoms", "sub")
VMEM_LIMIT = 48 * 1024 * 1024


def shifted(value, axis, steps):
    count = lax.axis_size(axis)
    first, last = (max(0, -steps), min(count, count - steps))
    return lax.ppermute(value, axis, [(source, source + steps) for source in range(first, last)])


def split(value):
    high = value.astype(jnp.bfloat16)
    return high, (value - high.astype(jnp.float32)).astype(jnp.bfloat16)


def fetch(rows_ref, columns_ref, copy_sem):
    copies = [
        pltpu.make_async_copy(
            rows_ref.at[:, c * LANES : (c + 1) * LANES], columns_ref.at[c], copy_sem.at[c]
        )
        for c in range(rows_ref.shape[1] // LANES)
    ]
    for copy in copies:
        copy.start()
    return copies


def gram(left_high, left_low, right_high, right_low):
    dot = functools.partial(
        lax.dot_general,
        dimension_numbers=(((1,), (1,)), ((), ())),
        preferred_element_type=jnp.float32,
    )
    return (
        dot(left_high, right_high) + dot(left_high, right_low) + dot(left_low, right_high)
    )


def pick_pairs(gram_ref, planes, rows, index, deriv, pair_ref):
    low = [part & 7 for part in index]
    high = [part >> 3 for part in index]
    pair = [[jnp.zeros((8, LANES), jnp.float32) for half in range(2)] for k in range(3)]
    for group in planes:

        def step(r, picked):
            hit = [part == r for part in high]
            out = []
            for at, (plane, block, key) in enumerate(group):
                tile = gram_ref[plane, pl.ds(pl.multiple_of(r * 8, 8), 8), block * LANES : (block + 1) * LANES]
                for half in range(2):
                    got = jnp.take_along_axis(tile, low[half], axis=0)
                    out.append(jnp.where(hit[half], got, picked[2 * at + half]))
            return tuple(out)

        start = tuple(jnp.zeros((8, LANES), jnp.float32) for plane in group for half in range(2))
        picked = lax.fori_loop(0, rows // 8, step, start, unroll=2)
        for at, (plane, block, key) in enumerate(group):
            for k in range(3):
                for half in range(2):
                    pair[k][half] = pair[k][half] + picked[2 * at + half] * deriv(k, key, half)
    for k in range(3):
        for half in range(2):
            pair_ref[16 * k + 8 * half : 16 * k + 8 * half + 8, :] = pair[k][half]
    return [jnp.sum(pair[k][0] + pair[k][1], axis=0, keepdims=True) for k in range(3)]


def spread(index_ref, pair_ref, spread_ref, rows):
    lane_rows = lax.broadcasted_iota(jnp.int32, (8, LANES), 0)

    def step(r, unused):
        at = pl.multiple_of(r * 8, 8)
        target = lane_rows + at
        total = [jnp.zeros((8, LANES), jnp.float32) for k in range(3)]
        for n in range(16):
            hit = jnp.broadcast_to(index_ref[n : n + 1, :], (8, LANES)) == target
            for k in range(3):
                term = jnp.broadcast_to(pair_ref[16 * k + n : 16 * k + n + 1, :], (8, LANES))
                total[k] = total[k] + jnp.where(hit, term, 0.0)
        for k in range(3):
            spread_ref[k, pl.ds(at, 8), :] = total[k]
        return unused

    lax.fori_loop(0, rows // 8, step, 0)
    ones = jnp.ones((8, LANES), jnp.float32)
    out = []
    for k in range(3):
        total = lax.dot_general(
            ones,
            spread_ref[k, :rows, :],
            (((1,), (1,)), ((), ())),
            precision=lax.Precision.HIGHEST,
            preferred_element_type=jnp.float32,
        )
        out.append(total[:1])
    return out


def inner_kernel(
    start_ref, coeffs_ref, occup_ref, energies_ref, nbr_ref, dham_ref, dovl_ref,
    own_high_ref, own_low_ref, force_ref,
    near_high_ref, near_low_ref, gram_ref, index_ref, pair_ref, spread_ref, columns_ref, copy_sem,
):
    atoms = nbr_ref.shape[1]
    occup = occup_ref[...]
    weights = [occup, occup * energies_ref[...]]
    columns = fetch(coeffs_ref, columns_ref, copy_sem)
    for c, copy in enumerate(columns):
        copy.wait()
        lanes = slice(c * LANES, (c + 1) * LANES)
        for a in range(4):
            for at in range(0, atoms, CHUNK):
                rows = columns_ref[c, pl.ds(a + 4 * at, CHUNK, stride=4), :]
                own = (at // LANES) * 512 + a * LANES + at % LANES
                own_high_ref[own : own + CHUNK, lanes], own_low_ref[own : own + CHUNK, lanes] = split(rows)
                for x in range(2):
                    near = (x * 4 + a) * atoms + at
                    near_high_ref[near : near + CHUNK, lanes], near_low_ref[near : near + CHUNK, lanes] = split(
                        rows * weights[x][:, lanes]
                    )
    force_ref[...] = jnp.zeros_like(force_ref)
    for tile in range(2):
        first = tile * LANES
        rows = atoms - first

        def multiply(xb, unused, first=first, rows=rows, tile=tile):
            at = pl.multiple_of(xb * atoms + first, LANES)
            gram_ref[xb, :rows, :] = gram(
                near_high_ref[pl.ds(at, rows), :],
                near_low_ref[pl.ds(at, rows), :],
                own_high_ref[tile * 512 : tile * 512 + 512, :],
                own_low_ref[tile * 512 : tile * 512 + 512, :],
            )
            return unused

        lax.fori_loop(0, 8, multiply, 0)
        index_ref[...] = nbr_ref[:, first : first + LANES] - (start_ref[0] + first)
        index = [index_ref[8 * half : 8 * half + 8, :] for half in range(2)]

        def deriv(k, key, half, first=first):
            x, ab = key
            block = (dham_ref, dovl_ref)[x][k * 16 + ab, 8 * half : 8 * half + 8, first : first + LANES]
            return -block if x else block

        planes = [
            [(x * 4 + b, a, (x, a * 4 + b)) for a in (2 * g, 2 * g + 1) for b in range(4)]
            for x in range(2)
            for g in range(2)
        ]
        mine = pick_pairs(gram_ref, planes, rows, index, deriv, pair_ref)
        theirs = spread(index_ref, pair_ref, spread_ref, rows)
        for k in range(3):
            force_ref[k : k + 1, first : first + LANES] += -2.0 * mine[k]
            force_ref[k : k + 1, first : first + rows] += 2.0 * theirs[k]


def cross_kernel(
    start_ref, above_ref, below_ref, blocks_ref, occup_ref, energies_ref, nbr_ref, dham_ref, dovl_ref,
    own_high_ref, own_low_ref, inner_ref,
    force_ref, up_ref, down_ref,
    near_high_ref, near_low_ref, gram_ref, index_ref, pair_ref, spread_ref,
    above_columns_ref, below_columns_ref, above_sem, below_sem,
):
    atoms = nbr_ref.shape[1]
    above_copies = fetch(above_ref, above_columns_ref, above_sem)
    below_copies = fetch(below_ref, below_columns_ref, below_sem)
    lower = above_ref.shape[0] // 4
    upper = below_ref.shape[0] // 4
    half_lanes = LANES // 2
    occup = occup_ref[...]
    weights = [occup, occup * energies_ref[...]]
    force_ref[...] = inner_ref[...]
    up_ref[...] = jnp.zeros_like(up_ref)
    down_ref[...] = jnp.zeros_like(down_ref)

    for c, copy in enumerate(above_copies):
        copy.wait()
        lanes = slice(c * LANES, (c + 1) * LANES)
        for b in range(4):
            rows = above_columns_ref[c, pl.ds(b, lower, stride=4), :]
            for x in range(2):
                at = (x * 4 + b) * lower
                near_high_ref[at : at + lower, lanes], near_low_ref[at : at + lower, lanes] = split(
                    rows * weights[x][:, lanes]
                )

    def multiply(xb, unused):
        at = pl.multiple_of(xb * lower, 16)
        gram_ref[xb, :lower, :] = gram(
            near_high_ref[pl.ds(at, lower), :],
            near_low_ref[pl.ds(at, lower), :],
            own_high_ref[512:, :],
            own_low_ref[512:, :],
        )
        return unused

    lax.fori_loop(0, 8, multiply, 0)
    index_ref[...] = nbr_ref[:, LANES:] - (start_ref[0] + atoms)
    index = [index_ref[8 * half : 8 * half + 8, :] for half in range(2)]

    def deriv(k, key, half):
        x, ab = key
        block = (dham_ref, dovl_ref)[x][k * 16 + ab, 8 * half : 8 * half + 8, LANES:]
        return -block if x else block

    planes = [
        [(x * 4 + b, a, (x, a * 4 + b)) for a in (2 * g, 2 * g + 1) for b in range(4)]
        for x in range(2)
        for g in range(2)
    ]
    mine = pick_pairs(gram_ref, planes, lower, index, deriv, pair_ref)
    theirs = spread(index_ref, pair_ref, spread_ref, lower)
    for k in range(3):
        force_ref[k : k + 1, LANES:] += -2.0 * mine[k]
        up_ref[k : k + 1, :lower] = 2.0 * theirs[k]

    if upper < half_lanes:
        near_high_ref[:512, :] = jnp.zeros_like(near_high_ref[:512, :])
        near_low_ref[:512, :] = jnp.zeros_like(near_low_ref[:512, :])
    for c, copy in enumerate(below_copies):
        copy.wait()
        lanes = slice(c * LANES, (c + 1) * LANES)
        for a in range(4):
            rows = below_columns_ref[c, pl.ds(a, upper, stride=4), :]
            for x in range(2):
                at = a * LANES + x * half_lanes
                near_high_ref[at : at + upper, lanes], near_low_ref[at : at + upper, lanes] = split(
                    rows * weights[x][:, lanes]
                )

    def multiply_lower(b, unused):
        at = pl.multiple_of(b * LANES + lower, 16)
        gram_ref[b, :upper, :] = gram(
            own_high_ref[pl.ds(at, upper), :],
            own_low_ref[pl.ds(at, upper), :],
            near_high_ref[:512, :],
            near_low_ref[:512, :],
        )
        return unused

    lax.fori_loop(0, 4, multiply_lower, 0)
    index_ref[...] = blocks_ref[48].astype(jnp.int32) - lower
    index = [index_ref[8 * half : 8 * half + 8, :] for half in range(2)]

    def deriv_lower(k, key, half):
        return blocks_ref[k * 16 + key, 8 * half : 8 * half + 8, :]

    planes = [[(b, a, a * 4 + b) for a in (2 * g, 2 * g + 1) for b in range(4)] for g in range(2)]
    mine = pick_pairs(gram_ref, planes, upper, index, deriv_lower, pair_ref)
    theirs = spread(index_ref, pair_ref, spread_ref, upper)
    for k in range(3):
        down_ref[k : k + 1, :] = -2.0 * mine[k]
        force_ref[k : k + 1, lower:LANES] += 2.0 * theirs[k]


def local(coeffs, occup, energies, nbr, dham, dovl):
    slots, atoms = nbr.shape
    states = coeffs.shape[1]
    halo = atoms // 2
    upper = halo // 2
    lower = halo - upper
    half_lanes = LANES // 2
    start = lax.axis_index(SHARD) * atoms
    above = shifted(coeffs[: 4 * lower], SHARD, -1)
    below = shifted(coeffs[4 * (atoms - upper) :], SHARD, 1)
    target = jnp.where(nbr[:, atoms - upper :] >= 0, nbr[:, atoms - upper :] - (start + atoms), -1)
    target = jnp.pad(target.astype(jnp.float32), ((0, 0), (0, half_lanes - upper)), constant_values=-1.0)
    blocks = jnp.concatenate(
        [
            jnp.pad(dham[:, :, atoms - upper :], ((0, 0), (0, 0), (0, half_lanes - upper))),
            jnp.pad(-dovl[:, :, atoms - upper :], ((0, 0), (0, 0), (0, half_lanes - upper))),
        ],
        2,
    )
    blocks = jnp.concatenate([blocks, jnp.concatenate([target, target], 1)[None]], 0)
    blocks = shifted(blocks, SHARD, 1)
    start = start.reshape(1).astype(jnp.int32)
    occup = occup.reshape(1, states)
    energies = energies.reshape(1, states)

    vmem = pl.BlockSpec(memory_space=pltpu.VMEM)
    hbm = pl.BlockSpec(memory_space=pl.ANY)
    smem = pl.BlockSpec(memory_space=pltpu.SMEM)
    own_high, own_low, inner = pl.pallas_call(
        inner_kernel,
        out_shape=(
            jax.ShapeDtypeStruct((4 * atoms, states), jnp.bfloat16),
            jax.ShapeDtypeStruct((4 * atoms, states), jnp.bfloat16),
            jax.ShapeDtypeStruct((8, atoms), jnp.float32),
        ),
        in_specs=[smem, hbm] + [vmem] * 5,
        out_specs=(vmem, vmem, vmem),
        scratch_shapes=[
            pltpu.VMEM((8 * atoms, states), jnp.bfloat16),
            pltpu.VMEM((8 * atoms, states), jnp.bfloat16),
            pltpu.VMEM((8, atoms, 512), jnp.float32),
            pltpu.VMEM((slots, LANES), jnp.int32),
            pltpu.VMEM((3 * slots, LANES), jnp.float32),
            pltpu.VMEM((3, atoms, LANES), jnp.float32),
            pltpu.VMEM((states // LANES, 4 * atoms, LANES), jnp.float32),
            pltpu.SemaphoreType.DMA((states // LANES,)),
        ],
        compiler_params=pltpu.CompilerParams(vmem_limit_bytes=VMEM_LIMIT),
        cost_estimate=pl.CostEstimate(
            flops=3 * 2 * 8 * 384 * 512 * states, bytes_accessed=16 * 1024 * 1024, transcendentals=0
        ),
        name="inner_pairs",
    )(start, coeffs, occup, energies, nbr, dham, dovl)

    own, up, down = pl.pallas_call(
        cross_kernel,
        out_shape=(
            jax.ShapeDtypeStruct((8, atoms), jnp.float32),
            jax.ShapeDtypeStruct((8, LANES), jnp.float32),
            jax.ShapeDtypeStruct((8, LANES), jnp.float32),
        ),
        in_specs=[smem, hbm, hbm] + [vmem] * 9,
        out_specs=(vmem, vmem, vmem),
        scratch_shapes=[
            pltpu.VMEM((8 * LANES, states), jnp.bfloat16),
            pltpu.VMEM((8 * LANES, states), jnp.bfloat16),
            pltpu.VMEM((8, LANES, 512), jnp.float32),
            pltpu.VMEM((slots, LANES), jnp.int32),
            pltpu.VMEM((3 * slots, LANES), jnp.float32),
            pltpu.VMEM((3, LANES, LANES), jnp.float32),
            pltpu.VMEM((states // LANES, 4 * lower, LANES), jnp.float32),
            pltpu.VMEM((states // LANES, 4 * upper, LANES), jnp.float32),
            pltpu.SemaphoreType.DMA((states // LANES,)),
            pltpu.SemaphoreType.DMA((states // LANES,)),
        ],
        compiler_params=pltpu.CompilerParams(vmem_limit_bytes=VMEM_LIMIT),
        name="cross_pairs",
    )(start, above, below, blocks, occup, energies, nbr, dham, dovl, own_high, own_low, inner)

    up = shifted(up[:3], SHARD, 1)
    down = shifted(down[:3], SHARD, -1)
    down = (down[:, :half_lanes] + down[:, half_lanes:])[:, :upper]
    own = own[:3] + jnp.pad(up, ((0, 0), (0, atoms - LANES))) + jnp.pad(down, ((0, 0), (atoms - upper, 0)))
    return lax.psum(own, "states")


def solution(mesh):
    in_specs = (
        P(("groups", "atoms", "sub"), "states"),
        P(("groups", "states")),
        P(("groups", "states")),
        P(None, ("groups", "atoms", "sub")),
        P(None, None, ("groups", "atoms", "sub")),
        P(None, None, ("groups", "atoms", "sub")),
    )
    out_specs = P(None, ("groups", "atoms", "sub"))
    return jax.shard_map(local, mesh=mesh, in_specs=in_specs, out_specs=out_specs, check_vma=False)
```

```python
import functools

import jax
import jax.numpy as jnp
from jax import lax
from jax.experimental import pallas as pl
from jax.experimental.pallas import tpu as pltpu
from jax.sharding import PartitionSpec as P

LANES = 128
BLOCK = 64
SHARD = ("atoms", "sub")


def split(value):
    high = value.astype(jnp.bfloat16)
    return high, (value - high.astype(jnp.float32)).astype(jnp.bfloat16)


def gram(left_high, left_low, right_high, right_low):
    dot = functools.partial(
        lax.dot_general,
        dimension_numbers=(((1,), (1,)), ((), ())),
        preferred_element_type=jnp.float32,
    )
    return (
        dot(left_high, right_high) + dot(left_high, right_low) + dot(left_low, right_high)
    )


def lane_numbers():
    return lax.broadcasted_iota(jnp.int32, (8, LANES), 1)


def swap_halves(value):
    return pltpu.roll(value, BLOCK, 1)


def side_by_side(left, right, odd):
    if odd:
        return jnp.where(lane_numbers() < BLOCK, swap_halves(left), right)
    return jnp.where(lane_numbers() < BLOCK, left, swap_halves(right))


def pick_pairs(gram_ref, column, blocks, index, deriv):
    low = [part & 7 for part in index]
    high = [part >> 3 for part in index]
    pair = [[None, None] for k in range(3)]
    for x in range(2):
        picked = {}
        for r in range(8 * blocks):
            hit = [part == r for part in high]
            for b in range(4):
                row = (r // 8) * 512 + x * 256 + b * BLOCK + (r % 8) * 8
                for g in range(2):
                    at = column + g * LANES
                    tile = gram_ref[row : row + 8, at : at + LANES]
                    for half in range(2):
                        got = jnp.take_along_axis(tile, low[half], axis=0)
                        before = picked.get((b, g, half), 0.0)
                        picked[b, g, half] = jnp.where(hit[half], got, before)
        for (b, g, half), value in picked.items():
            for k in range(3):
                term = value * deriv(k, x, b, g, half)
                pair[k][half] = term if pair[k][half] is None else pair[k][half] + term
    return pair


def fold(pair):
    return [[value + swap_halves(value) for value in parts] for parts in pair]


def merge(even, odd):
    left = lane_numbers() < BLOCK
    return [[jnp.where(left, even[k][half], odd[k][half]) for half in range(2)] for k in range(3)]


def slot_sum(pair):
    return [jnp.sum(pair[k][0] + pair[k][1], axis=0, keepdims=True) for k in range(3)]


def spread(index_ref, pair, spread_ref, rows):
    lane_rows = lax.broadcasted_iota(jnp.int32, (8, LANES), 0)
    for r in range(rows // 8):
        slot = jnp.full((8, LANES), 16, jnp.int32)
        for n in range(16):
            hit = jnp.broadcast_to(index_ref[n : n + 1, :], (8, LANES)) == lane_rows + 8 * r
            slot = jnp.where(hit, n, slot)
        low = slot & 7
        for k in range(3):
            first = jnp.take_along_axis(pair[k][0], low, axis=0)
            second = jnp.take_along_axis(pair[k][1], low, axis=0)
            value = jnp.where(slot < 8, first, jnp.where(slot < 16, second, 0.0))
            spread_ref[k, 8 * r : 8 * r + 8, :] = value
    ones = jnp.ones((8, LANES), jnp.float32)
    out = []
    for k in range(3):
        total = lax.dot_general(
            ones,
            spread_ref[k, :rows, :],
            (((1,), (1,)), ((), ())),
            precision=lax.Precision.HIGHEST,
            preferred_element_type=jnp.float32,
        )
        out.append(total[:1])
    return out


def own_deriv(dham_ref, dovl_ref, tile, odd):
    def deriv(k, x, b, g, half):
        ref = (dham_ref, dovl_ref)[x]
        parts = [
            ref[k * 16 + (2 * g + parity) * 4 + b, 8 * half : 8 * half + 8, tile * LANES : (tile + 1) * LANES]
            for parity in range(2)
        ]
        both = side_by_side(parts[0], parts[1], odd)
        return -both if x else both

    return deriv


def block_index(index_ref, odd):
    return [
        side_by_side(index_ref[8 * half : 8 * half + 8, :], index_ref[8 * half : 8 * half + 8, :], odd)
        for half in range(2)
    ]


def inner_kernel(
    start_ref, coeffs_ref, occup_ref, energies_ref, nbr_ref, dham_ref, dovl_ref,
    own_high_ref, own_low_ref, near1_high_ref, near1_low_ref, force_ref,
    near0_high_ref, near0_low_ref, near2_high_ref, near2_low_ref, near3_high_ref, near3_low_ref,
    gram0_ref, gram1_ref, gram2_ref, gram3_ref, index_ref, spread_ref, columns_ref, copy_sem,
):
    states = coeffs_ref.shape[1]
    count = states // LANES
    near = [
        (near0_high_ref, near0_low_ref),
        (near1_high_ref, near1_low_ref),
        (near2_high_ref, near2_low_ref),
        (near3_high_ref, near3_low_ref),
    ]
    grams = [gram0_ref, gram1_ref, gram2_ref, gram3_ref]
    copies = {}
    for j in (3, 2, 1, 0):
        for c in range(count):
            copies[j, c] = pltpu.make_async_copy(
                coeffs_ref.at[j * 256 : j * 256 + 256, c * LANES : (c + 1) * LANES],
                columns_ref.at[c, j * 256 : j * 256 + 256, :],
                copy_sem.at[j * count + c],
            )
            copies[j, c].start()
    occup = occup_ref[...]
    weights = [occup, occup * energies_ref[...]]

    def prepare(j):
        for c in range(count):
            copies[j, c].wait()
            lanes = slice(c * LANES, (c + 1) * LANES)
            for a in range(4):
                rows = columns_ref[c, pl.ds(j * 256 + a, BLOCK, stride=4), :]
                own = slice(j * 256 + a * BLOCK, j * 256 + (a + 1) * BLOCK)
                own_high_ref[own, lanes], own_low_ref[own, lanes] = split(rows)
                for x in range(2):
                    at = slice(x * 256 + a * BLOCK, x * 256 + (a + 1) * BLOCK)
                    near[j][0][at, lanes], near[j][1][at, lanes] = split(rows * weights[x][:, lanes])

    def multiply(h):
        own = slice(h * 256, h * 256 + 256)
        for j in range(h, min(h + 3, 4)):
            grams[h][(j - h) * 512 : (j - h) * 512 + 512, :] = gram(
                near[j][0][...], near[j][1][...], own_high_ref[own, :], own_low_ref[own, :]
            )

    for tile in range(2):
        index_ref[tile] = nbr_ref[:, tile * LANES : (tile + 1) * LANES] - (start_ref[0] + tile * LANES)

    def pick(h):
        index = [part - BLOCK * (h % 2) for part in block_index(index_ref.at[h // 2], h % 2)]
        blocks = min(h + 3, 4) - h
        return fold(pick_pairs(grams[h], 0, blocks, index, own_deriv(dham_ref, dovl_ref, h // 2, h % 2)))

    def finish(tile, even, odd):
        pair = merge(even, odd)
        mine = slot_sum(pair)
        rows = 256 - tile * LANES
        theirs = spread(index_ref.at[tile], pair, spread_ref, rows)
        return mine, theirs

    prepare(3)
    multiply(3)
    prepare(2)
    multiply(2)
    pair3 = pick(3)
    prepare(1)
    multiply(1)
    pair2 = pick(2)
    prepare(0)
    mine1, theirs1 = finish(1, pair2, pair3)
    multiply(0)
    pair1 = pick(1)
    pair0 = pick(0)
    mine0, theirs0 = finish(0, pair0, pair1)
    force_ref[...] = jnp.zeros_like(force_ref)
    for k in range(3):
        force_ref[k : k + 1, :LANES] = 2.0 * (theirs0[k][:, :LANES] - mine0[k])
        force_ref[k : k + 1, LANES:] = 2.0 * (theirs0[k][:, LANES:] + theirs1[k] - mine1[k])


def cross_kernel(
    parity,
    start_ref, rows_ref, blocks_ref, occup_ref, energies_ref, nbr_ref, dham_ref, dovl_ref,
    own_high_ref, own_low_ref, near_high_ref, near_low_ref,
    force_ref, sent_ref,
    cut_high_ref, cut_low_ref, gram_ref, index_ref, spread_ref, columns_ref, copy_sem,
):
    atoms = nbr_ref.shape[1]
    states = rows_ref.shape[1]
    copies = [
        pltpu.make_async_copy(
            rows_ref.at[:, c * LANES : (c + 1) * LANES], columns_ref.at[c], copy_sem.at[c]
        )
        for c in range(states // LANES)
    ]
    for copy in copies:
        copy.start()
    force_ref[...] = jnp.zeros_like(force_ref)
    sent_ref[...] = jnp.zeros_like(sent_ref)
    for copy in copies:
        copy.wait()
    first = ((start_ref[0] // atoms) & 1) == parity

    @pl.when(first)
    def above():
        occup = occup_ref[...]
        weights = [occup, occup * energies_ref[...]]
        for c in range(states // LANES):
            lanes = slice(c * LANES, (c + 1) * LANES)
            for b in range(4):
                rows = columns_ref[c, pl.ds(b, BLOCK, stride=4), :]
                for x in range(2):
                    at = slice(x * 256 + b * BLOCK, x * 256 + (b + 1) * BLOCK)
                    cut_high_ref[at, lanes], cut_low_ref[at, lanes] = split(rows * weights[x][:, lanes])
        gram_ref[...] = gram(
            cut_high_ref[...], cut_low_ref[...], own_high_ref[512:, :], own_low_ref[512:, :]
        )
        index_ref[...] = nbr_ref[:, LANES:] - (start_ref[0] + atoms)
        even, odd = (
            fold(
                pick_pairs(
                    gram_ref, h * 256, 1, block_index(index_ref, h), own_deriv(dham_ref, dovl_ref, 1, h)
                )
            )
            for h in range(2)
        )
        pair = merge(even, odd)
        mine = slot_sum(pair)
        theirs = spread(index_ref, pair, spread_ref, BLOCK)
        for k in range(3):
            force_ref[k : k + 1, LANES:] = -2.0 * mine[k]
            sent_ref[k : k + 1, :BLOCK] = 2.0 * theirs[k]

    @pl.when(jnp.logical_not(first))
    def below():
        for c in range(states // LANES):
            lanes = slice(c * LANES, (c + 1) * LANES)
            for a in range(4):
                rows = columns_ref[c, pl.ds(a, BLOCK, stride=4), :]
                at = slice(a * BLOCK, (a + 1) * BLOCK)
                cut_high_ref[at, lanes], cut_low_ref[at, lanes] = split(rows)
        gram_ref[:, :256] = gram(
            near_high_ref[...], near_low_ref[...], cut_high_ref[:256, :], cut_low_ref[:256, :]
        )
        index_ref[...] = blocks_ref[48].astype(jnp.int32) - BLOCK
        index = [index_ref[8 * half : 8 * half + 8, :] for half in range(2)]

        def deriv(k, x, b, g, half):
            return blocks_ref[x * 24 + k * 8 + g * 4 + b, 8 * half : 8 * half + 8, :]

        pair = pick_pairs(gram_ref, 0, 1, index, deriv)
        theirs = spread(index_ref, pair, spread_ref, BLOCK)
        mine = slot_sum(fold(pair))
        for k in range(3):
            force_ref[k : k + 1, BLOCK:LANES] = 2.0 * theirs[k]
            sent_ref[k : k + 1, atoms - BLOCK :] = -2.0 * mine[k][:, BLOCK:]


def core_swap(value):
    return lax.ppermute(value, "sub", [(0, 1), (1, 0)])


def core_up(value):
    return lax.ppermute(value, "sub", [(0, 1)])


def shard_swap(value):
    count = lax.axis_size(SHARD)
    pairs = [pair for at in range(1, count - 1, 2) for pair in ((at, at + 1), (at + 1, at))]
    return lax.ppermute(value, SHARD, pairs)


def shard_up(value):
    count = lax.axis_size(SHARD)
    return lax.ppermute(value, SHARD, [(at, at + 1) for at in range(1, count - 1, 2)])


def local(coeffs, occup, energies, nbr, dham, dovl):
    slots, atoms = nbr.shape
    states = coeffs.shape[1]
    sub = lax.axis_index("sub")
    start = lax.axis_index(SHARD) * atoms

    far_rows = shard_swap(lax.dynamic_slice_in_dim(coeffs, sub * (4 * (atoms - BLOCK)), 4 * BLOCK))
    core_rows = core_swap(lax.dynamic_slice_in_dim(coeffs, (1 - sub) * (4 * (atoms - BLOCK)), 4 * BLOCK))
    last = nbr[:, atoms - BLOCK :]
    target = jnp.where(last >= 0, last - (start + atoms), -1).astype(jnp.float32)

    def parities(deriv):
        deriv = deriv[:, :, atoms - BLOCK :].reshape(3, 2, 2, 4, slots, BLOCK)
        return jnp.concatenate([deriv[:, :, 0], deriv[:, :, 1]], -1).reshape(24, slots, LANES)

    blocks = jnp.concatenate(
        [parities(dham), -parities(dovl), jnp.concatenate([target, target], 1)[None]], 0
    )
    core_blocks = core_up(blocks)
    far_blocks = shard_up(blocks)
    start = start.reshape(1).astype(jnp.int32)
    occup = occup.reshape(1, states)
    energies = energies.reshape(1, states)

    vmem = pl.BlockSpec(memory_space=pltpu.VMEM)
    hbm = pl.BlockSpec(memory_space=pl.ANY)
    smem = pl.BlockSpec(memory_space=pltpu.SMEM)
    half = jax.ShapeDtypeStruct((512, states), jnp.bfloat16)
    whole = jax.ShapeDtypeStruct((4 * atoms, states), jnp.bfloat16)
    force = jax.ShapeDtypeStruct((8, atoms), jnp.float32)
    prepared = pltpu.VMEM((512, states), jnp.bfloat16)
    own_high, own_low, near_high, near_low, inner = pl.pallas_call(
        inner_kernel,
        out_shape=(whole, whole, half, half, force),
        in_specs=[smem, hbm] + [vmem] * 5,
        out_specs=(vmem,) * 5,
        scratch_shapes=[prepared] * 6
        + [pltpu.VMEM((512 * n, 256), jnp.float32) for n in (3, 3, 2, 1)]
        + [
            pltpu.VMEM((2, slots, LANES), jnp.int32),
            pltpu.VMEM((3, atoms, LANES), jnp.float32),
            pltpu.VMEM((states // LANES, 4 * atoms, LANES), jnp.float32),
            pltpu.SemaphoreType.DMA((4 * states // LANES,)),
        ],
        compiler_params=pltpu.CompilerParams(vmem_limit_bytes=32 * 1024 * 1024),
        cost_estimate=pl.CostEstimate(
            flops=3 * 2 * 9 * 512 * 256 * states, bytes_accessed=16 * 1024 * 1024, transcendentals=0
        ),
        name="inner_pairs",
    )(start, coeffs, occup, energies, nbr, dham, dovl)

    def cross(parity, rows, blocks, name):
        return pl.pallas_call(
            functools.partial(cross_kernel, parity),
            out_shape=(force, force),
            in_specs=[smem, hbm] + [vmem] * 10,
            out_specs=(vmem, vmem),
            scratch_shapes=[
                prepared,
                prepared,
                pltpu.VMEM((512, 512), jnp.float32),
                pltpu.VMEM((slots, LANES), jnp.int32),
                pltpu.VMEM((3, BLOCK, LANES), jnp.float32),
                pltpu.VMEM((states // LANES, 4 * BLOCK, LANES), jnp.float32),
                pltpu.SemaphoreType.DMA((states // LANES,)),
            ],
            compiler_params=pltpu.CompilerParams(vmem_limit_bytes=20 * 1024 * 1024),
            cost_estimate=pl.CostEstimate(
                flops=3 * 2 * 2 * 512 * 256 * states, bytes_accessed=6 * 1024 * 1024, transcendentals=0
            ),
            name=name,
        )(start, rows, blocks, occup, energies, nbr, dham, dovl, own_high, own_low, near_high, near_low)

    core_force, core_sent = cross(0, core_rows, core_blocks, "core_pairs")
    core_back = core_swap(core_sent[:3])
    far_force, far_sent = cross(1, far_rows, far_blocks, "far_pairs")
    far_back = shard_swap(far_sent[:3])
    total = inner[:3] + core_force[:3] + core_back + far_force[:3] + far_back
    return lax.psum(total, "states")


def solution(mesh):
    in_specs = (
        P(("groups", "atoms", "sub"), "states"),
        P(("groups", "states")),
        P(("groups", "states")),
        P(None, ("groups", "atoms", "sub")),
        P(None, None, ("groups", "atoms", "sub")),
        P(None, None, ("groups", "atoms", "sub")),
    )
    out_specs = P(None, ("groups", "atoms", "sub"))
    return jax.shard_map(local, mesh=mesh, in_specs=in_specs, out_specs=out_specs, check_vma=False)
```

```python
import functools

import jax
import jax.numpy as jnp
from jax import lax
from jax.experimental import pallas as pl
from jax.experimental.pallas import tpu as pltpu
from jax.sharding import PartitionSpec as P

LANES = 128
BLOCK = 64
UPPER = 48
SHARD = ("atoms", "sub")


def split(value):
    high = value.astype(jnp.bfloat16)
    return high, (value - high.astype(jnp.float32)).astype(jnp.bfloat16)


def gram(left_high, left_low, right_high, right_low):
    dot = functools.partial(
        lax.dot_general,
        dimension_numbers=(((1,), (1,)), ((), ())),
        preferred_element_type=jnp.float32,
    )
    return (
        dot(left_high, right_high) + dot(left_high, right_low) + dot(left_low, right_high)
    )


def lane_numbers():
    return lax.broadcasted_iota(jnp.int32, (8, LANES), 1)


def swap_halves(value):
    return pltpu.roll(value, BLOCK, 1)


def side_by_side(left, right, odd):
    if odd:
        return jnp.where(lane_numbers() < BLOCK, swap_halves(left), right)
    return jnp.where(lane_numbers() < BLOCK, left, swap_halves(right))


def pick_pairs(gram_ref, column, size, index, deriv, blocks=1):
    low = [part & 7 for part in index]
    high = [part >> 3 for part in index]
    pair = [[None, None] for k in range(3)]
    for x in range(2):
        picked = {}
        for r in range(size // 8 * blocks):
            hit = [part == r for part in high]
            for b in range(4):
                block, part = divmod(r, size // 8)
                row = ((block * 2 + x) * 4 + b) * size + part * 8
                for g in range(2):
                    at = column + g * LANES
                    tile = gram_ref[row : row + 8, at : at + LANES]
                    for half in range(2):
                        got = jnp.take_along_axis(tile, low[half], axis=0)
                        before = picked.get((b, g, half), 0.0)
                        picked[b, g, half] = jnp.where(hit[half], got, before)
        for (b, g, half), value in picked.items():
            for k in range(3):
                term = value * deriv(k, x, b, g, half)
                pair[k][half] = term if pair[k][half] is None else pair[k][half] + term
    return pair


def fold(pair):
    return [[value + swap_halves(value) for value in parts] for parts in pair]


def merge(even, odd):
    left = lane_numbers() < BLOCK
    return [[jnp.where(left, even[k][half], odd[k][half]) for half in range(2)] for k in range(3)]


def slot_sum(pair):
    return [jnp.sum(pair[k][0] + pair[k][1], axis=0, keepdims=True) for k in range(3)]


def spread(index_ref, pair, spread_ref, rows):
    lane_rows = lax.broadcasted_iota(jnp.int32, (8, LANES), 0)
    for r in range(rows // 8):
        slot = jnp.full((8, LANES), 16, jnp.int32)
        for n in range(16):
            hit = jnp.broadcast_to(index_ref[n : n + 1, :], (8, LANES)) == lane_rows + 8 * r
            slot = jnp.where(hit, n, slot)
        low = slot & 7
        for k in range(3):
            first = jnp.take_along_axis(pair[k][0], low, axis=0)
            second = jnp.take_along_axis(pair[k][1], low, axis=0)
            value = jnp.where(slot < 8, first, jnp.where(slot < 16, second, 0.0))
            spread_ref[k, 8 * r : 8 * r + 8, :] = value
    ones = jnp.ones((8, LANES), jnp.float32)
    out = []
    for k in range(3):
        total = lax.dot_general(
            ones,
            spread_ref[k, :rows, :],
            (((1,), (1,)), ((), ())),
            precision=lax.Precision.HIGHEST,
            preferred_element_type=jnp.float32,
        )
        out.append(total[:1])
    return out


def own_deriv(dham_ref, dovl_ref, tile, odd):
    def deriv(k, x, b, g, half):
        ref = (dham_ref, dovl_ref)[x]
        parts = [
            ref[k * 16 + (2 * g + parity) * 4 + b, 8 * half : 8 * half + 8, tile * LANES : (tile + 1) * LANES]
            for parity in range(2)
        ]
        both = side_by_side(parts[0], parts[1], odd)
        return -both if x else both

    return deriv


def block_index(index_ref, odd):
    return [
        side_by_side(index_ref[8 * half : 8 * half + 8, :], index_ref[8 * half : 8 * half + 8, :], odd)
        for half in range(2)
    ]


def inner_kernel(
    start_ref, coeffs_ref, occup_ref, energies_ref, nbr_ref, dham_ref, dovl_ref,
    own_high_ref, own_low_ref, near1_high_ref, near1_low_ref, force_ref,
    near0_high_ref, near0_low_ref, near2_high_ref, near2_low_ref, near3_high_ref, near3_low_ref,
    gram0_ref, gram1_ref, gram2_ref, gram3_ref, index_ref, spread_ref, columns_ref, copy_sem,
):
    states = coeffs_ref.shape[1]
    count = states // LANES
    near = [
        (near0_high_ref, near0_low_ref),
        (near1_high_ref, near1_low_ref),
        (near2_high_ref, near2_low_ref),
        (near3_high_ref, near3_low_ref),
    ]
    grams = [gram0_ref, gram1_ref, gram2_ref, gram3_ref]
    copies = {}
    for j in (3, 2, 1, 0):
        for c in range(count):
            copies[j, c] = pltpu.make_async_copy(
                coeffs_ref.at[j * 256 : j * 256 + 256, c * LANES : (c + 1) * LANES],
                columns_ref.at[c, j * 256 : j * 256 + 256, :],
                copy_sem.at[j * count + c],
            )
            copies[j, c].start()
    occup = occup_ref[...]
    weights = [occup, occup * energies_ref[...]]

    def prepare(j):
        for c in range(count):
            copies[j, c].wait()
            lanes = slice(c * LANES, (c + 1) * LANES)
            for a in range(4):
                rows = columns_ref[c, pl.ds(j * 256 + a, BLOCK, stride=4), :]
                own = slice(j * 256 + a * BLOCK, j * 256 + (a + 1) * BLOCK)
                own_high_ref[own, lanes], own_low_ref[own, lanes] = split(rows)
                for x in range(2):
                    at = slice(x * 256 + a * BLOCK, x * 256 + (a + 1) * BLOCK)
                    near[j][0][at, lanes], near[j][1][at, lanes] = split(rows * weights[x][:, lanes])

    def multiply(h):
        own = slice(h * 256, h * 256 + 256)
        for j in range(h, min(h + 3, 4)):
            grams[h][(j - h) * 512 : (j - h) * 512 + 512, :] = gram(
                near[j][0][...], near[j][1][...], own_high_ref[own, :], own_low_ref[own, :]
            )

    for tile in range(2):
        index_ref[tile] = nbr_ref[:, tile * LANES : (tile + 1) * LANES] - (start_ref[0] + tile * LANES)

    def pick(h):
        index = [part - BLOCK * (h % 2) for part in block_index(index_ref.at[h // 2], h % 2)]
        blocks = min(h + 3, 4) - h
        return fold(pick_pairs(grams[h], 0, BLOCK, index, own_deriv(dham_ref, dovl_ref, h // 2, h % 2), blocks))

    def finish(tile, even, odd):
        pair = merge(even, odd)
        mine = slot_sum(pair)
        rows = 256 - tile * LANES
        theirs = spread(index_ref.at[tile], pair, spread_ref, rows)
        return mine, theirs

    for j in (3, 2, 1, 0):
        prepare(j)
    for h in (3, 2, 1, 0):
        multiply(h)
    pair3 = pick(3)
    pair2 = pick(2)
    mine1, theirs1 = finish(1, pair2, pair3)
    pair1 = pick(1)
    pair0 = pick(0)
    mine0, theirs0 = finish(0, pair0, pair1)
    force_ref[...] = jnp.zeros_like(force_ref)
    for k in range(3):
        force_ref[k : k + 1, :LANES] = 2.0 * (theirs0[k][:, :LANES] - mine0[k])
        force_ref[k : k + 1, LANES:] = 2.0 * (theirs0[k][:, LANES:] + theirs1[k] - mine1[k])


def payload_rows(atoms, states):
    planes = -(-48 // (states // LANES))
    return max(4 * (atoms // 2 - UPPER), 4 * UPPER + 16 * planes + 16)


def pack_kernel(
    start_ref, coeffs_ref, nbr_ref, dham_ref, dovl_ref, core_ref, far_ref,
    ham_ref, ovl_ref, core_sem, far_sem, deriv_sem,
):
    atoms = nbr_ref.shape[1]
    count, rows, unused = core_ref.shape
    lower = 4 * (atoms // 2 - UPPER)
    first = ((start_ref[0] // atoms) & 1) == 0
    fetched = [
        pltpu.make_async_copy(source.at[:, :, atoms - LANES :], target, deriv_sem.at[at])
        for at, (source, target) in enumerate([(dham_ref, ham_ref), (dovl_ref, ovl_ref)])
    ]

    def fill(up_ref, up_sem, down_ref, down_sem):
        copies = []
        for c in range(count):
            lanes = slice(c * LANES, (c + 1) * LANES)
            up_rows = coeffs_ref.at[4 * (atoms - UPPER) :, lanes]
            copies.append(pltpu.make_async_copy(up_rows, up_ref.at[c, : 4 * UPPER, :], up_sem.at[c]))
            down_rows = coeffs_ref.at[:lower, lanes]
            copies.append(pltpu.make_async_copy(down_rows, down_ref.at[c, :lower, :], down_sem.at[c]))
        for copy in fetched + copies:
            copy.start()
        if rows > lower:
            down_ref[:, lower:, :] = jnp.zeros((count, rows - lower, LANES), jnp.float32)
        up_ref[:, 4 * UPPER :, :] = jnp.zeros((count, rows - 4 * UPPER, LANES), jnp.float32)
        planes = -(-48 // count)
        last = nbr_ref[:, atoms - LANES :]
        target = jnp.where(last >= 0, last - (start_ref[0] + atoms), -1).astype(jnp.float32)
        at = 4 * UPPER + 16 * planes
        for half in range(2):
            part = target[8 * half : 8 * half + 8]
            up_ref[0, at + 8 * half : at + 8 * half + 8, :] = side_by_side(part, part, 1)
        for copy in fetched:
            copy.wait()
        for x, ref in enumerate((ham_ref, ovl_ref)):
            for k in range(3):
                for g in range(2):
                    for b in range(4):
                        plane = x * 24 + k * 8 + g * 4 + b
                        for half in range(2):
                            parts = [
                                ref[k * 16 + (2 * g + parity) * 4 + b, 8 * half : 8 * half + 8, :]
                                for parity in range(2)
                            ]
                            both = side_by_side(parts[0], parts[1], 1)
                            at = 4 * UPPER + 16 * (plane // count) + 8 * half
                            up_ref[plane % count, at : at + 8, :] = -both if x else both
        for copy in copies:
            copy.wait()

    @pl.when(first)
    def even():
        fill(core_ref, core_sem, far_ref, far_sem)

    @pl.when(jnp.logical_not(first))
    def odd():
        fill(far_ref, far_sem, core_ref, core_sem)


def cross_kernel(
    parity,
    start_ref, payload_ref, before_ref, back_ref, occup_ref, energies_ref, nbr_ref, dham_ref, dovl_ref,
    own_high_ref, own_low_ref, near_high_ref, near_low_ref,
    force_ref, sent_ref,
    cut_high_ref, cut_low_ref, gram_ref, index_ref, spread_ref,
):
    atoms = nbr_ref.shape[1]
    count = payload_ref.shape[0]
    lower = atoms // 2 - UPPER
    force_ref[...] = before_ref[...] + back_ref[...]
    sent_ref[...] = jnp.zeros_like(sent_ref)
    first = ((start_ref[0] // atoms) & 1) == parity

    @pl.when(first)
    def above():
        occup = occup_ref[...]
        weights = [occup, occup * energies_ref[...]]
        for c in range(count):
            lanes = slice(c * LANES, (c + 1) * LANES)
            for b in range(4):
                rows = payload_ref[c, pl.ds(b, lower, stride=4), :]
                for x in range(2):
                    at = slice((x * 4 + b) * lower, (x * 4 + b + 1) * lower)
                    cut_high_ref[at, lanes], cut_low_ref[at, lanes] = split(rows * weights[x][:, lanes])
        gram_ref[...] = gram(
            cut_high_ref[...], cut_low_ref[...], own_high_ref[512:, :], own_low_ref[512:, :]
        )
        index_ref[...] = nbr_ref[:, LANES:] - (start_ref[0] + atoms)
        even, odd = (
            fold(
                pick_pairs(
                    gram_ref, h * 256, lower, block_index(index_ref, h), own_deriv(dham_ref, dovl_ref, 1, h)
                )
            )
            for h in range(2)
        )
        pair = merge(even, odd)
        mine = slot_sum(pair)
        theirs = spread(index_ref, pair, spread_ref, lower)
        for k in range(3):
            force_ref[k : k + 1, LANES:] += -2.0 * mine[k]
            sent_ref[k : k + 1, :lower] = 2.0 * theirs[k]

    @pl.when(jnp.logical_not(first))
    def below():
        skip = BLOCK - UPPER
        for c in range(count):
            lanes = slice(c * LANES, (c + 1) * LANES)
            for a in range(4):
                rows = payload_ref[c, pl.ds(a, UPPER, stride=4), :]
                at = slice(a * BLOCK + skip, (a + 1) * BLOCK)
                cut_high_ref[at, lanes], cut_low_ref[at, lanes] = split(rows)
                at = slice(a * BLOCK, a * BLOCK + skip)
                cut_high_ref[at, lanes] = jnp.zeros((skip, LANES), jnp.bfloat16)
                cut_low_ref[at, lanes] = jnp.zeros((skip, LANES), jnp.bfloat16)
        gram_ref[:512, :256] = gram(
            near_high_ref[...], near_low_ref[...], cut_high_ref[:256, :], cut_low_ref[:256, :]
        )
        planes = -(-48 // count)
        at = 4 * UPPER + 16 * planes
        target = payload_ref[0, at : at + 16, :].astype(jnp.int32)
        index_ref[...] = jnp.where(target >= lower, target - BLOCK, -1)
        index = [index_ref[8 * half : 8 * half + 8, :] for half in range(2)]

        def deriv(k, x, b, g, half):
            plane = x * 24 + k * 8 + g * 4 + b
            at = 4 * UPPER + 16 * (plane // count) + 8 * half
            return payload_ref[plane % count, at : at + 8, :]

        pair = pick_pairs(gram_ref, 0, BLOCK, index, deriv)
        theirs = spread(index_ref, pair, spread_ref, BLOCK)
        mine = slot_sum(fold(pair))
        for k in range(3):
            force_ref[k : k + 1, BLOCK:LANES] += 2.0 * theirs[k]
            sent_ref[k : k + 1, atoms - BLOCK :] = -2.0 * mine[k][:, BLOCK:]


def core_swap(value):
    return lax.ppermute(value, "sub", [(0, 1), (1, 0)])


def shard_swap(value):
    count = lax.axis_size(SHARD)
    pairs = [pair for at in range(1, count - 1, 2) for pair in ((at, at + 1), (at + 1, at))]
    return lax.ppermute(value, SHARD, pairs)


def local(coeffs, occup, energies, nbr, dham, dovl):
    slots, atoms = nbr.shape
    states = coeffs.shape[1]
    start = (lax.axis_index(SHARD) * atoms).reshape(1).astype(jnp.int32)
    occup = occup.reshape(1, states)
    energies = energies.reshape(1, states)
    count = states // LANES

    vmem = pl.BlockSpec(memory_space=pltpu.VMEM)
    hbm = pl.BlockSpec(memory_space=pltpu.HBM)
    smem = pl.BlockSpec(memory_space=pltpu.SMEM)
    half = jax.ShapeDtypeStruct((512, states), jnp.bfloat16)
    whole = jax.ShapeDtypeStruct((4 * atoms, states), jnp.bfloat16)
    force = jax.ShapeDtypeStruct((8, atoms), jnp.float32)
    prepared = pltpu.VMEM((512, states), jnp.bfloat16)
    lower = atoms // 2 - UPPER
    payload = jax.ShapeDtypeStruct((count, payload_rows(atoms, states), LANES), jnp.float32)
    core_payload, far_payload = pl.pallas_call(
        pack_kernel,
        out_shape=(payload, payload),
        in_specs=[smem, hbm, vmem, hbm, hbm],
        out_specs=(vmem, vmem),
        scratch_shapes=[
            pltpu.VMEM((48, slots, LANES), jnp.float32),
            pltpu.VMEM((48, slots, LANES), jnp.float32),
            pltpu.SemaphoreType.DMA((count,)),
            pltpu.SemaphoreType.DMA((count,)),
            pltpu.SemaphoreType.DMA((2,)),
        ],
        compiler_params=pltpu.CompilerParams(vmem_limit_bytes=52 * 1024 * 1024),
        name="pack",
    )(start, coeffs, nbr, dham, dovl)
    far_payload = shard_swap(far_payload)
    core_payload = core_swap(core_payload)
    own_high, own_low, near_high, near_low, inner = pl.pallas_call(
        inner_kernel,
        out_shape=(whole, whole, half, half, force),
        in_specs=[smem, hbm] + [vmem] * 5,
        out_specs=(vmem,) * 5,
        scratch_shapes=[prepared] * 6
        + [pltpu.VMEM((512 * n, 256), jnp.float32) for n in (3, 3, 2, 1)]
        + [
            pltpu.VMEM((2, slots, LANES), jnp.int32),
            pltpu.VMEM((3, atoms, LANES), jnp.float32),
            pltpu.VMEM((states // LANES, 4 * atoms, LANES), jnp.float32),
            pltpu.SemaphoreType.DMA((4 * states // LANES,)),
        ],
        compiler_params=pltpu.CompilerParams(vmem_limit_bytes=32 * 1024 * 1024),
        cost_estimate=pl.CostEstimate(
            flops=3 * 2 * 9 * 512 * 256 * states, bytes_accessed=16 * 1024 * 1024, transcendentals=0
        ),
        name="inner_pairs",
    )(start, coeffs, occup, energies, nbr, dham, dovl)

    def cross(parity, payload, before, back, name):
        cut = pltpu.VMEM((8 * lower, states), jnp.bfloat16)
        return pl.pallas_call(
            functools.partial(cross_kernel, parity),
            out_shape=(force, force),
            in_specs=[smem] + [vmem] * 12,
            out_specs=(vmem, vmem),
            scratch_shapes=[
                cut,
                cut,
                pltpu.VMEM((8 * lower, 512), jnp.float32),
                pltpu.VMEM((slots, LANES), jnp.int32),
                pltpu.VMEM((3, lower, LANES), jnp.float32),
            ],
            compiler_params=pltpu.CompilerParams(vmem_limit_bytes=20 * 1024 * 1024),
            cost_estimate=pl.CostEstimate(
                flops=3 * 2 * 2 * 512 * 256 * states, bytes_accessed=6 * 1024 * 1024, transcendentals=0
            ),
            name=name,
        )(start, payload, before, back, occup, energies, nbr, dham, dovl, own_high, own_low, near_high, near_low)

    total, core_sent = cross(0, core_payload, inner, jnp.zeros((8, atoms), jnp.float32), "core_pairs")
    total, far_sent = cross(1, far_payload, total, core_swap(core_sent), "far_pairs")
    total = (total + shard_swap(far_sent))[:3]
    if lax.axis_size("states") == 2:
        return total + lax.ppermute(total, "states", [(0, 1), (1, 0)])
    return lax.psum(total, "states")


def solution(mesh):
    in_specs = (
        P(("groups", "atoms", "sub"), "states"),
        P(("groups", "states")),
        P(("groups", "states")),
        P(None, ("groups", "atoms", "sub")),
        P(None, None, ("groups", "atoms", "sub")),
        P(None, None, ("groups", "atoms", "sub")),
    )
    out_specs = P(None, ("groups", "atoms", "sub"))
    return jax.shard_map(local, mesh=mesh, in_specs=in_specs, out_specs=out_specs, check_vma=False)
```

```python
import functools

import jax
import jax.numpy as jnp
from jax import lax
from jax.experimental import pallas as pl
from jax.experimental.pallas import tpu as pltpu
from jax.sharding import PartitionSpec as P

LANES = 128
BLOCK = 64
UPPER = 48
SHARD = ("atoms", "sub")


def split(value):
    high = value.astype(jnp.bfloat16)
    return high, (value - high.astype(jnp.float32)).astype(jnp.bfloat16)


def gram(left_high, left_low, right_high, right_low):
    dot = functools.partial(
        lax.dot_general,
        dimension_numbers=(((1,), (1,)), ((), ())),
        preferred_element_type=jnp.float32,
    )
    return (
        dot(left_high, right_high) + dot(left_high, right_low) + dot(left_low, right_high)
    )


def lane_numbers():
    return lax.broadcasted_iota(jnp.int32, (8, LANES), 1)


def swap_halves(value):
    return pltpu.roll(value, BLOCK, 1)


def side_by_side(left, right, odd):
    if odd:
        return jnp.where(lane_numbers() < BLOCK, swap_halves(left), right)
    return jnp.where(lane_numbers() < BLOCK, left, swap_halves(right))


def pick_pairs(gram_ref, column, size, index, deriv, blocks=1):
    low = [part & 7 for part in index]
    high = [part >> 3 for part in index]
    pair = [[None, None] for k in range(3)]
    for x in range(2):
        picked = {}
        for r in range(size // 8 * blocks):
            hit = [part == r for part in high]
            for b in range(4):
                block, part = divmod(r, size // 8)
                row = ((block * 2 + x) * 4 + b) * size + part * 8
                for g in range(2):
                    at = column + g * LANES
                    tile = gram_ref[row : row + 8, at : at + LANES]
                    for half in range(2):
                        got = jnp.take_along_axis(tile, low[half], axis=0)
                        before = picked.get((b, g, half), 0.0)
                        picked[b, g, half] = jnp.where(hit[half], got, before)
        for (b, g, half), value in picked.items():
            for k in range(3):
                term = value * deriv(k, x, b, g, half)
                pair[k][half] = term if pair[k][half] is None else pair[k][half] + term
    return pair


def fold(pair):
    return [[value + swap_halves(value) for value in parts] for parts in pair]


def merge(even, odd):
    left = lane_numbers() < BLOCK
    return [[jnp.where(left, even[k][half], odd[k][half]) for half in range(2)] for k in range(3)]


def slot_sum(pair):
    return [jnp.sum(pair[k][0] + pair[k][1], axis=0, keepdims=True) for k in range(3)]


def spread(index_ref, pair, spread_ref, rows):
    lane_rows = lax.broadcasted_iota(jnp.int32, (8, LANES), 0)
    for r in range(rows // 8):
        slot = jnp.full((8, LANES), 16, jnp.int32)
        for n in range(16):
            hit = jnp.broadcast_to(index_ref[n : n + 1, :], (8, LANES)) == lane_rows + 8 * r
            slot = jnp.where(hit, n, slot)
        low = slot & 7
        for k in range(3):
            first = jnp.take_along_axis(pair[k][0], low, axis=0)
            second = jnp.take_along_axis(pair[k][1], low, axis=0)
            value = jnp.where(slot < 8, first, jnp.where(slot < 16, second, 0.0))
            spread_ref[k, 8 * r : 8 * r + 8, :] = value
    ones = jnp.ones((8, LANES), jnp.float32)
    out = []
    for k in range(3):
        total = lax.dot_general(
            ones,
            spread_ref[k, :rows, :],
            (((1,), (1,)), ((), ())),
            precision=lax.Precision.HIGHEST,
            preferred_element_type=jnp.float32,
        )
        out.append(total[:1])
    return out


def own_deriv(dham_ref, dovl_ref, tile, odd):
    def deriv(k, x, b, g, half):
        ref = (dham_ref, dovl_ref)[x]
        parts = [
            ref[k * 16 + (2 * g + parity) * 4 + b, 8 * half : 8 * half + 8, tile * LANES : (tile + 1) * LANES]
            for parity in range(2)
        ]
        both = side_by_side(parts[0], parts[1], odd)
        return -both if x else both

    return deriv


def block_index(index_ref, odd):
    return [
        side_by_side(index_ref[8 * half : 8 * half + 8, :], index_ref[8 * half : 8 * half + 8, :], odd)
        for half in range(2)
    ]


def inner_kernel(
    start_ref, coeffs_ref, occup_ref, energies_ref, nbr_ref, dham_ref, dovl_ref,
    own_high_ref, own_low_ref, near1_high_ref, near1_low_ref, force_ref,
    near0_high_ref, near0_low_ref, near2_high_ref, near2_low_ref, near3_high_ref, near3_low_ref,
    gram0_ref, gram1_ref, gram2_ref, gram3_ref, index_ref, spread_ref, columns_ref, copy_sem,
):
    states = coeffs_ref.shape[1]
    count = states // LANES
    near = [
        (near0_high_ref, near0_low_ref),
        (near1_high_ref, near1_low_ref),
        (near2_high_ref, near2_low_ref),
        (near3_high_ref, near3_low_ref),
    ]
    grams = [gram0_ref, gram1_ref, gram2_ref, gram3_ref]
    copies = {}
    for j in (3, 2, 1, 0):
        for c in range(count):
            copies[j, c] = pltpu.make_async_copy(
                coeffs_ref.at[j * 256 : j * 256 + 256, c * LANES : (c + 1) * LANES],
                columns_ref.at[c, j * 256 : j * 256 + 256, :],
                copy_sem.at[j * count + c],
            )
            copies[j, c].start()
    occup = occup_ref[...]
    weights = [occup, occup * energies_ref[...]]

    def prepare(j):
        for c in range(count):
            copies[j, c].wait()
            lanes = slice(c * LANES, (c + 1) * LANES)
            for a in range(4):
                rows = columns_ref[c, pl.ds(j * 256 + a, BLOCK, stride=4), :]
                own = slice(j * 256 + a * BLOCK, j * 256 + (a + 1) * BLOCK)
                own_high_ref[own, lanes], own_low_ref[own, lanes] = split(rows)
                for x in range(2):
                    at = slice(x * 256 + a * BLOCK, x * 256 + (a + 1) * BLOCK)
                    near[j][0][at, lanes], near[j][1][at, lanes] = split(rows * weights[x][:, lanes])

    def multiply(h):
        own = slice(h * 256, h * 256 + 256)
        for j in range(h, min(h + 3, 4)):
            grams[h][(j - h) * 512 : (j - h) * 512 + 512, :] = gram(
                near[j][0][...], near[j][1][...], own_high_ref[own, :], own_low_ref[own, :]
            )

    for tile in range(2):
        index_ref[tile] = nbr_ref[:, tile * LANES : (tile + 1) * LANES] - (start_ref[0] + tile * LANES)

    def pick(h):
        index = [part - BLOCK * (h % 2) for part in block_index(index_ref.at[h // 2], h % 2)]
        blocks = min(h + 3, 4) - h
        return fold(pick_pairs(grams[h], 0, BLOCK, index, own_deriv(dham_ref, dovl_ref, h // 2, h % 2), blocks))

    def finish(tile, even, odd):
        pair = merge(even, odd)
        mine = slot_sum(pair)
        rows = 256 - tile * LANES
        theirs = spread(index_ref.at[tile], pair, spread_ref, rows)
        return mine, theirs

    for j in (3, 2, 1, 0):
        prepare(j)
    for h in (3, 2, 1, 0):
        multiply(h)
    pair3 = pick(3)
    pair2 = pick(2)
    mine1, theirs1 = finish(1, pair2, pair3)
    pair1 = pick(1)
    pair0 = pick(0)
    mine0, theirs0 = finish(0, pair0, pair1)
    force_ref[...] = jnp.zeros_like(force_ref)
    for k in range(3):
        force_ref[k : k + 1, :LANES] = 2.0 * (theirs0[k][:, :LANES] - mine0[k])
        force_ref[k : k + 1, LANES:] = 2.0 * (theirs0[k][:, LANES:] + theirs1[k] - mine1[k])


def payload_rows(atoms, states):
    planes = -(-48 // (states // LANES))
    return max(4 * (atoms // 2 - UPPER), 4 * UPPER + 16 * planes + 16)


def pack_kernel(
    start_ref, coeffs_ref, nbr_ref, dham_ref, dovl_ref, core_ref, far_ref,
    ham_ref, ovl_ref, last_ref, core_sem, far_sem, deriv_sem,
):
    atoms = nbr_ref.shape[1]
    count, rows, unused = core_ref.shape
    lower = 4 * (atoms // 2 - UPPER)
    first = ((start_ref[0] // atoms) & 1) == 0
    fetched = [
        pltpu.make_async_copy(source.at[:, :, atoms - LANES :], target, deriv_sem.at[at])
        for at, (source, target) in enumerate([(dham_ref, ham_ref), (dovl_ref, ovl_ref)])
    ]
    fetched.append(
        pltpu.make_async_copy(nbr_ref.at[:, atoms - LANES :], last_ref, deriv_sem.at[2])
    )

    def fill(up_ref, up_sem, down_ref, down_sem):
        copies = []
        for c in range(count):
            lanes = slice(c * LANES, (c + 1) * LANES)
            up_rows = coeffs_ref.at[4 * (atoms - UPPER) :, lanes]
            copies.append(pltpu.make_async_copy(up_rows, up_ref.at[c, : 4 * UPPER, :], up_sem.at[c]))
            down_rows = coeffs_ref.at[:lower, lanes]
            copies.append(pltpu.make_async_copy(down_rows, down_ref.at[c, :lower, :], down_sem.at[c]))
        for copy in fetched + copies:
            copy.start()
        if rows > lower:
            down_ref[:, lower:, :] = jnp.zeros((count, rows - lower, LANES), jnp.float32)
        up_ref[:, 4 * UPPER :, :] = jnp.zeros((count, rows - 4 * UPPER, LANES), jnp.float32)
        planes = -(-48 // count)
        for copy in fetched:
            copy.wait()
        last = last_ref[...]
        target = jnp.where(last >= 0, last - (start_ref[0] + atoms), -1).astype(jnp.float32)
        at = 4 * UPPER + 16 * planes
        for half in range(2):
            part = target[8 * half : 8 * half + 8]
            up_ref[0, at + 8 * half : at + 8 * half + 8, :] = side_by_side(part, part, 1)
        for x, ref in enumerate((ham_ref, ovl_ref)):
            for k in range(3):
                for g in range(2):
                    for b in range(4):
                        plane = x * 24 + k * 8 + g * 4 + b
                        for half in range(2):
                            parts = [
                                ref[k * 16 + (2 * g + parity) * 4 + b, 8 * half : 8 * half + 8, :]
                                for parity in range(2)
                            ]
                            both = side_by_side(parts[0], parts[1], 1)
                            at = 4 * UPPER + 16 * (plane // count) + 8 * half
                            up_ref[plane % count, at : at + 8, :] = -both if x else both
        for copy in copies:
            copy.wait()

    @pl.when(first)
    def even():
        fill(core_ref, core_sem, far_ref, far_sem)

    @pl.when(jnp.logical_not(first))
    def odd():
        fill(far_ref, far_sem, core_ref, core_sem)


def cross_kernel(
    parity,
    start_ref, payload_ref, before_ref, back_ref, occup_ref, energies_ref, nbr_ref, dham_ref, dovl_ref,
    own_high_ref, own_low_ref, near_high_ref, near_low_ref,
    force_ref, sent_ref,
    cut_high_ref, cut_low_ref, gram_ref, index_ref, spread_ref,
):
    atoms = nbr_ref.shape[1]
    count = payload_ref.shape[0]
    lower = atoms // 2 - UPPER
    force_ref[...] = before_ref[...] + back_ref[...]
    sent_ref[...] = jnp.zeros_like(sent_ref)
    first = ((start_ref[0] // atoms) & 1) == parity

    @pl.when(first)
    def above():
        occup = occup_ref[...]
        weights = [occup, occup * energies_ref[...]]
        for c in range(count):
            lanes = slice(c * LANES, (c + 1) * LANES)
            for b in range(4):
                rows = payload_ref[c, pl.ds(b, lower, stride=4), :]
                for x in range(2):
                    at = slice((x * 4 + b) * lower, (x * 4 + b + 1) * lower)
                    cut_high_ref[at, lanes], cut_low_ref[at, lanes] = split(rows * weights[x][:, lanes])
        gram_ref[...] = gram(
            cut_high_ref[...], cut_low_ref[...], own_high_ref[512:, :], own_low_ref[512:, :]
        )
        index_ref[...] = nbr_ref[:, LANES:] - (start_ref[0] + atoms)
        even, odd = (
            fold(
                pick_pairs(
                    gram_ref, h * 256, lower, block_index(index_ref, h), own_deriv(dham_ref, dovl_ref, 1, h)
                )
            )
            for h in range(2)
        )
        pair = merge(even, odd)
        mine = slot_sum(pair)
        theirs = spread(index_ref, pair, spread_ref, lower)
        for k in range(3):
            force_ref[k : k + 1, LANES:] += -2.0 * mine[k]
            sent_ref[k : k + 1, :lower] = 2.0 * theirs[k]

    @pl.when(jnp.logical_not(first))
    def below():
        skip = BLOCK - UPPER
        for c in range(count):
            lanes = slice(c * LANES, (c + 1) * LANES)
            for a in range(4):
                rows = payload_ref[c, pl.ds(a, UPPER, stride=4), :]
                at = slice(a * BLOCK + skip, (a + 1) * BLOCK)
                cut_high_ref[at, lanes], cut_low_ref[at, lanes] = split(rows)
                at = slice(a * BLOCK, a * BLOCK + skip)
                cut_high_ref[at, lanes] = jnp.zeros((skip, LANES), jnp.bfloat16)
                cut_low_ref[at, lanes] = jnp.zeros((skip, LANES), jnp.bfloat16)
        gram_ref[:512, :256] = gram(
            near_high_ref[...], near_low_ref[...], cut_high_ref[:256, :], cut_low_ref[:256, :]
        )
        planes = -(-48 // count)
        at = 4 * UPPER + 16 * planes
        target = payload_ref[0, at : at + 16, :].astype(jnp.int32)
        index_ref[...] = jnp.where(target >= lower, target - BLOCK, -1)
        index = [index_ref[8 * half : 8 * half + 8, :] for half in range(2)]

        def deriv(k, x, b, g, half):
            plane = x * 24 + k * 8 + g * 4 + b
            at = 4 * UPPER + 16 * (plane // count) + 8 * half
            return payload_ref[plane % count, at : at + 8, :]

        pair = pick_pairs(gram_ref, 0, BLOCK, index, deriv)
        theirs = spread(index_ref, pair, spread_ref, BLOCK)
        mine = slot_sum(fold(pair))
        for k in range(3):
            force_ref[k : k + 1, BLOCK:LANES] += 2.0 * theirs[k]
            sent_ref[k : k + 1, atoms - BLOCK :] = -2.0 * mine[k][:, BLOCK:]


def in_hbm(value):
    return pltpu.with_memory_space_constraint(value, pltpu.HBM)


def core_swap(value):
    return lax.ppermute(value, "sub", [(0, 1), (1, 0)])


def shard_swap(value):
    count = lax.axis_size(SHARD)
    pairs = [pair for at in range(1, count - 1, 2) for pair in ((at, at + 1), (at + 1, at))]
    return lax.ppermute(value, SHARD, pairs)


def local(coeffs, occup, energies, nbr, dham, dovl):
    slots, atoms = nbr.shape
    states = coeffs.shape[1]
    start = (lax.axis_index(SHARD) * atoms).reshape(1).astype(jnp.int32)
    occup = occup.reshape(1, states)
    energies = energies.reshape(1, states)
    count = states // LANES

    vmem = pl.BlockSpec(memory_space=pltpu.VMEM)
    hbm = pl.BlockSpec(memory_space=pltpu.HBM)
    smem = pl.BlockSpec(memory_space=pltpu.SMEM)
    half = jax.ShapeDtypeStruct((512, states), jnp.bfloat16)
    whole = jax.ShapeDtypeStruct((4 * atoms, states), jnp.bfloat16)
    force = jax.ShapeDtypeStruct((8, atoms), jnp.float32)
    prepared = pltpu.VMEM((512, states), jnp.bfloat16)
    lower = atoms // 2 - UPPER
    payload = jax.ShapeDtypeStruct((count, payload_rows(atoms, states), LANES), jnp.float32)
    core_payload, far_payload = pl.pallas_call(
        pack_kernel,
        out_shape=(payload, payload),
        in_specs=[smem] + [hbm] * 4,
        out_specs=(vmem, vmem),
        scratch_shapes=[
            pltpu.VMEM((48, slots, LANES), jnp.float32),
            pltpu.VMEM((48, slots, LANES), jnp.float32),
            pltpu.VMEM((slots, LANES), jnp.int32),
            pltpu.SemaphoreType.DMA((count,)),
            pltpu.SemaphoreType.DMA((count,)),
            pltpu.SemaphoreType.DMA((3,)),
        ],
        compiler_params=pltpu.CompilerParams(vmem_limit_bytes=12 * 1024 * 1024),
        name="pack",
    )(start, *(in_hbm(value) for value in (coeffs, nbr, dham, dovl)))
    far_payload = shard_swap(far_payload)
    core_payload = core_swap(core_payload)
    own_high, own_low, near_high, near_low, inner = pl.pallas_call(
        inner_kernel,
        out_shape=(whole, whole, half, half, force),
        in_specs=[smem, hbm] + [vmem] * 5,
        out_specs=(vmem,) * 5,
        scratch_shapes=[prepared] * 6
        + [pltpu.VMEM((512 * n, 256), jnp.float32) for n in (3, 3, 2, 1)]
        + [
            pltpu.VMEM((2, slots, LANES), jnp.int32),
            pltpu.VMEM((3, atoms, LANES), jnp.float32),
            pltpu.VMEM((states // LANES, 4 * atoms, LANES), jnp.float32),
            pltpu.SemaphoreType.DMA((4 * states // LANES,)),
        ],
        compiler_params=pltpu.CompilerParams(vmem_limit_bytes=32 * 1024 * 1024),
        cost_estimate=pl.CostEstimate(
            flops=3 * 2 * 9 * 512 * 256 * states, bytes_accessed=16 * 1024 * 1024, transcendentals=0
        ),
        name="inner_pairs",
    )(start, in_hbm(coeffs), occup, energies, nbr, dham, dovl)

    def cross(parity, payload, before, back, name):
        cut = pltpu.VMEM((8 * lower, states), jnp.bfloat16)
        return pl.pallas_call(
            functools.partial(cross_kernel, parity),
            out_shape=(force, force),
            in_specs=[smem] + [vmem] * 12,
            out_specs=(vmem, vmem),
            scratch_shapes=[
                cut,
                cut,
                pltpu.VMEM((8 * lower, 512), jnp.float32),
                pltpu.VMEM((slots, LANES), jnp.int32),
                pltpu.VMEM((3, lower, LANES), jnp.float32),
            ],
            compiler_params=pltpu.CompilerParams(vmem_limit_bytes=20 * 1024 * 1024),
            cost_estimate=pl.CostEstimate(
                flops=3 * 2 * 2 * 512 * 256 * states, bytes_accessed=6 * 1024 * 1024, transcendentals=0
            ),
            name=name,
        )(start, payload, before, back, occup, energies, nbr, dham, dovl, own_high, own_low, near_high, near_low)

    total, core_sent = cross(0, core_payload, inner, jnp.zeros((8, atoms), jnp.float32), "core_pairs")
    total, far_sent = cross(1, far_payload, total, core_swap(core_sent), "far_pairs")
    total = (total + shard_swap(far_sent))[:3]
    if lax.axis_size("states") == 2:
        return total + lax.ppermute(total, "states", [(0, 1), (1, 0)])
    return lax.psum(total, "states")


def solution(mesh):
    in_specs = (
        P(("groups", "atoms", "sub"), "states"),
        P(("groups", "states")),
        P(("groups", "states")),
        P(None, ("groups", "atoms", "sub")),
        P(None, None, ("groups", "atoms", "sub")),
        P(None, None, ("groups", "atoms", "sub")),
    )
    out_specs = P(None, ("groups", "atoms", "sub"))
    return jax.shard_map(local, mesh=mesh, in_specs=in_specs, out_specs=out_specs, check_vma=False)
```

```python
import functools

import jax
import jax.numpy as jnp
from jax import lax
from jax.experimental import pallas as pl
from jax.experimental.pallas import tpu as pltpu
from jax.sharding import PartitionSpec as P

LANES = 128
BLOCK = 64
UPPER = 48
SHARD = ("atoms", "sub")


def split(value):
    high = value.astype(jnp.bfloat16)
    return high, (value - high.astype(jnp.float32)).astype(jnp.bfloat16)


def gram(left_high, left_low, right_high, right_low):
    dot = functools.partial(
        lax.dot_general,
        dimension_numbers=(((1,), (1,)), ((), ())),
        preferred_element_type=jnp.float32,
    )
    return (
        dot(left_high, right_high) + dot(left_high, right_low) + dot(left_low, right_high)
    )


def lane_numbers():
    return lax.broadcasted_iota(jnp.int32, (8, LANES), 1)


def swap_halves(value):
    return pltpu.roll(value, BLOCK, 1)


def side_by_side(left, right, odd):
    if odd:
        return jnp.where(lane_numbers() < BLOCK, swap_halves(left), right)
    return jnp.where(lane_numbers() < BLOCK, left, swap_halves(right))


def pick_pairs(gram_ref, column, size, index, deriv, blocks=1):
    low = [part & 7 for part in index]
    high = [part >> 3 for part in index]
    pair = [[None, None] for k in range(3)]
    for x in range(2):
        picked = {}
        for r in range(size // 8 * blocks):
            hit = [part == r for part in high]
            for b in range(4):
                block, part = divmod(r, size // 8)
                row = ((block * 2 + x) * 4 + b) * size + part * 8
                for g in range(2):
                    at = column + g * LANES
                    tile = gram_ref[row : row + 8, at : at + LANES]
                    for half in range(2):
                        got = jnp.take_along_axis(tile, low[half], axis=0)
                        before = picked.get((b, g, half), 0.0)
                        picked[b, g, half] = jnp.where(hit[half], got, before)
        for (b, g, half), value in picked.items():
            for k in range(3):
                term = value * deriv(k, x, b, g, half)
                if pair[k][half] is None:
                    pair[k][half] = term
                else:
                    pair[k][half] = pair[k][half] - term if x else pair[k][half] + term
    return pair


def fold(pair):
    return [[value + swap_halves(value) for value in parts] for parts in pair]


def merge(even, odd):
    left = lane_numbers() < BLOCK
    return [[jnp.where(left, even[k][half], odd[k][half]) for half in range(2)] for k in range(3)]


def slot_sum(pair):
    return [jnp.sum(pair[k][0] + pair[k][1], axis=0, keepdims=True) for k in range(3)]


def spread(index_ref, pair, spread_ref, rows):
    lane_rows = lax.broadcasted_iota(jnp.int32, (8, LANES), 0)
    for r in range(rows // 8):
        slot = jnp.full((8, LANES), 16, jnp.int32)
        for n in range(16):
            hit = jnp.broadcast_to(index_ref[n : n + 1, :], (8, LANES)) == lane_rows + 8 * r
            slot = jnp.where(hit, n, slot)
        low = slot & 7
        for k in range(3):
            first = jnp.take_along_axis(pair[k][0], low, axis=0)
            second = jnp.take_along_axis(pair[k][1], low, axis=0)
            value = jnp.where(slot < 8, first, jnp.where(slot < 16, second, 0.0))
            spread_ref[k, 8 * r : 8 * r + 8, :] = value
    ones = jnp.ones((8, LANES), jnp.float32)
    out = []
    for k in range(3):
        total = lax.dot_general(
            ones,
            spread_ref[k, :rows, :],
            (((1,), (1,)), ((), ())),
            precision=lax.Precision.HIGHEST,
            preferred_element_type=jnp.float32,
        )
        out.append(total[:1])
    return out


def own_deriv(dham_ref, dovl_ref, tile, odd):
    def deriv(k, x, b, g, half):
        ref = (dham_ref, dovl_ref)[x]
        parts = [
            ref[k * 16 + (2 * g + parity) * 4 + b, 8 * half : 8 * half + 8, tile * LANES : (tile + 1) * LANES]
            for parity in range(2)
        ]
        return side_by_side(parts[0], parts[1], odd)

    return deriv


def block_index(index_ref, odd):
    return [
        side_by_side(index_ref[8 * half : 8 * half + 8, :], index_ref[8 * half : 8 * half + 8, :], odd)
        for half in range(2)
    ]


def inner_kernel(
    start_ref, coeffs_ref, occup_ref, energies_ref, nbr_ref, dham_ref, dovl_ref,
    own_high_ref, own_low_ref, near1_high_ref, near1_low_ref, force_ref,
    near0_high_ref, near0_low_ref, near2_high_ref, near2_low_ref, near3_high_ref, near3_low_ref,
    gram0_ref, gram1_ref, gram2_ref, gram3_ref, index_ref, spread_ref, columns_ref, ham_ref, ovl_ref, copy_sem, deriv_sem,
):
    states = coeffs_ref.shape[1]
    count = states // LANES
    near = [
        (near0_high_ref, near0_low_ref),
        (near1_high_ref, near1_low_ref),
        (near2_high_ref, near2_low_ref),
        (near3_high_ref, near3_low_ref),
    ]
    grams = [gram0_ref, gram1_ref, gram2_ref, gram3_ref]
    copies = [
        pltpu.make_async_copy(
            coeffs_ref.at[:, c * LANES : (c + 1) * LANES], columns_ref.at[c], copy_sem.at[c]
        )
        for c in range(count)
    ]
    derivs = [
        pltpu.make_async_copy(source, target, deriv_sem.at[at])
        for at, (source, target) in enumerate([(dham_ref, ham_ref), (dovl_ref, ovl_ref)])
    ]
    for copy in copies + derivs:
        copy.start()
    occup = occup_ref[...]
    weights = [occup, occup * energies_ref[...]]

    for c, copy in enumerate(copies):
        copy.wait()
        lanes = slice(c * LANES, (c + 1) * LANES)
        for j in range(4):
            for a in range(4):
                rows = columns_ref[c, pl.ds(j * 256 + a, BLOCK, stride=4), :]
                own = slice(j * 256 + a * BLOCK, j * 256 + (a + 1) * BLOCK)
                own_high_ref[own, lanes], own_low_ref[own, lanes] = split(rows)
                for x in range(2):
                    at = slice(x * 256 + a * BLOCK, x * 256 + (a + 1) * BLOCK)
                    near[j][0][at, lanes], near[j][1][at, lanes] = split(rows * weights[x][:, lanes])

    def multiply(h):
        own = slice(h * 256, h * 256 + 256)
        for j in range(h, min(h + 3, 4)):
            grams[h][(j - h) * 512 : (j - h) * 512 + 512, :] = gram(
                near[j][0][...], near[j][1][...], own_high_ref[own, :], own_low_ref[own, :]
            )

    for tile in range(2):
        index_ref[tile] = nbr_ref[:, tile * LANES : (tile + 1) * LANES] - (start_ref[0] + tile * LANES)

    def pick(h):
        index = [part - BLOCK * (h % 2) for part in block_index(index_ref.at[h // 2], h % 2)]
        blocks = min(h + 3, 4) - h
        return fold(pick_pairs(grams[h], 0, BLOCK, index, own_deriv(ham_ref, ovl_ref, h // 2, h % 2), blocks))

    def finish(tile, even, odd):
        pair = merge(even, odd)
        mine = slot_sum(pair)
        rows = 256 - tile * LANES
        theirs = spread(index_ref.at[tile], pair, spread_ref, rows)
        return mine, theirs

    for h in (3, 2, 1, 0):
        multiply(h)
    for copy in derivs:
        copy.wait()
    pair3 = pick(3)
    pair2 = pick(2)
    mine1, theirs1 = finish(1, pair2, pair3)
    pair1 = pick(1)
    pair0 = pick(0)
    mine0, theirs0 = finish(0, pair0, pair1)
    force_ref[...] = jnp.zeros_like(force_ref)
    for k in range(3):
        force_ref[k : k + 1, :LANES] = 2.0 * (theirs0[k][:, :LANES] - mine0[k])
        force_ref[k : k + 1, LANES:] = 2.0 * (theirs0[k][:, LANES:] + theirs1[k] - mine1[k])


def payload_rows(atoms, states):
    planes = -(-48 // (states // LANES))
    return max(4 * (atoms // 2 - UPPER), 4 * UPPER + 16 * planes + 16)


def pack_kernel(
    start_ref, coeffs_ref, nbr_ref, dham_ref, dovl_ref, core_ref, far_ref,
    ham_ref, ovl_ref, last_ref, core_sem, far_sem, deriv_sem,
):
    atoms = nbr_ref.shape[1]
    count, rows, unused = core_ref.shape
    lower = 4 * (atoms // 2 - UPPER)
    first = ((start_ref[0] // atoms) & 1) == 0
    fetched = [
        pltpu.make_async_copy(source.at[:, :, atoms - LANES :], target, deriv_sem.at[at])
        for at, (source, target) in enumerate([(dham_ref, ham_ref), (dovl_ref, ovl_ref)])
    ]
    fetched.append(
        pltpu.make_async_copy(nbr_ref.at[:, atoms - LANES :], last_ref, deriv_sem.at[2])
    )

    def fill(up_ref, up_sem, down_ref, down_sem):
        copies = []
        for c in range(count):
            lanes = slice(c * LANES, (c + 1) * LANES)
            up_rows = coeffs_ref.at[4 * (atoms - UPPER) :, lanes]
            copies.append(pltpu.make_async_copy(up_rows, up_ref.at[c, : 4 * UPPER, :], up_sem.at[c]))
            down_rows = coeffs_ref.at[:lower, lanes]
            copies.append(pltpu.make_async_copy(down_rows, down_ref.at[c, :lower, :], down_sem.at[c]))
        for copy in fetched + copies:
            copy.start()
        if rows > lower:
            down_ref[:, lower:, :] = jnp.zeros((count, rows - lower, LANES), jnp.float32)
        up_ref[:, 4 * UPPER :, :] = jnp.zeros((count, rows - 4 * UPPER, LANES), jnp.float32)
        planes = -(-48 // count)
        for copy in fetched:
            copy.wait()
        last = last_ref[...]
        target = jnp.where(last >= 0, last - (start_ref[0] + atoms), -1).astype(jnp.float32)
        at = 4 * UPPER + 16 * planes
        for half in range(2):
            part = target[8 * half : 8 * half + 8]
            up_ref[0, at + 8 * half : at + 8 * half + 8, :] = side_by_side(part, part, 1)
        for x, ref in enumerate((ham_ref, ovl_ref)):
            for k in range(3):
                for g in range(2):
                    for b in range(4):
                        plane = x * 24 + k * 8 + g * 4 + b
                        for half in range(2):
                            parts = [
                                ref[k * 16 + (2 * g + parity) * 4 + b, 8 * half : 8 * half + 8, :]
                                for parity in range(2)
                            ]
                            at = 4 * UPPER + 16 * (plane // count) + 8 * half
                            up_ref[plane % count, at : at + 8, :] = side_by_side(parts[0], parts[1], 1)
        for copy in copies:
            copy.wait()

    @pl.when(first)
    def even():
        fill(core_ref, core_sem, far_ref, far_sem)

    @pl.when(jnp.logical_not(first))
    def odd():
        fill(far_ref, far_sem, core_ref, core_sem)


def cross_kernel(
    parity,
    start_ref, payload_ref, before_ref, occup_ref, energies_ref, nbr_ref, dham_ref, dovl_ref,
    own_high_ref, own_low_ref, near_high_ref, near_low_ref,
    force_ref, sent_ref,
    cut_high_ref, cut_low_ref, gram_ref, index_ref, spread_ref, ham_ref, ovl_ref, deriv_sem,
):
    atoms = nbr_ref.shape[1]
    count = payload_ref.shape[0]
    lower = atoms // 2 - UPPER
    force_ref[...] = before_ref[...]
    sent_ref[...] = jnp.zeros_like(sent_ref)
    first = ((start_ref[0] // atoms) & 1) == parity

    @pl.when(first)
    def above():
        derivs = [
            pltpu.make_async_copy(source.at[:, :, LANES:], target, deriv_sem.at[at])
            for at, (source, target) in enumerate([(dham_ref, ham_ref), (dovl_ref, ovl_ref)])
        ]
        for copy in derivs:
            copy.start()
        occup = occup_ref[...]
        weights = [occup, occup * energies_ref[...]]
        for c in range(count):
            lanes = slice(c * LANES, (c + 1) * LANES)
            for b in range(4):
                rows = payload_ref[c, pl.ds(b, lower, stride=4), :]
                for x in range(2):
                    at = slice((x * 4 + b) * lower, (x * 4 + b + 1) * lower)
                    cut_high_ref[at, lanes], cut_low_ref[at, lanes] = split(rows * weights[x][:, lanes])
        gram_ref[...] = gram(
            cut_high_ref[...], cut_low_ref[...], own_high_ref[512:, :], own_low_ref[512:, :]
        )
        for copy in derivs:
            copy.wait()
        index_ref[...] = nbr_ref[:, LANES:] - (start_ref[0] + atoms)
        even, odd = (
            fold(
                pick_pairs(
                    gram_ref, h * 256, lower, block_index(index_ref, h), own_deriv(ham_ref, ovl_ref, 0, h)
                )
            )
            for h in range(2)
        )
        pair = merge(even, odd)
        mine = slot_sum(pair)
        theirs = spread(index_ref, pair, spread_ref, lower)
        for k in range(3):
            force_ref[k : k + 1, LANES:] += -2.0 * mine[k]
            sent_ref[k : k + 1, :lower] = 2.0 * theirs[k]

    @pl.when(jnp.logical_not(first))
    def below():
        skip = BLOCK - UPPER
        for c in range(count):
            lanes = slice(c * LANES, (c + 1) * LANES)
            for a in range(4):
                rows = payload_ref[c, pl.ds(a, UPPER, stride=4), :]
                at = slice(a * BLOCK + skip, (a + 1) * BLOCK)
                cut_high_ref[at, lanes], cut_low_ref[at, lanes] = split(rows)
                at = slice(a * BLOCK, a * BLOCK + skip)
                cut_high_ref[at, lanes] = jnp.zeros((skip, LANES), jnp.bfloat16)
                cut_low_ref[at, lanes] = jnp.zeros((skip, LANES), jnp.bfloat16)
        gram_ref[:512, :256] = gram(
            near_high_ref[...], near_low_ref[...], cut_high_ref[:256, :], cut_low_ref[:256, :]
        )
        planes = -(-48 // count)
        at = 4 * UPPER + 16 * planes
        target = payload_ref[0, at : at + 16, :].astype(jnp.int32)
        index_ref[...] = jnp.where(target >= lower, target - BLOCK, -1)
        index = [index_ref[8 * half : 8 * half + 8, :] for half in range(2)]

        def deriv(k, x, b, g, half):
            plane = x * 24 + k * 8 + g * 4 + b
            at = 4 * UPPER + 16 * (plane // count) + 8 * half
            return payload_ref[plane % count, at : at + 8, :]

        pair = pick_pairs(gram_ref, 0, BLOCK, index, deriv)
        theirs = spread(index_ref, pair, spread_ref, BLOCK)
        mine = slot_sum(fold(pair))
        for k in range(3):
            force_ref[k : k + 1, BLOCK:LANES] += 2.0 * theirs[k]
            sent_ref[k : k + 1, atoms - BLOCK :] = -2.0 * mine[k][:, BLOCK:]


def in_hbm(value):
    return pltpu.with_memory_space_constraint(value, pltpu.HBM)


def core_swap(value):
    return lax.ppermute(value, "sub", [(0, 1), (1, 0)])


def shard_swap(value):
    count = lax.axis_size(SHARD)
    pairs = [pair for at in range(1, count - 1, 2) for pair in ((at, at + 1), (at + 1, at))]
    return lax.ppermute(value, SHARD, pairs)


def local(coeffs, occup, energies, nbr, dham, dovl):
    slots, atoms = nbr.shape
    states = coeffs.shape[1]
    start = (lax.axis_index(SHARD) * atoms).reshape(1).astype(jnp.int32)
    occup = occup.reshape(1, states)
    energies = energies.reshape(1, states)
    count = states // LANES

    vmem = pl.BlockSpec(memory_space=pltpu.VMEM)
    hbm = pl.BlockSpec(memory_space=pltpu.HBM)
    smem = pl.BlockSpec(memory_space=pltpu.SMEM)
    half = jax.ShapeDtypeStruct((512, states), jnp.bfloat16)
    whole = jax.ShapeDtypeStruct((4 * atoms, states), jnp.bfloat16)
    force = jax.ShapeDtypeStruct((8, atoms), jnp.float32)
    prepared = pltpu.VMEM((512, states), jnp.bfloat16)
    lower = atoms // 2 - UPPER
    payload = jax.ShapeDtypeStruct((count, payload_rows(atoms, states), LANES), jnp.float32)
    core_payload, far_payload = pl.pallas_call(
        pack_kernel,
        out_shape=(payload, payload),
        in_specs=[smem] + [hbm] * 4,
        out_specs=(vmem, vmem),
        scratch_shapes=[
            pltpu.VMEM((48, slots, LANES), jnp.float32),
            pltpu.VMEM((48, slots, LANES), jnp.float32),
            pltpu.VMEM((slots, LANES), jnp.int32),
            pltpu.SemaphoreType.DMA((count,)),
            pltpu.SemaphoreType.DMA((count,)),
            pltpu.SemaphoreType.DMA((3,)),
        ],
        compiler_params=pltpu.CompilerParams(vmem_limit_bytes=12 * 1024 * 1024),
        name="pack",
    )(start, *(in_hbm(value) for value in (coeffs, nbr, dham, dovl)))
    far_payload = shard_swap(far_payload)
    core_payload = core_swap(core_payload)
    own_high, own_low, near_high, near_low, inner = pl.pallas_call(
        inner_kernel,
        out_shape=(whole, whole, half, half, force),
        in_specs=[smem, hbm, vmem, vmem, vmem, hbm, hbm],
        out_specs=(vmem,) * 5,
        scratch_shapes=[prepared] * 6
        + [pltpu.VMEM((512 * n, 256), jnp.float32) for n in (3, 3, 2, 1)]
        + [
            pltpu.VMEM((2, slots, LANES), jnp.int32),
            pltpu.VMEM((3, atoms, LANES), jnp.float32),
            pltpu.VMEM((states // LANES, 4 * atoms, LANES), jnp.float32),
            pltpu.VMEM((48, slots, atoms), jnp.float32),
            pltpu.VMEM((48, slots, atoms), jnp.float32),
            pltpu.SemaphoreType.DMA((count,)),
            pltpu.SemaphoreType.DMA((2,)),
        ],
        compiler_params=pltpu.CompilerParams(vmem_limit_bytes=32 * 1024 * 1024),
        cost_estimate=pl.CostEstimate(
            flops=3 * 2 * 9 * 512 * 256 * states, bytes_accessed=16 * 1024 * 1024, transcendentals=0
        ),
        name="inner_pairs",
    )(start, in_hbm(coeffs), occup, energies, nbr, in_hbm(dham), in_hbm(dovl))

    def cross(parity, payload, before, name):
        cut = pltpu.VMEM((8 * lower, states), jnp.bfloat16)
        return pl.pallas_call(
            functools.partial(cross_kernel, parity),
            out_shape=(force, force),
            in_specs=[smem] + [vmem] * 5 + [hbm, hbm] + [vmem] * 4,
            out_specs=(vmem, vmem),
            scratch_shapes=[
                cut,
                cut,
                pltpu.VMEM((8 * lower, 512), jnp.float32),
                pltpu.VMEM((slots, LANES), jnp.int32),
                pltpu.VMEM((3, lower, LANES), jnp.float32),
                pltpu.VMEM((48, slots, LANES), jnp.float32),
                pltpu.VMEM((48, slots, LANES), jnp.float32),
                pltpu.SemaphoreType.DMA((2,)),
            ],
            compiler_params=pltpu.CompilerParams(vmem_limit_bytes=20 * 1024 * 1024),
            cost_estimate=pl.CostEstimate(
                flops=3 * 2 * 2 * 512 * 256 * states, bytes_accessed=6 * 1024 * 1024, transcendentals=0
            ),
            name=name,
        )(start, payload, before, occup, energies, nbr, in_hbm(dham), in_hbm(dovl), own_high, own_low, near_high, near_low)

    total, core_sent = cross(0, core_payload, inner, "core_pairs")
    core_back = core_swap(core_sent)
    total, far_sent = cross(1, far_payload, total, "far_pairs")
    total = (total + core_back + shard_swap(far_sent))[:3]
    if lax.axis_size("states") == 2:
        return total + lax.ppermute(total, "states", [(0, 1), (1, 0)])
    return lax.psum(total, "states")


def solution(mesh):
    in_specs = (
        P(("groups", "atoms", "sub"), "states"),
        P(("groups", "states")),
        P(("groups", "states")),
        P(None, ("groups", "atoms", "sub")),
        P(None, None, ("groups", "atoms", "sub")),
        P(None, None, ("groups", "atoms", "sub")),
    )
    out_specs = P(None, ("groups", "atoms", "sub"))
    return jax.shard_map(local, mesh=mesh, in_specs=in_specs, out_specs=out_specs, check_vma=False)
```

```python
import functools

import jax
import jax.numpy as jnp
from jax import lax
from jax.experimental import pallas as pl
from jax.experimental.pallas import tpu as pltpu
from jax.sharding import PartitionSpec as P

LANES = 128
BLOCK = 64
UPPER = 48
SHARD = ("atoms", "sub")


def split(value):
    high = value.astype(jnp.bfloat16)
    return high, (value - high.astype(jnp.float32)).astype(jnp.bfloat16)


def gram(left_high, left_low, right_high, right_low):
    dot = functools.partial(
        lax.dot_general,
        dimension_numbers=(((1,), (1,)), ((), ())),
        preferred_element_type=jnp.float32,
    )
    return (
        dot(left_high, right_high) + dot(left_high, right_low) + dot(left_low, right_high)
    )


def lane_numbers():
    return lax.broadcasted_iota(jnp.int32, (8, LANES), 1)


def swap_halves(value):
    return pltpu.roll(value, BLOCK, 1)


def side_by_side(left, right, odd):
    if odd:
        return jnp.where(lane_numbers() < BLOCK, swap_halves(left), right)
    return jnp.where(lane_numbers() < BLOCK, left, swap_halves(right))


def pick_pairs(gram_ref, column, size, index, deriv, blocks=1):
    low = [part & 7 for part in index]
    high = [part >> 3 for part in index]
    pair = [[None, None] for k in range(3)]
    for x in range(2):
        picked = {}
        for r in range(size // 8 * blocks):
            hit = [part == r for part in high]
            for b in range(4):
                block, part = divmod(r, size // 8)
                row = ((block * 2 + x) * 4 + b) * size + part * 8
                for g in range(2):
                    at = column + g * LANES
                    tile = gram_ref[row : row + 8, at : at + LANES]
                    for half in range(2):
                        got = jnp.take_along_axis(tile, low[half], axis=0)
                        before = picked.get((b, g, half), 0.0)
                        picked[b, g, half] = jnp.where(hit[half], got, before)
        for (b, g, half), value in picked.items():
            for k in range(3):
                term = value * deriv(k, x, b, g, half)
                if pair[k][half] is None:
                    pair[k][half] = term
                else:
                    pair[k][half] = pair[k][half] - term if x else pair[k][half] + term
    return pair


def fold(pair):
    return [[value + swap_halves(value) for value in parts] for parts in pair]


def merge(even, odd):
    left = lane_numbers() < BLOCK
    return [[jnp.where(left, even[k][half], odd[k][half]) for half in range(2)] for k in range(3)]


def slot_sum(pair):
    return [jnp.sum(pair[k][0] + pair[k][1], axis=0, keepdims=True) for k in range(3)]


def spread(index_ref, pair, spread_ref, rows):
    lane_rows = lax.broadcasted_iota(jnp.int32, (8, LANES), 0)
    for r in range(rows // 8):
        slot = jnp.full((8, LANES), 16, jnp.int32)
        for n in range(16):
            hit = jnp.broadcast_to(index_ref[n : n + 1, :], (8, LANES)) == lane_rows + 8 * r
            slot = jnp.where(hit, n, slot)
        low = slot & 7
        for k in range(3):
            first = jnp.take_along_axis(pair[k][0], low, axis=0)
            second = jnp.take_along_axis(pair[k][1], low, axis=0)
            value = jnp.where(slot < 8, first, jnp.where(slot < 16, second, 0.0))
            spread_ref[k, 8 * r : 8 * r + 8, :] = value
    ones = jnp.ones((8, LANES), jnp.float32)
    out = []
    for k in range(3):
        total = lax.dot_general(
            ones,
            spread_ref[k, :rows, :],
            (((1,), (1,)), ((), ())),
            precision=lax.Precision.HIGHEST,
            preferred_element_type=jnp.float32,
        )
        out.append(total[:1])
    return out


def own_deriv(dham_ref, dovl_ref, tile, odd):
    def deriv(k, x, b, g, half):
        ref = (dham_ref, dovl_ref)[x]
        parts = [
            ref[k * 16 + (2 * g + parity) * 4 + b, 8 * half : 8 * half + 8, tile * LANES : (tile + 1) * LANES]
            for parity in range(2)
        ]
        return side_by_side(parts[0], parts[1], odd)

    return deriv


def block_index(index_ref, odd):
    return [
        side_by_side(index_ref[8 * half : 8 * half + 8, :], index_ref[8 * half : 8 * half + 8, :], odd)
        for half in range(2)
    ]


def inner_kernel(
    start_ref, coeffs_ref, occup_ref, energies_ref, nbr_ref, dham_ref, dovl_ref,
    own_high_ref, own_low_ref, near1_high_ref, near1_low_ref, force_ref,
    near0_high_ref, near0_low_ref, near2_high_ref, near2_low_ref, near3_high_ref, near3_low_ref,
    gram0_ref, gram1_ref, gram2_ref, gram3_ref, index_ref, spread_ref, columns_ref, copy_sem,
):
    states = coeffs_ref.shape[1]
    count = states // LANES
    near = [
        (near0_high_ref, near0_low_ref),
        (near1_high_ref, near1_low_ref),
        (near2_high_ref, near2_low_ref),
        (near3_high_ref, near3_low_ref),
    ]
    grams = [gram0_ref, gram1_ref, gram2_ref, gram3_ref]
    copies = [
        pltpu.make_async_copy(
            coeffs_ref.at[:, c * LANES : (c + 1) * LANES], columns_ref.at[c], copy_sem.at[c]
        )
        for c in range(count)
    ]
    for copy in copies:
        copy.start()
    occup = occup_ref[...]
    weights = [occup, occup * energies_ref[...]]

    for c, copy in enumerate(copies):
        copy.wait()
        lanes = slice(c * LANES, (c + 1) * LANES)
        for j in range(4):
            for a in range(4):
                rows = columns_ref[c, pl.ds(j * 256 + a, BLOCK, stride=4), :]
                own = slice(j * 256 + a * BLOCK, j * 256 + (a + 1) * BLOCK)
                own_high_ref[own, lanes], own_low_ref[own, lanes] = split(rows)
                for x in range(2):
                    at = slice(x * 256 + a * BLOCK, x * 256 + (a + 1) * BLOCK)
                    near[j][0][at, lanes], near[j][1][at, lanes] = split(rows * weights[x][:, lanes])

    def multiply(h):
        own = slice(h * 256, h * 256 + 256)
        for j in range(h, min(h + 3, 4)):
            grams[h][(j - h) * 512 : (j - h) * 512 + 512, :] = gram(
                near[j][0][...], near[j][1][...], own_high_ref[own, :], own_low_ref[own, :]
            )

    for tile in range(2):
        index_ref[tile] = nbr_ref[:, tile * LANES : (tile + 1) * LANES] - (start_ref[0] + tile * LANES)

    def pick(h):
        index = [part - BLOCK * (h % 2) for part in block_index(index_ref.at[h // 2], h % 2)]
        blocks = min(h + 3, 4) - h
        return fold(pick_pairs(grams[h], 0, BLOCK, index, own_deriv(dham_ref, dovl_ref, h // 2, h % 2), blocks))

    def finish(tile, even, odd):
        pair = merge(even, odd)
        mine = slot_sum(pair)
        rows = 256 - tile * LANES
        theirs = spread(index_ref.at[tile], pair, spread_ref, rows)
        return mine, theirs

    for h in (3, 2, 1, 0):
        multiply(h)
    pair3 = pick(3)
    pair2 = pick(2)
    mine1, theirs1 = finish(1, pair2, pair3)
    pair1 = pick(1)
    pair0 = pick(0)
    mine0, theirs0 = finish(0, pair0, pair1)
    force_ref[...] = jnp.zeros_like(force_ref)
    for k in range(3):
        force_ref[k : k + 1, :LANES] = 2.0 * (theirs0[k][:, :LANES] - mine0[k])
        force_ref[k : k + 1, LANES:] = 2.0 * (theirs0[k][:, LANES:] + theirs1[k] - mine1[k])


def payload_rows(atoms, states):
    planes = -(-48 // (states // LANES))
    return max(4 * (atoms // 2 - UPPER), 4 * UPPER + 16 * planes + 16)


def pack_kernel(
    start_ref, coeffs_ref, nbr_ref, dham_ref, dovl_ref, core_ref, far_ref,
    ham_ref, ovl_ref, last_ref, core_sem, far_sem, deriv_sem,
):
    atoms = nbr_ref.shape[1]
    count, rows, unused = core_ref.shape
    lower = 4 * (atoms // 2 - UPPER)
    first = ((start_ref[0] // atoms) & 1) == 0
    fetched = [
        pltpu.make_async_copy(source.at[:, :, atoms - LANES :], target, deriv_sem.at[at])
        for at, (source, target) in enumerate([(dham_ref, ham_ref), (dovl_ref, ovl_ref)])
    ]
    fetched.append(
        pltpu.make_async_copy(nbr_ref.at[:, atoms - LANES :], last_ref, deriv_sem.at[2])
    )

    def fill(up_ref, up_sem, down_ref, down_sem):
        copies = []
        for c in range(count):
            lanes = slice(c * LANES, (c + 1) * LANES)
            up_rows = coeffs_ref.at[4 * (atoms - UPPER) :, lanes]
            copies.append(pltpu.make_async_copy(up_rows, up_ref.at[c, : 4 * UPPER, :], up_sem.at[c]))
            down_rows = coeffs_ref.at[:lower, lanes]
            copies.append(pltpu.make_async_copy(down_rows, down_ref.at[c, :lower, :], down_sem.at[c]))
        for copy in fetched + copies:
            copy.start()
        if rows > lower:
            down_ref[:, lower:, :] = jnp.zeros((count, rows - lower, LANES), jnp.float32)
        up_ref[:, 4 * UPPER :, :] = jnp.zeros((count, rows - 4 * UPPER, LANES), jnp.float32)
        planes = -(-48 // count)
        for copy in fetched:
            copy.wait()
        last = last_ref[...]
        target = jnp.where(last >= 0, last - (start_ref[0] + atoms), -1).astype(jnp.float32)
        at = 4 * UPPER + 16 * planes
        for half in range(2):
            part = target[8 * half : 8 * half + 8]
            up_ref[0, at + 8 * half : at + 8 * half + 8, :] = side_by_side(part, part, 1)
        for x, ref in enumerate((ham_ref, ovl_ref)):
            for k in range(3):
                for g in range(2):
                    for b in range(4):
                        plane = x * 24 + k * 8 + g * 4 + b
                        for half in range(2):
                            parts = [
                                ref[k * 16 + (2 * g + parity) * 4 + b, 8 * half : 8 * half + 8, :]
                                for parity in range(2)
                            ]
                            at = 4 * UPPER + 16 * (plane // count) + 8 * half
                            up_ref[plane % count, at : at + 8, :] = side_by_side(parts[0], parts[1], 1)
        for copy in copies:
            copy.wait()

    @pl.when(first)
    def even():
        fill(core_ref, core_sem, far_ref, far_sem)

    @pl.when(jnp.logical_not(first))
    def odd():
        fill(far_ref, far_sem, core_ref, core_sem)


def cross_kernel(
    parity,
    start_ref, payload_ref, before_ref, occup_ref, energies_ref, nbr_ref, dham_ref, dovl_ref,
    own_high_ref, own_low_ref, near_high_ref, near_low_ref,
    force_ref, sent_ref,
    cut_high_ref, cut_low_ref, gram_ref, index_ref, spread_ref,
):
    atoms = nbr_ref.shape[1]
    count = payload_ref.shape[0]
    lower = atoms // 2 - UPPER
    force_ref[...] = before_ref[...]
    sent_ref[...] = jnp.zeros_like(sent_ref)
    first = ((start_ref[0] // atoms) & 1) == parity

    @pl.when(first)
    def above():
        occup = occup_ref[...]
        weights = [occup, occup * energies_ref[...]]
        for c in range(count):
            lanes = slice(c * LANES, (c + 1) * LANES)
            for b in range(4):
                rows = payload_ref[c, pl.ds(b, lower, stride=4), :]
                for x in range(2):
                    at = slice((x * 4 + b) * lower, (x * 4 + b + 1) * lower)
                    cut_high_ref[at, lanes], cut_low_ref[at, lanes] = split(rows * weights[x][:, lanes])
        gram_ref[...] = gram(
            cut_high_ref[...], cut_low_ref[...], own_high_ref[512:, :], own_low_ref[512:, :]
        )
        index_ref[...] = nbr_ref[:, LANES:] - (start_ref[0] + atoms)
        even, odd = (
            fold(
                pick_pairs(
                    gram_ref, h * 256, lower, block_index(index_ref, h), own_deriv(dham_ref, dovl_ref, 1, h)
                )
            )
            for h in range(2)
        )
        pair = merge(even, odd)
        mine = slot_sum(pair)
        theirs = spread(index_ref, pair, spread_ref, lower)
        for k in range(3):
            force_ref[k : k + 1, LANES:] += -2.0 * mine[k]
            sent_ref[k : k + 1, :lower] = 2.0 * theirs[k]

    @pl.when(jnp.logical_not(first))
    def below():
        skip = BLOCK - UPPER
        for c in range(count):
            lanes = slice(c * LANES, (c + 1) * LANES)
            for a in range(4):
                rows = payload_ref[c, pl.ds(a, UPPER, stride=4), :]
                at = slice(a * BLOCK + skip, (a + 1) * BLOCK)
                cut_high_ref[at, lanes], cut_low_ref[at, lanes] = split(rows)
                at = slice(a * BLOCK, a * BLOCK + skip)
                cut_high_ref[at, lanes] = jnp.zeros((skip, LANES), jnp.bfloat16)
                cut_low_ref[at, lanes] = jnp.zeros((skip, LANES), jnp.bfloat16)
        gram_ref[:512, :256] = gram(
            near_high_ref[...], near_low_ref[...], cut_high_ref[:256, :], cut_low_ref[:256, :]
        )
        planes = -(-48 // count)
        at = 4 * UPPER + 16 * planes
        target = payload_ref[0, at : at + 16, :].astype(jnp.int32)
        index_ref[...] = jnp.where(target >= lower, target - BLOCK, -1)
        index = [index_ref[8 * half : 8 * half + 8, :] for half in range(2)]

        def deriv(k, x, b, g, half):
            plane = x * 24 + k * 8 + g * 4 + b
            at = 4 * UPPER + 16 * (plane // count) + 8 * half
            return payload_ref[plane % count, at : at + 8, :]

        pair = pick_pairs(gram_ref, 0, BLOCK, index, deriv)
        theirs = spread(index_ref, pair, spread_ref, BLOCK)
        mine = slot_sum(fold(pair))
        for k in range(3):
            force_ref[k : k + 1, BLOCK:LANES] += 2.0 * theirs[k]
            sent_ref[k : k + 1, atoms - BLOCK :] = -2.0 * mine[k][:, BLOCK:]


def in_hbm(value):
    return pltpu.with_memory_space_constraint(value, pltpu.HBM)


def core_swap(value):
    return lax.ppermute(value, "sub", [(0, 1), (1, 0)])


def shard_swap(value):
    count = lax.axis_size(SHARD)
    pairs = [pair for at in range(1, count - 1, 2) for pair in ((at, at + 1), (at + 1, at))]
    return lax.ppermute(value, SHARD, pairs)


def local(coeffs, occup, energies, nbr, dham, dovl):
    slots, atoms = nbr.shape
    states = coeffs.shape[1]
    start = (lax.axis_index(SHARD) * atoms).reshape(1).astype(jnp.int32)
    occup = occup.reshape(1, states)
    energies = energies.reshape(1, states)
    count = states // LANES

    vmem = pl.BlockSpec(memory_space=pltpu.VMEM)
    hbm = pl.BlockSpec(memory_space=pltpu.HBM)
    smem = pl.BlockSpec(memory_space=pltpu.SMEM)
    half = jax.ShapeDtypeStruct((512, states), jnp.bfloat16)
    whole = jax.ShapeDtypeStruct((4 * atoms, states), jnp.bfloat16)
    force = jax.ShapeDtypeStruct((8, atoms), jnp.float32)
    prepared = pltpu.VMEM((512, states), jnp.bfloat16)
    lower = atoms // 2 - UPPER
    payload = jax.ShapeDtypeStruct((count, payload_rows(atoms, states), LANES), jnp.float32)
    core_payload, far_payload = pl.pallas_call(
        pack_kernel,
        out_shape=(payload, payload),
        in_specs=[smem] + [hbm] * 4,
        out_specs=(vmem, vmem),
        scratch_shapes=[
            pltpu.VMEM((48, slots, LANES), jnp.float32),
            pltpu.VMEM((48, slots, LANES), jnp.float32),
            pltpu.VMEM((slots, LANES), jnp.int32),
            pltpu.SemaphoreType.DMA((count,)),
            pltpu.SemaphoreType.DMA((count,)),
            pltpu.SemaphoreType.DMA((3,)),
        ],
        compiler_params=pltpu.CompilerParams(vmem_limit_bytes=12 * 1024 * 1024),
        name="pack",
    )(start, *(in_hbm(value) for value in (coeffs, nbr, dham, dovl)))
    far_payload = shard_swap(far_payload)
    core_payload = core_swap(core_payload)
    own_high, own_low, near_high, near_low, inner = pl.pallas_call(
        inner_kernel,
        out_shape=(whole, whole, half, half, force),
        in_specs=[smem, hbm] + [vmem] * 5,
        out_specs=(vmem,) * 5,
        scratch_shapes=[prepared] * 6
        + [pltpu.VMEM((512 * n, 256), jnp.float32) for n in (3, 3, 2, 1)]
        + [
            pltpu.VMEM((2, slots, LANES), jnp.int32),
            pltpu.VMEM((3, atoms, LANES), jnp.float32),
            pltpu.VMEM((states // LANES, 4 * atoms, LANES), jnp.float32),
            pltpu.SemaphoreType.DMA((count,)),
        ],
        compiler_params=pltpu.CompilerParams(vmem_limit_bytes=32 * 1024 * 1024),
        cost_estimate=pl.CostEstimate(
            flops=3 * 2 * 9 * 512 * 256 * states, bytes_accessed=16 * 1024 * 1024, transcendentals=0
        ),
        name="inner_pairs",
    )(start, in_hbm(coeffs), occup, energies, nbr, dham, dovl)

    def cross(parity, payload, before, name):
        cut = pltpu.VMEM((8 * lower, states), jnp.bfloat16)
        return pl.pallas_call(
            functools.partial(cross_kernel, parity),
            out_shape=(force, force),
            in_specs=[smem] + [vmem] * 11,
            out_specs=(vmem, vmem),
            scratch_shapes=[
                cut,
                cut,
                pltpu.VMEM((8 * lower, 512), jnp.float32),
                pltpu.VMEM((slots, LANES), jnp.int32),
                pltpu.VMEM((3, lower, LANES), jnp.float32),
            ],
            compiler_params=pltpu.CompilerParams(vmem_limit_bytes=20 * 1024 * 1024),
            cost_estimate=pl.CostEstimate(
                flops=3 * 2 * 2 * 512 * 256 * states, bytes_accessed=6 * 1024 * 1024, transcendentals=0
            ),
            name=name,
        )(start, payload, before, occup, energies, nbr, dham, dovl, own_high, own_low, near_high, near_low)

    total, core_sent = cross(0, core_payload, inner, "core_pairs")
    core_back = core_swap(core_sent)
    total, far_sent = cross(1, far_payload, total, "far_pairs")
    total = (total + core_back + shard_swap(far_sent))[:3]
    if lax.axis_size("states") == 2:
        return total + lax.ppermute(total, "states", [(0, 1), (1, 0)])
    return lax.psum(total, "states")


def solution(mesh):
    in_specs = (
        P(("groups", "atoms", "sub"), "states"),
        P(("groups", "states")),
        P(("groups", "states")),
        P(None, ("groups", "atoms", "sub")),
        P(None, None, ("groups", "atoms", "sub")),
        P(None, None, ("groups", "atoms", "sub")),
    )
    out_specs = P(None, ("groups", "atoms", "sub"))
    return jax.shard_map(local, mesh=mesh, in_specs=in_specs, out_specs=out_specs, check_vma=False)
```

```python
import functools

import jax
import jax.numpy as jnp
from jax import lax
from jax.experimental import pallas as pl
from jax.experimental.pallas import tpu as pltpu
from jax.sharding import PartitionSpec as P

LANES = 128
BLOCK = 64
UPPER = 48
SHARD = ("atoms", "sub")


def split(value):
    high = value.astype(jnp.bfloat16)
    return high, (value - high.astype(jnp.float32)).astype(jnp.bfloat16)


def gram(left_high, left_low, right_high, right_low):
    dot = functools.partial(
        lax.dot_general,
        dimension_numbers=(((1,), (1,)), ((), ())),
        preferred_element_type=jnp.float32,
    )
    return (
        dot(left_high, right_high) + dot(left_high, right_low) + dot(left_low, right_high)
    )


def lane_numbers():
    return lax.broadcasted_iota(jnp.int32, (8, LANES), 1)


def swap_halves(value):
    return pltpu.roll(value, BLOCK, 1)


def side_by_side(left, right, odd):
    if odd:
        return jnp.where(lane_numbers() < BLOCK, swap_halves(left), right)
    return jnp.where(lane_numbers() < BLOCK, left, swap_halves(right))


def pick_pairs(tile, steps, index, deriv):
    low = [part & 7 for part in index]
    high = [part >> 3 for part in index]
    pair = [[None, None] for k in range(3)]
    for x in range(2):
        picked = {}
        for r in range(steps):
            hit = [part == r for part in high]
            for b in range(4):
                for g in range(2):
                    rows = tile(r, x, b, g)
                    for half in range(2):
                        got = jnp.take_along_axis(rows, low[half], axis=0)
                        before = picked.get((b, g, half), 0.0)
                        picked[b, g, half] = jnp.where(hit[half], got, before)
        for (b, g, half), value in picked.items():
            for k in range(3):
                term = value * deriv(k, x, b, g, half)
                if pair[k][half] is None:
                    pair[k][half] = term
                else:
                    pair[k][half] = pair[k][half] - term if x else pair[k][half] + term
    return pair


def tiles(gram_ref, column, size):
    def tile(r, x, b, g):
        block, part = divmod(r, size // 8)
        row = ((block * 2 + x) * 4 + b) * size + part * 8
        return gram_ref[row : row + 8, column + g * LANES : column + (g + 1) * LANES]

    return tile


def fold(pair):
    return [[value + swap_halves(value) for value in parts] for parts in pair]


def merge(even, odd):
    left = lane_numbers() < BLOCK
    return [[jnp.where(left, even[k][half], odd[k][half]) for half in range(2)] for k in range(3)]


def slot_sum(pair):
    return [jnp.sum(pair[k][0] + pair[k][1], axis=0, keepdims=True) for k in range(3)]


def slot_map(index_ref, r):
    target = lax.broadcasted_iota(jnp.int32, (8, LANES), 0) + 8 * r
    slot = jnp.full((8, LANES), 16, jnp.int32)
    for n in range(16):
        hit = jnp.broadcast_to(index_ref[n : n + 1, :], (8, LANES)) == target
        slot = jnp.where(hit, n, slot)
    return slot


def spread(slot, pair, spread_ref, rows):
    for r in range(rows // 8):
        slots = slot(r)
        low = slots & 7
        for k in range(3):
            first = jnp.take_along_axis(pair[k][0], low, axis=0)
            second = jnp.take_along_axis(pair[k][1], low, axis=0)
            value = jnp.where(slots < 8, first, jnp.where(slots < 16, second, 0.0))
            spread_ref[k, 8 * r : 8 * r + 8, :] = value
    ones = jnp.ones((8, LANES), jnp.float32)
    out = []
    for k in range(3):
        total = lax.dot_general(
            ones,
            spread_ref[k, :rows, :],
            (((1,), (1,)), ((), ())),
            precision=lax.Precision.HIGHEST,
            preferred_element_type=jnp.float32,
        )
        out.append(total[:1])
    return out


def deriv_at(k, x, b, g, half):
    return (((k * 2 + x) * 4 + b) * 2 + g) * 2 + half


def block_index(index_ref, odd):
    return [
        side_by_side(index_ref[8 * half : 8 * half + 8, :], index_ref[8 * half : 8 * half + 8, :], odd)
        for half in range(2)
    ]


def inner_kernel(
    start_ref, coeffs_ref, occup_ref, energies_ref, nbr_ref, dham_ref, dovl_ref,
    own_high_ref, own_low_ref, near1_high_ref, near1_low_ref, force_ref, deriv_ref, slot_ref,
    near0_high_ref, near0_low_ref, near2_high_ref, near2_low_ref, near3_high_ref, near3_low_ref,
    gram0_ref, gram1_ref, gram2_ref, gram3_ref, index_ref, spread_ref, columns_ref, copy_sem,
):
    states = coeffs_ref.shape[1]
    count = states // LANES
    near = [
        (near0_high_ref, near0_low_ref),
        (near1_high_ref, near1_low_ref),
        (near2_high_ref, near2_low_ref),
        (near3_high_ref, near3_low_ref),
    ]
    grams = [gram0_ref, gram1_ref, gram2_ref, gram3_ref]
    copies = [
        pltpu.make_async_copy(
            coeffs_ref.at[:, c * LANES : (c + 1) * LANES], columns_ref.at[c], copy_sem.at[c]
        )
        for c in range(count)
    ]
    for copy in copies:
        copy.start()
    occup = occup_ref[...]
    weights = [occup, occup * energies_ref[...]]

    for tile in range(2):
        index_ref[tile] = nbr_ref[:, tile * LANES : (tile + 1) * LANES] - (start_ref[0] + tile * LANES)
    for h in range(4):
        lanes = slice(h // 2 * LANES, (h // 2 + 1) * LANES)
        for x, ref in enumerate((dham_ref, dovl_ref)):
            for k in range(3):
                for b in range(4):
                    for g in range(2):
                        for half in range(2):
                            parts = [
                                ref[k * 16 + (2 * g + parity) * 4 + b, 8 * half : 8 * half + 8, lanes]
                                for parity in range(2)
                            ]
                            at = deriv_at(k, x, b, g, half)
                            deriv_ref[h, at] = side_by_side(parts[0], parts[1], h % 2)
    for r in range(32):
        slot_ref[r] = slot_map(index_ref.at[0], r)
    for r in range(32 - UPPER // 8):
        slot_ref[32 + r] = slot_map(index_ref.at[1], r)
    for c, copy in enumerate(copies):
        copy.wait()
        lanes = slice(c * LANES, (c + 1) * LANES)
        for j in range(4):
            for a in range(4):
                rows = columns_ref[c, pl.ds(j * 256 + a, BLOCK, stride=4), :]
                own = slice(j * 256 + a * BLOCK, j * 256 + (a + 1) * BLOCK)
                own_high_ref[own, lanes], own_low_ref[own, lanes] = split(rows)
                for x in range(2):
                    at = slice(x * 256 + a * BLOCK, x * 256 + (a + 1) * BLOCK)
                    near[j][0][at, lanes], near[j][1][at, lanes] = split(rows * weights[x][:, lanes])

    def multiply(h):
        own = slice(h * 256, h * 256 + 256)
        for j in range(h, min(h + 3, 4)):
            grams[h][(j - h) * 512 : (j - h) * 512 + 512, :] = gram(
                near[j][0][...], near[j][1][...], own_high_ref[own, :], own_low_ref[own, :]
            )

    def pick(h):
        index = [part - BLOCK * (h % 2) for part in block_index(index_ref.at[h // 2], h % 2)]
        steps = (min(h + 3, 4) - h) * BLOCK // 8
        return fold(
            pick_pairs(tiles(grams[h], 0, BLOCK), steps, index, lambda *key: deriv_ref[h, deriv_at(*key)])
        )

    def finish(tile, even, odd):
        pair = merge(even, odd)
        mine = slot_sum(pair)
        theirs = spread(lambda r: slot_ref[32 * tile + r], pair, spread_ref, 256 - tile * LANES)
        return mine, theirs

    for h in (3, 2, 1, 0):
        multiply(h)
    pair3 = pick(3)
    pair2 = pick(2)
    mine1, theirs1 = finish(1, pair2, pair3)
    pair1 = pick(1)
    pair0 = pick(0)
    mine0, theirs0 = finish(0, pair0, pair1)
    force_ref[...] = jnp.zeros_like(force_ref)
    for k in range(3):
        force_ref[k : k + 1, :LANES] = 2.0 * (theirs0[k][:, :LANES] - mine0[k])
        force_ref[k : k + 1, LANES:] = 2.0 * (theirs0[k][:, LANES:] + theirs1[k] - mine1[k])


def payload_rows(atoms, states):
    planes = -(-48 // (states // LANES))
    return max(4 * (atoms // 2 - UPPER), 4 * UPPER + 16 * planes + 16)


def pack_kernel(
    start_ref, coeffs_ref, nbr_ref, dham_ref, dovl_ref, core_ref, far_ref,
    ham_ref, ovl_ref, last_ref, core_sem, far_sem, deriv_sem,
):
    atoms = nbr_ref.shape[1]
    count, rows, unused = core_ref.shape
    lower = 4 * (atoms // 2 - UPPER)
    first = ((start_ref[0] // atoms) & 1) == 0
    fetched = [
        pltpu.make_async_copy(source.at[:, :, atoms - LANES :], target, deriv_sem.at[at])
        for at, (source, target) in enumerate([(dham_ref, ham_ref), (dovl_ref, ovl_ref)])
    ]
    fetched.append(
        pltpu.make_async_copy(nbr_ref.at[:, atoms - LANES :], last_ref, deriv_sem.at[2])
    )

    def fill(up_ref, up_sem, down_ref, down_sem):
        copies = []
        for c in range(count):
            lanes = slice(c * LANES, (c + 1) * LANES)
            up_rows = coeffs_ref.at[4 * (atoms - UPPER) :, lanes]
            copies.append(pltpu.make_async_copy(up_rows, up_ref.at[c, : 4 * UPPER, :], up_sem.at[c]))
            down_rows = coeffs_ref.at[:lower, lanes]
            copies.append(pltpu.make_async_copy(down_rows, down_ref.at[c, :lower, :], down_sem.at[c]))
        for copy in fetched + copies:
            copy.start()
        if rows > lower:
            down_ref[:, lower:, :] = jnp.zeros((count, rows - lower, LANES), jnp.float32)
        up_ref[:, 4 * UPPER :, :] = jnp.zeros((count, rows - 4 * UPPER, LANES), jnp.float32)
        planes = -(-48 // count)
        for copy in fetched:
            copy.wait()
        last = last_ref[...]
        target = jnp.where(last >= 0, last - (start_ref[0] + atoms), -1).astype(jnp.float32)
        at = 4 * UPPER + 16 * planes
        for half in range(2):
            part = target[8 * half : 8 * half + 8]
            up_ref[0, at + 8 * half : at + 8 * half + 8, :] = side_by_side(part, part, 1)
        for x, ref in enumerate((ham_ref, ovl_ref)):
            for k in range(3):
                for g in range(2):
                    for b in range(4):
                        plane = x * 24 + k * 8 + g * 4 + b
                        for half in range(2):
                            parts = [
                                ref[k * 16 + (2 * g + parity) * 4 + b, 8 * half : 8 * half + 8, :]
                                for parity in range(2)
                            ]
                            at = 4 * UPPER + 16 * (plane // count) + 8 * half
                            up_ref[plane % count, at : at + 8, :] = side_by_side(parts[0], parts[1], 1)
        for copy in copies:
            copy.wait()

    @pl.when(first)
    def even():
        fill(core_ref, core_sem, far_ref, far_sem)

    @pl.when(jnp.logical_not(first))
    def odd():
        fill(far_ref, far_sem, core_ref, core_sem)


def cross_kernel(
    parity,
    start_ref, payload_ref, before_ref, occup_ref, energies_ref, nbr_ref, deriv_ref, slot_ref,
    own_high_ref, own_low_ref, near_high_ref, near_low_ref,
    force_ref, sent_ref,
    cut_high_ref, cut_low_ref, gram_ref, index_ref, spread_ref,
):
    atoms = nbr_ref.shape[1]
    count = payload_ref.shape[0]
    lower = atoms // 2 - UPPER
    force_ref[...] = before_ref[...]
    sent_ref[...] = jnp.zeros_like(sent_ref)
    first = ((start_ref[0] // atoms) & 1) == parity

    @pl.when(first)
    def above():
        occup = occup_ref[...]
        weights = [occup, occup * energies_ref[...]]
        extra = lower - BLOCK
        for c in range(count):
            lanes = slice(c * LANES, (c + 1) * LANES)
            for b in range(4):
                rows = payload_ref[c, pl.ds(b, BLOCK, stride=4), :]
                for x in range(2):
                    at = slice((x * 4 + b) * BLOCK, (x * 4 + b + 1) * BLOCK)
                    cut_high_ref[at, lanes], cut_low_ref[at, lanes] = split(rows * weights[x][:, lanes])
                rows = payload_ref[c, pl.ds(4 * BLOCK + b, extra, stride=4), :]
                for x in range(2):
                    at = slice(512 + (x * 4 + b) * extra, 512 + (x * 4 + b + 1) * extra)
                    cut_high_ref[at, lanes], cut_low_ref[at, lanes] = split(rows * weights[x][:, lanes])
        gram_ref[:512, :] = gram(
            cut_high_ref[:512, :], cut_low_ref[:512, :], own_high_ref[512:, :], own_low_ref[512:, :]
        )
        gram_ref[512:, 256:] = gram(
            cut_high_ref[512:, :], cut_low_ref[512:, :], own_high_ref[768:, :], own_low_ref[768:, :]
        )
        index_ref[...] = nbr_ref[:, LANES:] - (start_ref[0] + atoms)
        near_tile = tiles(gram_ref, 256, BLOCK)
        extra_tile = tiles(gram_ref.at[512:, :], 256, extra)

        def odd_tile(r, *key):
            return near_tile(r, *key) if r < BLOCK // 8 else extra_tile(r - BLOCK // 8, *key)

        pairs = [
            pick_pairs(
                (tiles(gram_ref, 0, BLOCK), odd_tile)[h],
                (BLOCK, lower)[h] // 8,
                block_index(index_ref, h),
                lambda *key: deriv_ref[2 + h, deriv_at(*key)],
            )
            for h in range(2)
        ]
        pair = merge(fold(pairs[0]), fold(pairs[1]))
        mine = slot_sum(pair)
        theirs = spread(lambda r: slot_ref[48 + r], pair, spread_ref, lower)
        for k in range(3):
            force_ref[k : k + 1, LANES:] += -2.0 * mine[k]
            sent_ref[k : k + 1, :lower] = 2.0 * theirs[k]

    @pl.when(jnp.logical_not(first))
    def below():
        skip = BLOCK - UPPER
        for c in range(count):
            lanes = slice(c * LANES, (c + 1) * LANES)
            for a in range(4):
                rows = payload_ref[c, pl.ds(a, UPPER, stride=4), :]
                at = slice(a * BLOCK + skip, (a + 1) * BLOCK)
                cut_high_ref[at, lanes], cut_low_ref[at, lanes] = split(rows)
                at = slice(a * BLOCK, a * BLOCK + skip)
                cut_high_ref[at, lanes] = jnp.zeros((skip, LANES), jnp.bfloat16)
                cut_low_ref[at, lanes] = jnp.zeros((skip, LANES), jnp.bfloat16)
        gram_ref[:512, :256] = gram(
            near_high_ref[...], near_low_ref[...], cut_high_ref[:256, :], cut_low_ref[:256, :]
        )
        planes = -(-48 // count)
        at = 4 * UPPER + 16 * planes
        target = payload_ref[0, at : at + 16, :].astype(jnp.int32)
        index_ref[...] = jnp.where(target >= lower, target - BLOCK, -1)
        index = [index_ref[8 * half : 8 * half + 8, :] for half in range(2)]

        def deriv(k, x, b, g, half):
            plane = x * 24 + k * 8 + g * 4 + b
            at = 4 * UPPER + 16 * (plane // count) + 8 * half
            return payload_ref[plane % count, at : at + 8, :]

        pair = pick_pairs(tiles(gram_ref, 0, BLOCK), BLOCK // 8, index, deriv)
        theirs = spread(functools.partial(slot_map, index_ref), pair, spread_ref, BLOCK)
        mine = slot_sum(fold(pair))
        for k in range(3):
            force_ref[k : k + 1, BLOCK:LANES] += 2.0 * theirs[k]
            sent_ref[k : k + 1, atoms - BLOCK :] = -2.0 * mine[k][:, BLOCK:]


def in_hbm(value):
    return pltpu.with_memory_space_constraint(value, pltpu.HBM)


def core_swap(value):
    return lax.ppermute(value, "sub", [(0, 1), (1, 0)])


def shard_swap(value):
    count = lax.axis_size(SHARD)
    pairs = [pair for at in range(1, count - 1, 2) for pair in ((at, at + 1), (at + 1, at))]
    return lax.ppermute(value, SHARD, pairs)


def local(coeffs, occup, energies, nbr, dham, dovl):
    slots, atoms = nbr.shape
    states = coeffs.shape[1]
    start = (lax.axis_index(SHARD) * atoms).reshape(1).astype(jnp.int32)
    occup = occup.reshape(1, states)
    energies = energies.reshape(1, states)
    count = states // LANES

    vmem = pl.BlockSpec(memory_space=pltpu.VMEM)
    hbm = pl.BlockSpec(memory_space=pltpu.HBM)
    smem = pl.BlockSpec(memory_space=pltpu.SMEM)
    half = jax.ShapeDtypeStruct((512, states), jnp.bfloat16)
    whole = jax.ShapeDtypeStruct((4 * atoms, states), jnp.bfloat16)
    force = jax.ShapeDtypeStruct((8, atoms), jnp.float32)
    prepared = pltpu.VMEM((512, states), jnp.bfloat16)
    lower = atoms // 2 - UPPER
    payload = jax.ShapeDtypeStruct((count, payload_rows(atoms, states), LANES), jnp.float32)
    core_payload, far_payload = pl.pallas_call(
        pack_kernel,
        out_shape=(payload, payload),
        in_specs=[smem] + [hbm] * 4,
        out_specs=(vmem, vmem),
        scratch_shapes=[
            pltpu.VMEM((48, slots, LANES), jnp.float32),
            pltpu.VMEM((48, slots, LANES), jnp.float32),
            pltpu.VMEM((slots, LANES), jnp.int32),
            pltpu.SemaphoreType.DMA((count,)),
            pltpu.SemaphoreType.DMA((count,)),
            pltpu.SemaphoreType.DMA((3,)),
        ],
        compiler_params=pltpu.CompilerParams(vmem_limit_bytes=12 * 1024 * 1024),
        name="pack",
    )(start, *(in_hbm(value) for value in (coeffs, nbr, dham, dovl)))
    far_payload = shard_swap(far_payload)
    core_payload = core_swap(core_payload)
    own_high, own_low, near_high, near_low, inner, derivs, slot_maps = pl.pallas_call(
        inner_kernel,
        out_shape=(
            whole, whole, half, half, force,
            jax.ShapeDtypeStruct((4, 96, 8, LANES), jnp.float32),
            jax.ShapeDtypeStruct((64 - UPPER // 8, 8, LANES), jnp.int32),
        ),
        in_specs=[smem, hbm] + [vmem] * 5,
        out_specs=(vmem,) * 7,
        scratch_shapes=[prepared] * 6
        + [pltpu.VMEM((512 * n, 256), jnp.float32) for n in (3, 3, 2, 1)]
        + [
            pltpu.VMEM((2, slots, LANES), jnp.int32),
            pltpu.VMEM((3, atoms, LANES), jnp.float32),
            pltpu.VMEM((states // LANES, 4 * atoms, LANES), jnp.float32),
            pltpu.SemaphoreType.DMA((count,)),
        ],
        compiler_params=pltpu.CompilerParams(vmem_limit_bytes=32 * 1024 * 1024),
        cost_estimate=pl.CostEstimate(
            flops=3 * 2 * 9 * 512 * 256 * states, bytes_accessed=16 * 1024 * 1024, transcendentals=0
        ),
        name="inner_pairs",
    )(start, in_hbm(coeffs), occup, energies, nbr, dham, dovl)

    def cross(parity, payload, before, name):
        cut = pltpu.VMEM((8 * lower, states), jnp.bfloat16)
        return pl.pallas_call(
            functools.partial(cross_kernel, parity),
            out_shape=(force, force),
            in_specs=[smem] + [vmem] * 11,
            out_specs=(vmem, vmem),
            scratch_shapes=[
                cut,
                cut,
                pltpu.VMEM((8 * lower, 512), jnp.float32),
                pltpu.VMEM((slots, LANES), jnp.int32),
                pltpu.VMEM((3, lower, LANES), jnp.float32),
            ],
            compiler_params=pltpu.CompilerParams(vmem_limit_bytes=20 * 1024 * 1024),
            cost_estimate=pl.CostEstimate(
                flops=3 * 2 * 2 * 512 * 256 * states, bytes_accessed=6 * 1024 * 1024, transcendentals=0
            ),
            name=name,
        )(start, payload, before, occup, energies, nbr, derivs, slot_maps, own_high, own_low, near_high, near_low)

    total, core_sent = cross(0, core_payload, inner, "core_pairs")
    core_back = core_swap(core_sent)
    total, far_sent = cross(1, far_payload, total, "far_pairs")
    total = (total + core_back + shard_swap(far_sent))[:3]
    if lax.axis_size("states") == 2:
        return total + lax.ppermute(total, "states", [(0, 1), (1, 0)])
    return lax.psum(total, "states")


def solution(mesh):
    in_specs = (
        P(("groups", "atoms", "sub"), "states"),
        P(("groups", "states")),
        P(("groups", "states")),
        P(None, ("groups", "atoms", "sub")),
        P(None, None, ("groups", "atoms", "sub")),
        P(None, None, ("groups", "atoms", "sub")),
    )
    out_specs = P(None, ("groups", "atoms", "sub"))
    return jax.shard_map(local, mesh=mesh, in_specs=in_specs, out_specs=out_specs, check_vma=False)
```

```python
import functools

import jax
import jax.numpy as jnp
from jax import lax
from jax.experimental import pallas as pl
from jax.experimental.pallas import tpu as pltpu
from jax.sharding import PartitionSpec as P

LANES = 128
BLOCK = 64
UPPER = 48
SHARD = ("atoms", "sub")


def split(value):
    high = value.astype(jnp.bfloat16)
    return high, (value - high.astype(jnp.float32)).astype(jnp.bfloat16)


def gram(left_high, left_low, right_high, right_low):
    dot = functools.partial(
        lax.dot_general,
        dimension_numbers=(((1,), (1,)), ((), ())),
        preferred_element_type=jnp.float32,
    )
    return (
        dot(left_high, right_high) + dot(left_high, right_low) + dot(left_low, right_high)
    )


def lane_numbers():
    return lax.broadcasted_iota(jnp.int32, (8, LANES), 1)


def swap_halves(value):
    return pltpu.roll(value, BLOCK, 1)


def side_by_side(left, right, odd):
    if odd:
        return jnp.where(lane_numbers() < BLOCK, swap_halves(left), right)
    return jnp.where(lane_numbers() < BLOCK, left, swap_halves(right))


def pick_pairs(tile, steps, index, deriv):
    low = [part & 7 for part in index]
    high = [part >> 3 for part in index]
    pair = [[None, None] for k in range(3)]
    for x in range(2):
        picked = {}
        for r in range(steps):
            hit = [part == r for part in high]
            for b in range(4):
                for g in range(2):
                    rows = tile(r, x, b, g)
                    for half in range(2):
                        got = jnp.take_along_axis(rows, low[half], axis=0)
                        before = picked.get((b, g, half), 0.0)
                        picked[b, g, half] = jnp.where(hit[half], got, before)
        for (b, g, half), value in picked.items():
            for k in range(3):
                term = value * deriv(k, x, b, g, half)
                if pair[k][half] is None:
                    pair[k][half] = term
                else:
                    pair[k][half] = pair[k][half] - term if x else pair[k][half] + term
    return pair


def tiles(gram_ref, column, size):
    def tile(r, x, b, g):
        block, part = divmod(r, size // 8)
        row = ((block * 2 + x) * 4 + b) * size + part * 8
        return gram_ref[row : row + 8, column + g * LANES : column + (g + 1) * LANES]

    return tile


def fold(pair):
    return [[value + swap_halves(value) for value in parts] for parts in pair]


def merge(even, odd):
    left = lane_numbers() < BLOCK
    return [[jnp.where(left, even[k][half], odd[k][half]) for half in range(2)] for k in range(3)]


def slot_sum(pair):
    return [jnp.sum(pair[k][0] + pair[k][1], axis=0, keepdims=True) for k in range(3)]


def slot_map(index_ref, r):
    target = lax.broadcasted_iota(jnp.int32, (8, LANES), 0) + 8 * r
    slot = jnp.full((8, LANES), 16, jnp.int32)
    for n in range(16):
        hit = jnp.broadcast_to(index_ref[n : n + 1, :], (8, LANES)) == target
        slot = jnp.where(hit, n, slot)
    return slot


def spread(slot, pair, spread_ref, rows):
    for r in range(rows // 8):
        slots = slot(r)
        low = slots & 7
        for k in range(3):
            first = jnp.take_along_axis(pair[k][0], low, axis=0)
            second = jnp.take_along_axis(pair[k][1], low, axis=0)
            value = jnp.where(slots < 8, first, jnp.where(slots < 16, second, 0.0))
            spread_ref[k, 8 * r : 8 * r + 8, :] = value
    ones = jnp.ones((8, LANES), jnp.float32)
    out = []
    for k in range(3):
        total = lax.dot_general(
            ones,
            spread_ref[k, :rows, :],
            (((1,), (1,)), ((), ())),
            precision=lax.Precision.HIGHEST,
            preferred_element_type=jnp.float32,
        )
        out.append(total[:1])
    return out


def deriv_at(k, x, b, g, half):
    return (((k * 2 + x) * 4 + b) * 2 + g) * 2 + half


def block_index(index_ref, odd):
    return [
        side_by_side(index_ref[8 * half : 8 * half + 8, :], index_ref[8 * half : 8 * half + 8, :], odd)
        for half in range(2)
    ]


def inner_kernel(
    start_ref, coeffs_ref, occup_ref, energies_ref, nbr_ref, dham_ref, dovl_ref,
    own_high_ref, own_low_ref, near1_high_ref, near1_low_ref, force_ref, deriv_ref, slot_ref,
    near0_high_ref, near0_low_ref, near2_high_ref, near2_low_ref, near3_high_ref, near3_low_ref,
    gram0_ref, gram1_ref, gram2_ref, gram3_ref, index_ref, spread_ref, columns_ref, copy_sem,
):
    states = coeffs_ref.shape[1]
    count = states // LANES
    near = [
        (near0_high_ref, near0_low_ref),
        (near1_high_ref, near1_low_ref),
        (near2_high_ref, near2_low_ref),
        (near3_high_ref, near3_low_ref),
    ]
    grams = [gram0_ref, gram1_ref, gram2_ref, gram3_ref]
    copies = [
        pltpu.make_async_copy(
            coeffs_ref.at[:, c * LANES : (c + 1) * LANES], columns_ref.at[c], copy_sem.at[c]
        )
        for c in range(count)
    ]
    for copy in copies:
        copy.start()
    occup = occup_ref[...]
    weights = [occup, occup * energies_ref[...]]

    for tile in range(2):
        index_ref[tile] = nbr_ref[:, tile * LANES : (tile + 1) * LANES] - (start_ref[0] + tile * LANES)
    for h in range(4):
        lanes = slice(h // 2 * LANES, (h // 2 + 1) * LANES)
        for x, ref in enumerate((dham_ref, dovl_ref)):
            for k in range(3):
                for b in range(4):
                    for g in range(2):
                        for half in range(2):
                            parts = [
                                ref[k * 16 + (2 * g + parity) * 4 + b, 8 * half : 8 * half + 8, lanes]
                                for parity in range(2)
                            ]
                            at = deriv_at(k, x, b, g, half)
                            deriv_ref[h, at] = side_by_side(parts[0], parts[1], h % 2)
    for r in range(32):
        slot_ref[r] = slot_map(index_ref.at[0], r)
    for r in range(32):
        slot_ref[32 + r] = slot_map(index_ref.at[1], r)
    for c, copy in enumerate(copies):
        copy.wait()
        lanes = slice(c * LANES, (c + 1) * LANES)
        for j in range(4):
            for a in range(4):
                rows = columns_ref[c, pl.ds(j * 256 + a, BLOCK, stride=4), :]
                own = slice(j * 256 + a * BLOCK, j * 256 + (a + 1) * BLOCK)
                own_high_ref[own, lanes], own_low_ref[own, lanes] = split(rows)
                for x in range(2):
                    at = slice(x * 256 + a * BLOCK, x * 256 + (a + 1) * BLOCK)
                    near[j][0][at, lanes], near[j][1][at, lanes] = split(rows * weights[x][:, lanes])

    def multiply(h):
        own = slice(h * 256, h * 256 + 256)
        for j in range(h, min(h + 3, 4)):
            grams[h][(j - h) * 512 : (j - h) * 512 + 512, :] = gram(
                near[j][0][...], near[j][1][...], own_high_ref[own, :], own_low_ref[own, :]
            )

    def pick(h):
        index = [part - BLOCK * (h % 2) for part in block_index(index_ref.at[h // 2], h % 2)]
        steps = (min(h + 3, 4) - h) * BLOCK // 8
        return fold(
            pick_pairs(tiles(grams[h], 0, BLOCK), steps, index, lambda *key: deriv_ref[h, deriv_at(*key)])
        )

    def finish(tile, even, odd):
        pair = merge(even, odd)
        mine = slot_sum(pair)
        theirs = spread(lambda r: slot_ref[32 * tile + r], pair, spread_ref, 256 - tile * LANES)
        return mine, theirs

    for h in (3, 2, 1, 0):
        multiply(h)
    pair3 = pick(3)
    pair2 = pick(2)
    mine1, theirs1 = finish(1, pair2, pair3)
    pair1 = pick(1)
    pair0 = pick(0)
    mine0, theirs0 = finish(0, pair0, pair1)
    force_ref[...] = jnp.zeros_like(force_ref)
    for k in range(3):
        force_ref[k : k + 1, :LANES] = 2.0 * (theirs0[k][:, :LANES] - mine0[k])
        force_ref[k : k + 1, LANES:] = 2.0 * (theirs0[k][:, LANES:] + theirs1[k] - mine1[k])


def payload_rows(atoms, states):
    planes = -(-48 // (states // LANES))
    return max(4 * (atoms // 2 - UPPER), 4 * UPPER + 16 * planes + 16)


def is_lower(start_ref, atoms):
    return ((start_ref[0] // atoms) & 1) == 0


def far_pack_kernel(
    start_ref, coeffs_ref, nbr_ref, dham_ref, dovl_ref, far_ref,
    ham_ref, ovl_ref, last_ref, rows_sem, deriv_sem,
):
    atoms = nbr_ref.shape[1]
    count, rows, unused = far_ref.shape
    lower = 4 * (atoms // 2 - UPPER)

    def copy_rows(first, size):
        copies = [
            pltpu.make_async_copy(
                coeffs_ref.at[first : first + size, c * LANES : (c + 1) * LANES],
                far_ref.at[c, :size, :],
                rows_sem.at[c],
            )
            for c in range(count)
        ]
        for copy in copies:
            copy.start()
        if rows > size:
            far_ref[:, size:, :] = jnp.zeros((count, rows - size, LANES), jnp.float32)
        return copies

    @pl.when(is_lower(start_ref, atoms))
    def down():
        for copy in copy_rows(0, lower):
            copy.wait()

    @pl.when(jnp.logical_not(is_lower(start_ref, atoms)))
    def up():
        sources = ((dham_ref.at[:, :, atoms - LANES :], ham_ref), (dovl_ref.at[:, :, atoms - LANES :], ovl_ref))
        sources += ((nbr_ref.at[:, atoms - LANES :], last_ref),)
        fetched = [
            pltpu.make_async_copy(source, target, deriv_sem.at[at])
            for at, (source, target) in enumerate(sources)
        ]
        for copy in fetched:
            copy.start()
        copies = copy_rows(4 * (atoms - UPPER), 4 * UPPER)
        for copy in fetched:
            copy.wait()
        last = last_ref[...]
        target = jnp.where(last >= 0, last - (start_ref[0] + atoms), -1).astype(jnp.float32)
        at = 4 * UPPER + 16 * -(-48 // count)
        for half in range(2):
            part = target[8 * half : 8 * half + 8]
            far_ref[0, at + 8 * half : at + 8 * half + 8, :] = side_by_side(part, part, 1)
        for x, ref in enumerate((ham_ref, ovl_ref)):
            for k in range(3):
                for g in range(2):
                    for b in range(4):
                        plane = x * 24 + k * 8 + g * 4 + b
                        for half in range(2):
                            parts = [
                                ref[k * 16 + (2 * g + parity) * 4 + b, 8 * half : 8 * half + 8, :]
                                for parity in range(2)
                            ]
                            at = 4 * UPPER + 16 * (plane // count) + 8 * half
                            far_ref[plane % count, at : at + 8, :] = side_by_side(parts[0], parts[1], 1)
        for copy in copies:
            copy.wait()


def core_pack_kernel(start_ref, coeffs_ref, far_ref, first_ref, second_ref, copy_sem):
    count, rows, unused = first_ref.shape

    @pl.when(jnp.logical_not(is_lower(start_ref, rows)))
    def pack():
        copies = [
            pltpu.make_async_copy(
                coeffs_ref.at[at * rows : (at + 1) * rows, c * LANES : (c + 1) * LANES],
                half_ref.at[c],
                copy_sem.at[at * count + c],
            )
            for at, half_ref in enumerate((first_ref, second_ref))
            for c in range(count)
        ]
        for copy in copies:
            copy.start()
        for copy in copies:
            copy.wait()


def above(
    lower, start_ref, payload_refs, occup_ref, energies_ref, nbr_ref, deriv_ref, slot_ref,
    own_high_ref, own_low_ref, force_ref, sent_ref,
    cut_high_ref, cut_low_ref, gram_ref, index_ref, spread_ref,
):
    atoms = nbr_ref.shape[1]
    occup = occup_ref[...]
    weights = [occup, occup * energies_ref[...]]
    size = BLOCK if lower % BLOCK == 0 else lower
    for c in range(payload_refs[0].shape[0]):
        lanes = slice(c * LANES, (c + 1) * LANES)
        for block in range(lower // size):
            for b in range(4):
                rows = payload_refs[block][c, pl.ds(b, size, stride=4), :]
                for x in range(2):
                    at = ((block * 2 + x) * 4 + b) * size
                    cut_high_ref[at : at + size, lanes], cut_low_ref[at : at + size, lanes] = split(
                        rows * weights[x][:, lanes]
                    )
    for block in range(lower // size):
        rows = slice(block * 8 * size, (block + 1) * 8 * size)
        skip = 256 * block
        gram_ref[rows, skip:] = gram(
            cut_high_ref[rows, :], cut_low_ref[rows, :], own_high_ref[512 + skip :, :], own_low_ref[512 + skip :, :]
        )
    index_ref[...] = nbr_ref[:, LANES:] - (start_ref[0] + atoms)
    even, odd = (
        fold(
            pick_pairs(
                tiles(gram_ref, 256 * h, size),
                (BLOCK, lower)[h] // 8,
                block_index(index_ref, h),
                lambda *key: deriv_ref[2 + h, deriv_at(*key)],
            )
        )
        for h in range(2)
    )
    pair = merge(even, odd)
    mine = slot_sum(pair)
    theirs = spread(lambda r: slot_ref[48 + r], pair, spread_ref, lower)
    for k in range(3):
        force_ref[k : k + 1, LANES:] += -2.0 * mine[k]
        sent_ref[k : k + 1, :lower] = 2.0 * theirs[k]


def core_kernel(
    start_ref, first_ref, second_ref, before_ref, occup_ref, energies_ref, nbr_ref, deriv_ref, slot_ref,
    own_high_ref, own_low_ref, force_ref, sent_ref, *scratch,
):
    atoms = nbr_ref.shape[1]
    force_ref[...] = before_ref[...]
    sent_ref[...] = jnp.zeros_like(sent_ref)

    @pl.when(is_lower(start_ref, atoms))
    def run():
        above(
            atoms // 2, start_ref, (first_ref, second_ref), occup_ref, energies_ref, nbr_ref, deriv_ref, slot_ref,
            own_high_ref, own_low_ref, force_ref, sent_ref, *scratch,
        )


def far_kernel(
    start_ref, payload_ref, before_ref, occup_ref, energies_ref, nbr_ref, deriv_ref, slot_ref,
    own_high_ref, own_low_ref, near_high_ref, near_low_ref, force_ref, sent_ref,
    cut_high_ref, cut_low_ref, gram_ref, index_ref, spread_ref,
):
    atoms = nbr_ref.shape[1]
    count = payload_ref.shape[0]
    lower = atoms // 2 - UPPER
    force_ref[...] = before_ref[...]
    sent_ref[...] = jnp.zeros_like(sent_ref)

    @pl.when(jnp.logical_not(is_lower(start_ref, atoms)))
    def run():
        above(
            lower, start_ref, (payload_ref,), occup_ref, energies_ref, nbr_ref, deriv_ref, slot_ref,
            own_high_ref, own_low_ref, force_ref, sent_ref,
            cut_high_ref, cut_low_ref, gram_ref, index_ref, spread_ref,
        )

    @pl.when(is_lower(start_ref, atoms))
    def below():
        skip = BLOCK - UPPER
        for c in range(count):
            lanes = slice(c * LANES, (c + 1) * LANES)
            for a in range(4):
                rows = payload_ref[c, pl.ds(a, UPPER, stride=4), :]
                at = slice(a * BLOCK + skip, (a + 1) * BLOCK)
                cut_high_ref[at, lanes], cut_low_ref[at, lanes] = split(rows)
                at = slice(a * BLOCK, a * BLOCK + skip)
                cut_high_ref[at, lanes] = jnp.zeros((skip, LANES), jnp.bfloat16)
                cut_low_ref[at, lanes] = jnp.zeros((skip, LANES), jnp.bfloat16)
        gram_ref[:512, :256] = gram(
            near_high_ref[...], near_low_ref[...], cut_high_ref[:256, :], cut_low_ref[:256, :]
        )
        planes = -(-48 // count)
        at = 4 * UPPER + 16 * planes
        target = payload_ref[0, at : at + 16, :].astype(jnp.int32)
        index_ref[...] = jnp.where(target >= lower, target - BLOCK, -1)
        index = [index_ref[8 * half : 8 * half + 8, :] for half in range(2)]

        def deriv(k, x, b, g, half):
            plane = x * 24 + k * 8 + g * 4 + b
            at = 4 * UPPER + 16 * (plane // count) + 8 * half
            return payload_ref[plane % count, at : at + 8, :]

        pair = pick_pairs(tiles(gram_ref, 0, BLOCK), BLOCK // 8, index, deriv)
        theirs = spread(functools.partial(slot_map, index_ref), pair, spread_ref, BLOCK)
        mine = slot_sum(fold(pair))
        for k in range(3):
            force_ref[k : k + 1, BLOCK:LANES] += 2.0 * theirs[k]
            sent_ref[k : k + 1, atoms - BLOCK :] = -2.0 * mine[k][:, BLOCK:]


def in_hbm(value):
    return pltpu.with_memory_space_constraint(value, pltpu.HBM)


def core_down(value):
    return lax.ppermute(value, "sub", [(1, 0)])


def core_up(value):
    return lax.ppermute(value, "sub", [(0, 1)])


def shard_swap(value):
    count = lax.axis_size(SHARD)
    pairs = [pair for at in range(1, count - 1, 2) for pair in ((at, at + 1), (at + 1, at))]
    return lax.ppermute(value, SHARD, pairs)


def local(coeffs, occup, energies, nbr, dham, dovl):
    slots, atoms = nbr.shape
    states = coeffs.shape[1]
    start = (lax.axis_index(SHARD) * atoms).reshape(1).astype(jnp.int32)
    occup = occup.reshape(1, states)
    energies = energies.reshape(1, states)
    count = states // LANES

    vmem = pl.BlockSpec(memory_space=pltpu.VMEM)
    hbm = pl.BlockSpec(memory_space=pltpu.HBM)
    smem = pl.BlockSpec(memory_space=pltpu.SMEM)
    half = jax.ShapeDtypeStruct((512, states), jnp.bfloat16)
    whole = jax.ShapeDtypeStruct((4 * atoms, states), jnp.bfloat16)
    force = jax.ShapeDtypeStruct((8, atoms), jnp.float32)
    prepared = pltpu.VMEM((512, states), jnp.bfloat16)
    coeffs, nbr_hbm, dham_hbm, dovl_hbm = (in_hbm(value) for value in (coeffs, nbr, dham, dovl))
    far_payload = pl.pallas_call(
        far_pack_kernel,
        out_shape=jax.ShapeDtypeStruct((count, payload_rows(atoms, states), LANES), jnp.float32),
        in_specs=[smem] + [hbm] * 4,
        out_specs=vmem,
        scratch_shapes=[
            pltpu.VMEM((48, slots, LANES), jnp.float32),
            pltpu.VMEM((48, slots, LANES), jnp.float32),
            pltpu.VMEM((slots, LANES), jnp.int32),
            pltpu.SemaphoreType.DMA((count,)),
            pltpu.SemaphoreType.DMA((3,)),
        ],
        compiler_params=pltpu.CompilerParams(vmem_limit_bytes=12 * 1024 * 1024),
        name="far_pack",
    )(start, coeffs, nbr_hbm, dham_hbm, dovl_hbm)
    core_half = jax.ShapeDtypeStruct((count, atoms, LANES), jnp.float32)
    core_payload = pl.pallas_call(
        core_pack_kernel,
        out_shape=(core_half, core_half),
        in_specs=[smem, hbm, pl.BlockSpec(memory_space=pl.ANY)],
        out_specs=(vmem, vmem),
        scratch_shapes=[pltpu.SemaphoreType.DMA((2 * count,))],
        compiler_params=pltpu.CompilerParams(vmem_limit_bytes=12 * 1024 * 1024),
        name="core_pack",
    )(start, coeffs, far_payload)
    far_payload = shard_swap(far_payload)
    core_payload = [core_down(half) for half in core_payload]
    own_high, own_low, near_high, near_low, inner, derivs, slot_maps = pl.pallas_call(
        inner_kernel,
        out_shape=(
            whole, whole, half, half, force,
            jax.ShapeDtypeStruct((4, 96, 8, LANES), jnp.float32),
            jax.ShapeDtypeStruct((64, 8, LANES), jnp.int32),
        ),
        in_specs=[smem, hbm] + [vmem] * 5,
        out_specs=(vmem,) * 7,
        scratch_shapes=[prepared] * 6
        + [pltpu.VMEM((512 * n, 256), jnp.float32) for n in (3, 3, 2, 1)]
        + [
            pltpu.VMEM((2, slots, LANES), jnp.int32),
            pltpu.VMEM((3, atoms, LANES), jnp.float32),
            pltpu.VMEM((states // LANES, 4 * atoms, LANES), jnp.float32),
            pltpu.SemaphoreType.DMA((count,)),
        ],
        compiler_params=pltpu.CompilerParams(vmem_limit_bytes=32 * 1024 * 1024),
        cost_estimate=pl.CostEstimate(
            flops=3 * 2 * 9 * 512 * 256 * states, bytes_accessed=16 * 1024 * 1024, transcendentals=0
        ),
        name="inner_pairs",
    )(start, coeffs, occup, energies, nbr, dham, dovl)

    def cross(kernel, rows, flops, name, *operands):
        cut = pltpu.VMEM((8 * rows, states), jnp.bfloat16)
        return pl.pallas_call(
            kernel,
            out_shape=(force, force),
            in_specs=[smem] + [vmem] * len(operands),
            out_specs=(vmem, vmem),
            scratch_shapes=[
                cut,
                cut,
                pltpu.VMEM((8 * rows, 512), jnp.float32),
                pltpu.VMEM((slots, LANES), jnp.int32),
                pltpu.VMEM((3, rows, LANES), jnp.float32),
            ],
            compiler_params=pltpu.CompilerParams(vmem_limit_bytes=20 * 1024 * 1024),
            cost_estimate=pl.CostEstimate(
                flops=flops, bytes_accessed=0, transcendentals=0
            ),
            name=name,
        )(start, *operands)

    shared = (occup, energies, nbr, derivs, slot_maps, own_high, own_low)
    total, core_sent = cross(core_kernel, atoms // 2, 0, "core_pairs", *core_payload, inner, *shared)
    core_back = core_up(core_sent)
    total, far_sent = cross(
        far_kernel, atoms // 2 - UPPER, 3 * 2 * 2 * 512 * 256 * states, "far_pairs", far_payload, total, *shared, near_high, near_low
    )
    total = (total + core_back + shard_swap(far_sent))[:3]
    if lax.axis_size("states") == 2:
        return total + lax.ppermute(total, "states", [(0, 1), (1, 0)])
    return lax.psum(total, "states")


def solution(mesh):
    in_specs = (
        P(("groups", "atoms", "sub"), "states"),
        P(("groups", "states")),
        P(("groups", "states")),
        P(None, ("groups", "atoms", "sub")),
        P(None, None, ("groups", "atoms", "sub")),
        P(None, None, ("groups", "atoms", "sub")),
    )
    out_specs = P(None, ("groups", "atoms", "sub"))
    return jax.shard_map(local, mesh=mesh, in_specs=in_specs, out_specs=out_specs, check_vma=False)
```

```python
import functools

import jax
import jax.numpy as jnp
from jax import lax
from jax.experimental import pallas as pl
from jax.experimental.pallas import tpu as pltpu
from jax.sharding import PartitionSpec as P

LANES = 128
BLOCK = 64
UPPER = 52
SHARD = ("atoms", "sub")


def split(value):
    high = value.astype(jnp.bfloat16)
    return high, (value - high.astype(jnp.float32)).astype(jnp.bfloat16)


def gram(left_high, left_low, right_high, right_low):
    dot = functools.partial(
        lax.dot_general,
        dimension_numbers=(((1,), (1,)), ((), ())),
        preferred_element_type=jnp.float32,
    )
    return (
        dot(left_high, right_high) + dot(left_high, right_low) + dot(left_low, right_high)
    )


def lane_numbers():
    return lax.broadcasted_iota(jnp.int32, (8, LANES), 1)


def swap_halves(value):
    return pltpu.roll(value, BLOCK, 1)


def side_by_side(left, right, odd):
    if odd:
        return jnp.where(lane_numbers() < BLOCK, swap_halves(left), right)
    return jnp.where(lane_numbers() < BLOCK, left, swap_halves(right))


def pick_pairs(tile, steps, index, deriv):
    low = [part & 7 for part in index]
    high = [part >> 3 for part in index]
    pair = [[None, None] for k in range(3)]
    for x in range(2):
        picked = {}
        for r in range(steps):
            hit = [part == r for part in high]
            for b in range(4):
                for g in range(2):
                    rows = tile(r, x, b, g)
                    for half in range(2):
                        got = jnp.take_along_axis(rows, low[half], axis=0)
                        before = picked.get((b, g, half), 0.0)
                        picked[b, g, half] = jnp.where(hit[half], got, before)
        for (b, g, half), value in picked.items():
            for k in range(3):
                term = value * deriv(k, x, b, g, half)
                if pair[k][half] is None:
                    pair[k][half] = term
                else:
                    pair[k][half] = pair[k][half] - term if x else pair[k][half] + term
    return pair


def tiles(gram_ref, column, size):
    def tile(r, x, b, g):
        block, part = divmod(r, size // 8)
        row = ((block * 2 + x) * 4 + b) * size + part * 8
        return gram_ref[row : row + 8, column + g * LANES : column + (g + 1) * LANES]

    return tile


def fold(pair):
    return [[value + swap_halves(value) for value in parts] for parts in pair]


def merge(even, odd):
    left = lane_numbers() < BLOCK
    return [[jnp.where(left, even[k][half], odd[k][half]) for half in range(2)] for k in range(3)]


def slot_sum(pair):
    return [jnp.sum(pair[k][0] + pair[k][1], axis=0, keepdims=True) for k in range(3)]


def slot_map(index_ref, base, first=0):
    target = lax.broadcasted_iota(jnp.int32, (8, LANES), 0) + base
    slot = jnp.full((8, LANES), 16, jnp.int32)
    for n in range(16):
        hit = jnp.broadcast_to(index_ref[n : n + 1, :], (8, LANES)) == target
        slot = jnp.where(hit, n, slot)
    return jnp.where(target < first, 16, slot) if first else slot


def spread(slot, pair, spread_ref, rows):
    for r in range(rows // 8):
        slots = slot(r)
        low = slots & 7
        for k in range(3):
            first = jnp.take_along_axis(pair[k][0], low, axis=0)
            second = jnp.take_along_axis(pair[k][1], low, axis=0)
            value = jnp.where(slots < 8, first, jnp.where(slots < 16, second, 0.0))
            spread_ref[k, 8 * r : 8 * r + 8, :] = value
    ones = jnp.ones((8, LANES), jnp.float32)
    out = []
    for k in range(3):
        total = lax.dot_general(
            ones,
            spread_ref[k, :rows, :],
            (((1,), (1,)), ((), ())),
            precision=lax.Precision.HIGHEST,
            preferred_element_type=jnp.float32,
        )
        out.append(total[:1])
    return out


def deriv_at(k, x, b, g, half):
    return (((k * 2 + x) * 4 + b) * 2 + g) * 2 + half


def block_index(index_ref, odd):
    return [
        side_by_side(index_ref[8 * half : 8 * half + 8, :], index_ref[8 * half : 8 * half + 8, :], odd)
        for half in range(2)
    ]


def inner_kernel(
    start_ref, coeffs_ref, occup_ref, energies_ref, nbr_ref, dham_ref, dovl_ref,
    own_high_ref, own_low_ref, near1_high_ref, near1_low_ref, force_ref, deriv_ref, slot_ref,
    near0_high_ref, near0_low_ref, near2_high_ref, near2_low_ref, near3_high_ref, near3_low_ref,
    gram0_ref, gram1_ref, gram2_ref, gram3_ref, index_ref, spread_ref, columns_ref, copy_sem,
):
    states = coeffs_ref.shape[1]
    count = states // LANES
    near = [
        (near0_high_ref, near0_low_ref),
        (near1_high_ref, near1_low_ref),
        (near2_high_ref, near2_low_ref),
        (near3_high_ref, near3_low_ref),
    ]
    grams = [gram0_ref, gram1_ref, gram2_ref, gram3_ref]
    copies = [
        pltpu.make_async_copy(
            coeffs_ref.at[:, c * LANES : (c + 1) * LANES], columns_ref.at[c], copy_sem.at[c]
        )
        for c in range(count)
    ]
    for copy in copies:
        copy.start()
    occup = occup_ref[...]
    weights = [occup, occup * energies_ref[...]]

    for tile in range(2):
        index_ref[tile] = nbr_ref[:, tile * LANES : (tile + 1) * LANES] - (start_ref[0] + tile * LANES)
    for h in range(4):
        lanes = slice(h // 2 * LANES, (h // 2 + 1) * LANES)
        for x, ref in enumerate((dham_ref, dovl_ref)):
            for k in range(3):
                for b in range(4):
                    for g in range(2):
                        for half in range(2):
                            parts = [
                                ref[k * 16 + (2 * g + parity) * 4 + b, 8 * half : 8 * half + 8, lanes]
                                for parity in range(2)
                            ]
                            at = deriv_at(k, x, b, g, half)
                            deriv_ref[h, at] = side_by_side(parts[0], parts[1], h % 2)
    for r in range(32):
        slot_ref[r] = slot_map(index_ref.at[0], 8 * r)
    lower = LANES - UPPER
    for r in range(16 + lower // 8):
        slot_ref[32 + r] = slot_map(index_ref.at[1], 8 * r)
    slot_ref[48 + lower // 8] = slot_map(index_ref.at[1], LANES + lower - 8, LANES + lower // 8 * 8)
    for c, copy in enumerate(copies):
        copy.wait()
        lanes = slice(c * LANES, (c + 1) * LANES)
        for j in range(4):
            for a in range(4):
                rows = columns_ref[c, pl.ds(j * 256 + a, BLOCK, stride=4), :]
                own = slice(j * 256 + a * BLOCK, j * 256 + (a + 1) * BLOCK)
                own_high_ref[own, lanes], own_low_ref[own, lanes] = split(rows)
                for x in range(2):
                    at = slice(x * 256 + a * BLOCK, x * 256 + (a + 1) * BLOCK)
                    near[j][0][at, lanes], near[j][1][at, lanes] = split(rows * weights[x][:, lanes])

    def multiply(h):
        own = slice(h * 256, h * 256 + 256)
        for j in range(h, min(h + 3, 4)):
            grams[h][(j - h) * 512 : (j - h) * 512 + 512, :] = gram(
                near[j][0][...], near[j][1][...], own_high_ref[own, :], own_low_ref[own, :]
            )

    def pick(h):
        index = [part - BLOCK * (h % 2) for part in block_index(index_ref.at[h // 2], h % 2)]
        steps = (min(h + 3, 4) - h) * BLOCK // 8
        return fold(
            pick_pairs(tiles(grams[h], 0, BLOCK), steps, index, lambda *key: deriv_ref[h, deriv_at(*key)])
        )

    def finish(tile, even, odd):
        pair = merge(even, odd)
        mine = slot_sum(pair)
        theirs = spread(lambda r: slot_ref[32 * tile + r], pair, spread_ref, 256 - tile * LANES)
        return mine, theirs

    for h in (3, 2, 1, 0):
        multiply(h)
    pair3 = pick(3)
    pair2 = pick(2)
    mine1, theirs1 = finish(1, pair2, pair3)
    pair1 = pick(1)
    pair0 = pick(0)
    mine0, theirs0 = finish(0, pair0, pair1)
    force_ref[...] = jnp.zeros_like(force_ref)
    for k in range(3):
        force_ref[k : k + 1, :LANES] = 2.0 * (theirs0[k][:, :LANES] - mine0[k])
        force_ref[k : k + 1, LANES:] = 2.0 * (theirs0[k][:, LANES:] + theirs1[k] - mine1[k])


def payload_rows(atoms, states):
    groups = -(-48 // (states // LANES))
    return max(4 * (atoms // 2 - UPPER), 4 * BLOCK + 16 * (groups - 3))


def plane_row(plane, count):
    group = plane // count
    return 16 * group if group < 3 else 4 * BLOCK + 16 * (group - 3)


def pack_kernel(
    start_ref, coeffs_ref, nbr_ref, dham_ref, dovl_ref, core_ref, far_ref,
    ham_ref, ovl_ref, last_ref, core_sem, far_sem, deriv_sem,
):
    atoms = nbr_ref.shape[1]
    count, rows, unused = core_ref.shape
    lower = 4 * (atoms // 2 - UPPER)
    first = ((start_ref[0] // atoms) & 1) == 0
    fetched = [
        pltpu.make_async_copy(source.at[:, :, atoms - LANES :], target, deriv_sem.at[at])
        for at, (source, target) in enumerate([(dham_ref, ham_ref), (dovl_ref, ovl_ref)])
    ]
    fetched.append(
        pltpu.make_async_copy(nbr_ref.at[:, atoms - LANES :], last_ref, deriv_sem.at[2])
    )

    def fill(up_ref, up_sem, down_ref, down_sem):
        copies = []
        skip = 4 * (BLOCK - UPPER)
        for c in range(count):
            lanes = slice(c * LANES, (c + 1) * LANES)
            up_rows = coeffs_ref.at[4 * (atoms - UPPER) :, lanes]
            copies.append(pltpu.make_async_copy(up_rows, up_ref.at[c, skip : 4 * BLOCK, :], up_sem.at[c]))
            down_rows = coeffs_ref.at[:lower, lanes]
            copies.append(pltpu.make_async_copy(down_rows, down_ref.at[c, :lower, :], down_sem.at[c]))
        for copy in fetched + copies:
            copy.start()
        if rows > lower:
            down_ref[:, lower:, :] = jnp.zeros((count, rows - lower, LANES), jnp.float32)
        for plane in range(48, -(-48 // count) * count):
            up_ref[plane % count, plane_row(plane, count) : plane_row(plane, count) + 16, :] = jnp.zeros(
                (16, LANES), jnp.float32
            )
        for copy in fetched:
            copy.wait()
        last = last_ref[...]
        target = jnp.where(last >= 0, last - (start_ref[0] + atoms), -1).astype(jnp.float32)
        free = BLOCK - UPPER
        pieces = [
            [
                pltpu.roll(target[8 * half : 8 * half + 8], LANES - BLOCK - (piece + 1) * free, 1)
                for half in range(2)
            ]
            for piece in range(-(-UPPER // free))
        ]
        for x, ref in enumerate((ham_ref, ovl_ref)):
            for k in range(3):
                for g in range(2):
                    for b in range(4):
                        plane = x * 24 + k * 8 + g * 4 + b
                        for half in range(2):
                            parts = [
                                ref[k * 16 + (2 * g + parity) * 4 + b, 8 * half : 8 * half + 8, :]
                                for parity in range(2)
                            ]
                            both = side_by_side(parts[0], parts[1], 1)
                            if plane < len(pieces):
                                both = jnp.where(lane_numbers() < free, pieces[plane][half], both)
                            at = plane_row(plane, count) + 8 * half
                            up_ref[plane % count, at : at + 8, :] = both
        for copy in copies:
            copy.wait()

    @pl.when(first)
    def even():
        fill(core_ref, core_sem, far_ref, far_sem)

    @pl.when(jnp.logical_not(first))
    def odd():
        fill(far_ref, far_sem, core_ref, core_sem)


def cross_kernel(
    parity,
    start_ref, payload_ref, before_ref, occup_ref, energies_ref, nbr_ref, deriv_ref, slot_ref,
    own_high_ref, own_low_ref, near_high_ref, near_low_ref,
    force_ref, sent_ref,
    cut_high_ref, cut_low_ref, gram_ref, index_ref, spread_ref,
):
    atoms = nbr_ref.shape[1]
    count = payload_ref.shape[0]
    lower = atoms // 2 - UPPER
    force_ref[...] = before_ref[...]
    sent_ref[...] = jnp.zeros_like(sent_ref)
    first = ((start_ref[0] // atoms) & 1) == parity

    @pl.when(first)
    def above():
        occup = occup_ref[...]
        weights = [occup, occup * energies_ref[...]]
        size = cut_high_ref.shape[0] // 8
        even = lower // 8 * 8
        for c in range(count):
            lanes = slice(c * LANES, (c + 1) * LANES)
            for b in range(4):
                rows = jnp.concatenate(
                    [
                        payload_ref[c, pl.ds(b, even, stride=4), :],
                        payload_ref[c, pl.ds(4 * (lower - 8) + b, 8, stride=4), :],
                    ],
                    0,
                )
                for x in range(2):
                    at = slice((x * 4 + b) * size, (x * 4 + b + 1) * size)
                    cut_high_ref[at, lanes], cut_low_ref[at, lanes] = split(rows * weights[x][:, lanes])
        gram_ref[...] = gram(
            cut_high_ref[...], cut_low_ref[...], own_high_ref[512:, :], own_low_ref[512:, :]
        )
        target = nbr_ref[:, LANES:] - (start_ref[0] + atoms)
        index_ref[...] = jnp.where(target >= even, target + (size - lower), target)
        pairs = [
            pick_pairs(
                tiles(gram_ref, 256 * h, size),
                (BLOCK, size)[h] // 8,
                block_index(index_ref, h),
                lambda *key: deriv_ref[2 + h, deriv_at(*key)],
            )
            for h in range(2)
        ]
        pair = merge(fold(pairs[0]), fold(pairs[1]))
        mine = slot_sum(pair)
        theirs = spread(lambda r: slot_ref[48 + r], pair, spread_ref, size)
        for k in range(3):
            force_ref[k : k + 1, LANES:] += -2.0 * mine[k]
            sent_ref[k : k + 1, :even] = 2.0 * theirs[k][:, :even]
            sent_ref[k : k + 1, lower - 8 : lower] += 2.0 * theirs[k][:, even:]

    @pl.when(jnp.logical_not(first))
    def below():
        for c in range(count):
            lanes = slice(c * LANES, (c + 1) * LANES)
            for a in range(4):
                at = slice(a * BLOCK, (a + 1) * BLOCK)
                cut_high_ref[at, lanes], cut_low_ref[at, lanes] = split(
                    payload_ref[c, pl.ds(a, BLOCK, stride=4), :]
                )
        gram_ref[:512, :256] = gram(
            near_high_ref[...], near_low_ref[...], cut_high_ref[:256, :], cut_low_ref[:256, :]
        )
        free = BLOCK - UPPER
        lane = lane_numbers()
        for half in range(2):
            target = jnp.zeros((8, LANES), jnp.float32)
            for piece in range(-(-UPPER // free)):
                at = plane_row(piece, count) + 8 * half
                first_lane = (piece + 1) * free
                moved = pltpu.roll(payload_ref[piece % count, at : at + 8, :], first_lane, 1)
                target = jnp.where((lane >= first_lane) & (lane < first_lane + free), moved, target)
            target = side_by_side(target, target, 0).astype(jnp.int32)
            index_ref[8 * half : 8 * half + 8, :] = jnp.where(target >= lower, target - BLOCK, -1)
        index = [index_ref[8 * half : 8 * half + 8, :] for half in range(2)]

        def deriv(k, x, b, g, half):
            plane = x * 24 + k * 8 + g * 4 + b
            at = plane_row(plane, count) + 8 * half
            return payload_ref[plane % count, at : at + 8, :]

        pair = pick_pairs(tiles(gram_ref, 0, BLOCK), BLOCK // 8, index, deriv)
        theirs = spread(lambda r: slot_map(index_ref, 8 * r), pair, spread_ref, BLOCK)
        mine = slot_sum(fold(pair))
        for k in range(3):
            force_ref[k : k + 1, BLOCK:LANES] += 2.0 * theirs[k]
            sent_ref[k : k + 1, atoms - BLOCK :] = -2.0 * mine[k][:, BLOCK:]


def in_hbm(value):
    return pltpu.with_memory_space_constraint(value, pltpu.HBM)


def core_swap(value):
    return lax.ppermute(value, "sub", [(0, 1), (1, 0)])


def shard_swap(value):
    count = lax.axis_size(SHARD)
    pairs = [pair for at in range(1, count - 1, 2) for pair in ((at, at + 1), (at + 1, at))]
    return lax.ppermute(value, SHARD, pairs)


def local(coeffs, occup, energies, nbr, dham, dovl):
    slots, atoms = nbr.shape
    states = coeffs.shape[1]
    start = (lax.axis_index(SHARD) * atoms).reshape(1).astype(jnp.int32)
    occup = occup.reshape(1, states)
    energies = energies.reshape(1, states)
    count = states // LANES

    vmem = pl.BlockSpec(memory_space=pltpu.VMEM)
    hbm = pl.BlockSpec(memory_space=pltpu.HBM)
    smem = pl.BlockSpec(memory_space=pltpu.SMEM)
    half = jax.ShapeDtypeStruct((512, states), jnp.bfloat16)
    whole = jax.ShapeDtypeStruct((4 * atoms, states), jnp.bfloat16)
    force = jax.ShapeDtypeStruct((8, atoms), jnp.float32)
    prepared = pltpu.VMEM((512, states), jnp.bfloat16)
    padded = -(-(atoms // 2 - UPPER) // 16) * 16
    payload = jax.ShapeDtypeStruct((count, payload_rows(atoms, states), LANES), jnp.float32)
    core_payload, far_payload = pl.pallas_call(
        pack_kernel,
        out_shape=(payload, payload),
        in_specs=[smem] + [hbm] * 4,
        out_specs=(vmem, vmem),
        scratch_shapes=[
            pltpu.VMEM((48, slots, LANES), jnp.float32),
            pltpu.VMEM((48, slots, LANES), jnp.float32),
            pltpu.VMEM((slots, LANES), jnp.int32),
            pltpu.SemaphoreType.DMA((count,)),
            pltpu.SemaphoreType.DMA((count,)),
            pltpu.SemaphoreType.DMA((3,)),
        ],
        compiler_params=pltpu.CompilerParams(vmem_limit_bytes=12 * 1024 * 1024),
        name="pack",
    )(start, *(in_hbm(value) for value in (coeffs, nbr, dham, dovl)))
    far_payload = shard_swap(far_payload)
    core_payload = core_swap(core_payload)
    own_high, own_low, near_high, near_low, inner, derivs, slot_maps = pl.pallas_call(
        inner_kernel,
        out_shape=(
            whole, whole, half, half, force,
            jax.ShapeDtypeStruct((4, 96, 8, LANES), jnp.float32),
            jax.ShapeDtypeStruct((64 - UPPER // 8, 8, LANES), jnp.int32),
        ),
        in_specs=[smem, hbm] + [vmem] * 5,
        out_specs=(vmem,) * 7,
        scratch_shapes=[prepared] * 6
        + [pltpu.VMEM((512 * n, 256), jnp.float32) for n in (3, 3, 2, 1)]
        + [
            pltpu.VMEM((2, slots, LANES), jnp.int32),
            pltpu.VMEM((3, atoms, LANES), jnp.float32),
            pltpu.VMEM((states // LANES, 4 * atoms, LANES), jnp.float32),
            pltpu.SemaphoreType.DMA((count,)),
        ],
        compiler_params=pltpu.CompilerParams(vmem_limit_bytes=32 * 1024 * 1024),
        cost_estimate=pl.CostEstimate(
            flops=3 * 2 * 9 * 512 * 256 * states, bytes_accessed=16 * 1024 * 1024, transcendentals=0
        ),
        name="inner_pairs",
    )(start, in_hbm(coeffs), occup, energies, nbr, dham, dovl)

    def cross(parity, payload, before, name):
        cut = pltpu.VMEM((8 * padded, states), jnp.bfloat16)
        return pl.pallas_call(
            functools.partial(cross_kernel, parity),
            out_shape=(force, force),
            in_specs=[smem] + [vmem] * 11,
            out_specs=(vmem, vmem),
            scratch_shapes=[
                cut,
                cut,
                pltpu.VMEM((8 * padded, 512), jnp.float32),
                pltpu.VMEM((slots, LANES), jnp.int32),
                pltpu.VMEM((3, padded, LANES), jnp.float32),
            ],
            compiler_params=pltpu.CompilerParams(vmem_limit_bytes=20 * 1024 * 1024),
            cost_estimate=pl.CostEstimate(
                flops=3 * 2 * 2 * 512 * 256 * states, bytes_accessed=6 * 1024 * 1024, transcendentals=0
            ),
            name=name,
        )(start, payload, before, occup, energies, nbr, derivs, slot_maps, own_high, own_low, near_high, near_low)

    total, core_sent = cross(0, core_payload, inner, "core_pairs")
    core_back = core_swap(core_sent)
    total, far_sent = cross(1, far_payload, total, "far_pairs")
    total = (total + core_back + shard_swap(far_sent))[:3]
    if lax.axis_size("states") == 2:
        return total + lax.ppermute(total, "states", [(0, 1), (1, 0)])
    return lax.psum(total, "states")


def solution(mesh):
    in_specs = (
        P(("groups", "atoms", "sub"), "states"),
        P(("groups", "states")),
        P(("groups", "states")),
        P(None, ("groups", "atoms", "sub")),
        P(None, None, ("groups", "atoms", "sub")),
        P(None, None, ("groups", "atoms", "sub")),
    )
    out_specs = P(None, ("groups", "atoms", "sub"))
    return jax.shard_map(local, mesh=mesh, in_specs=in_specs, out_specs=out_specs, check_vma=False)
```

```python
import functools

import jax
import jax.numpy as jnp
from jax import lax
from jax.experimental import pallas as pl
from jax.experimental.pallas import tpu as pltpu
from jax.sharding import PartitionSpec as P

LANES = 128
BLOCK = 64
UPPER = 52
SHARD = ("atoms", "sub")


def split(value):
    high = value.astype(jnp.bfloat16)
    return high, (value - high.astype(jnp.float32)).astype(jnp.bfloat16)


def gram(left_high, left_low, right_high, right_low):
    dot = functools.partial(
        lax.dot_general,
        dimension_numbers=(((1,), (1,)), ((), ())),
        preferred_element_type=jnp.float32,
    )
    return (
        dot(left_high, right_high) + dot(left_high, right_low) + dot(left_low, right_high)
    )


def lane_numbers():
    return lax.broadcasted_iota(jnp.int32, (8, LANES), 1)


def swap_halves(value):
    return pltpu.roll(value, BLOCK, 1)


def side_by_side(left, right, odd):
    if odd:
        return jnp.where(lane_numbers() < BLOCK, swap_halves(left), right)
    return jnp.where(lane_numbers() < BLOCK, left, swap_halves(right))


def pick_pairs(tile, steps, index, deriv):
    low = [part & 7 for part in index]
    high = [part >> 3 for part in index]
    pair = [[None, None] for k in range(3)]
    for x in range(2):
        picked = {}
        for r in range(steps):
            hit = [part == r for part in high]
            for b in range(4):
                for g in range(2):
                    rows = tile(r, x, b, g)
                    for half in range(2):
                        got = jnp.take_along_axis(rows, low[half], axis=0)
                        before = picked.get((b, g, half), 0.0)
                        picked[b, g, half] = jnp.where(hit[half], got, before)
        for (b, g, half), value in picked.items():
            for k in range(3):
                term = value * deriv(k, x, b, g, half)
                if pair[k][half] is None:
                    pair[k][half] = term
                else:
                    pair[k][half] = pair[k][half] - term if x else pair[k][half] + term
    return pair


def tiles(gram_ref, column, size):
    def tile(r, x, b, g):
        block, part = divmod(r, size // 8)
        row = ((block * 2 + x) * 4 + b) * size + part * 8
        return gram_ref[row : row + 8, column + g * LANES : column + (g + 1) * LANES]

    return tile


def fold(pair):
    return [[value + swap_halves(value) for value in parts] for parts in pair]


def merge(even, odd):
    left = lane_numbers() < BLOCK
    return [[jnp.where(left, even[k][half], odd[k][half]) for half in range(2)] for k in range(3)]


def slot_sum(pair):
    return [jnp.sum(pair[k][0] + pair[k][1], axis=0, keepdims=True) for k in range(3)]


def slot_map(index_ref, base, first=0):
    target = lax.broadcasted_iota(jnp.int32, (8, LANES), 0) + base
    slot = jnp.full((8, LANES), 16, jnp.int32)
    for n in range(16):
        hit = jnp.broadcast_to(index_ref[n : n + 1, :], (8, LANES)) == target
        slot = jnp.where(hit, n, slot)
    return jnp.where(target < first, 16, slot) if first else slot


def spread(slot, pair, spread_ref, rows):
    for r in range(rows // 8):
        slots = slot(r)
        low = slots & 7
        for k in range(3):
            first = jnp.take_along_axis(pair[k][0], low, axis=0)
            second = jnp.take_along_axis(pair[k][1], low, axis=0)
            value = jnp.where(slots < 8, first, jnp.where(slots < 16, second, 0.0))
            spread_ref[k, 8 * r : 8 * r + 8, :] = value
    ones = jnp.ones((8, LANES), jnp.float32)
    out = []
    for k in range(3):
        total = lax.dot_general(
            ones,
            spread_ref[k, :rows, :],
            (((1,), (1,)), ((), ())),
            precision=lax.Precision.HIGHEST,
            preferred_element_type=jnp.float32,
        )
        out.append(total[:1])
    return out


def deriv_at(k, x, b, g, half):
    return (((k * 2 + x) * 4 + b) * 2 + g) * 2 + half


def block_index(index_ref, odd):
    return [
        side_by_side(index_ref[8 * half : 8 * half + 8, :], index_ref[8 * half : 8 * half + 8, :], odd)
        for half in range(2)
    ]


def inner_kernel(
    start_ref, coeffs_ref, occup_ref, energies_ref, nbr_ref, dham_ref, dovl_ref,
    own_high_ref, own_low_ref, near1_high_ref, near1_low_ref, near3_high_ref, near3_low_ref,
    force_ref, deriv_ref, slot_ref,
    near0_high_ref, near0_low_ref, near2_high_ref, near2_low_ref,
    gram0_ref, gram1_ref, gram2_ref, index_ref, spread_ref, columns_ref, copy_sem,
):
    states = coeffs_ref.shape[1]
    count = states // LANES
    near = [
        (near0_high_ref, near0_low_ref),
        (near1_high_ref, near1_low_ref),
        (near2_high_ref, near2_low_ref),
        (near3_high_ref, near3_low_ref),
    ]
    grams = [gram0_ref, gram1_ref, gram2_ref]
    copies = [
        pltpu.make_async_copy(
            coeffs_ref.at[:, c * LANES : (c + 1) * LANES], columns_ref.at[c], copy_sem.at[c]
        )
        for c in range(count)
    ]
    for copy in copies:
        copy.start()
    occup = occup_ref[...]
    weights = [occup, occup * energies_ref[...]]

    for tile in range(2):
        index_ref[tile] = nbr_ref[:, tile * LANES : (tile + 1) * LANES] - (start_ref[0] + tile * LANES)
    for h in range(4):
        lanes = slice(h // 2 * LANES, (h // 2 + 1) * LANES)
        for x, ref in enumerate((dham_ref, dovl_ref)):
            for k in range(3):
                for b in range(4):
                    for g in range(2):
                        for half in range(2):
                            parts = [
                                ref[k * 16 + (2 * g + parity) * 4 + b, 8 * half : 8 * half + 8, lanes]
                                for parity in range(2)
                            ]
                            at = deriv_at(k, x, b, g, half)
                            deriv_ref[h, at] = side_by_side(parts[0], parts[1], h % 2)
    for r in range(32):
        slot_ref[r] = slot_map(index_ref.at[0], 8 * r)
    lower = LANES - UPPER
    for r in range(16 + lower // 8):
        slot_ref[32 + r] = slot_map(index_ref.at[1], 8 * r)
    slot_ref[48 + lower // 8] = slot_map(index_ref.at[1], LANES + lower - 8, LANES + lower // 8 * 8)
    for c, copy in enumerate(copies):
        copy.wait()
        lanes = slice(c * LANES, (c + 1) * LANES)
        for j in range(4):
            for a in range(4):
                rows = columns_ref[c, pl.ds(j * 256 + a, BLOCK, stride=4), :]
                own = slice(j * 256 + a * BLOCK, j * 256 + (a + 1) * BLOCK)
                own_high_ref[own, lanes], own_low_ref[own, lanes] = split(rows)
                for x in range(2):
                    at = slice(x * 256 + a * BLOCK, x * 256 + (a + 1) * BLOCK)
                    near[j][0][at, lanes], near[j][1][at, lanes] = split(rows * weights[x][:, lanes])

    def multiply(h):
        own = slice(h * 256, h * 256 + 256)
        for j in range(h, min(h + 3, 4)):
            grams[h][(j - h) * 512 : (j - h) * 512 + 512, :] = gram(
                near[j][0][...], near[j][1][...], own_high_ref[own, :], own_low_ref[own, :]
            )

    def pick(h):
        index = [part - BLOCK * (h % 2) for part in block_index(index_ref.at[h // 2], h % 2)]
        steps = (min(h + 3, 4) - h) * BLOCK // 8
        return fold(
            pick_pairs(tiles(grams[h], 0, BLOCK), steps, index, lambda *key: deriv_ref[h, deriv_at(*key)])
        )

    def finish(tile, even, odd):
        pair = merge(even, odd)
        mine = slot_sum(pair)
        theirs = spread(lambda r: slot_ref[32 * tile + r], pair, spread_ref, 256 - tile * LANES)
        return mine, theirs

    for h in (2, 1, 0):
        multiply(h)
    nothing = [[jnp.zeros((8, LANES), jnp.float32)] * 2] * 3
    mine1, theirs1 = finish(1, pick(2), nothing)
    pair1 = pick(1)
    pair0 = pick(0)
    mine0, theirs0 = finish(0, pair0, pair1)
    force_ref[...] = jnp.zeros_like(force_ref)
    for k in range(3):
        force_ref[k : k + 1, :LANES] = 2.0 * (theirs0[k][:, :LANES] - mine0[k])
        force_ref[k : k + 1, LANES:] = 2.0 * (theirs0[k][:, LANES:] + theirs1[k] - mine1[k])


def payload_rows(atoms, states):
    groups = -(-48 // (states // LANES))
    return max(4 * (atoms // 2 - UPPER), 4 * BLOCK + 16 * (groups - 3))


def plane_row(plane, count):
    group = plane // count
    return 16 * group if group < 3 else 4 * BLOCK + 16 * (group - 3)


def pack_kernel(
    start_ref, coeffs_ref, nbr_ref, dham_ref, dovl_ref, core_ref, far_ref,
    ham_ref, ovl_ref, last_ref, core_sem, far_sem, deriv_sem,
):
    atoms = nbr_ref.shape[1]
    count, rows, unused = core_ref.shape
    lower = 4 * (atoms // 2 - UPPER)
    first = ((start_ref[0] // atoms) & 1) == 0
    fetched = [
        pltpu.make_async_copy(source.at[:, :, atoms - LANES :], target, deriv_sem.at[at])
        for at, (source, target) in enumerate([(dham_ref, ham_ref), (dovl_ref, ovl_ref)])
    ]
    fetched.append(
        pltpu.make_async_copy(nbr_ref.at[:, atoms - LANES :], last_ref, deriv_sem.at[2])
    )

    def fill(up_ref, up_sem, down_ref, down_sem):
        copies = []
        skip = 4 * (BLOCK - UPPER)
        for c in range(count):
            lanes = slice(c * LANES, (c + 1) * LANES)
            up_rows = coeffs_ref.at[4 * (atoms - UPPER) :, lanes]
            copies.append(pltpu.make_async_copy(up_rows, up_ref.at[c, skip : 4 * BLOCK, :], up_sem.at[c]))
            down_rows = coeffs_ref.at[:lower, lanes]
            copies.append(pltpu.make_async_copy(down_rows, down_ref.at[c, :lower, :], down_sem.at[c]))
        for copy in fetched + copies:
            copy.start()
        if rows > lower:
            down_ref[:, lower:, :] = jnp.zeros((count, rows - lower, LANES), jnp.float32)
        for plane in range(48, -(-48 // count) * count):
            up_ref[plane % count, plane_row(plane, count) : plane_row(plane, count) + 16, :] = jnp.zeros(
                (16, LANES), jnp.float32
            )
        for copy in fetched:
            copy.wait()
        last = last_ref[...]
        target = jnp.where(last >= 0, last - (start_ref[0] + atoms), -1).astype(jnp.float32)
        free = BLOCK - UPPER
        pieces = [
            [
                pltpu.roll(target[8 * half : 8 * half + 8], LANES - BLOCK - (piece + 1) * free, 1)
                for half in range(2)
            ]
            for piece in range(-(-UPPER // free))
        ]
        for x, ref in enumerate((ham_ref, ovl_ref)):
            for k in range(3):
                for g in range(2):
                    for b in range(4):
                        plane = x * 24 + k * 8 + g * 4 + b
                        for half in range(2):
                            parts = [
                                ref[k * 16 + (2 * g + parity) * 4 + b, 8 * half : 8 * half + 8, :]
                                for parity in range(2)
                            ]
                            both = side_by_side(parts[0], parts[1], 1)
                            if plane < len(pieces):
                                both = jnp.where(lane_numbers() < free, pieces[plane][half], both)
                            at = plane_row(plane, count) + 8 * half
                            up_ref[plane % count, at : at + 8, :] = both
        for copy in copies:
            copy.wait()

    @pl.when(first)
    def even():
        fill(core_ref, core_sem, far_ref, far_sem)

    @pl.when(jnp.logical_not(first))
    def odd():
        fill(far_ref, far_sem, core_ref, core_sem)


def cross_kernel(
    parity,
    start_ref, payload_ref, before_ref, occup_ref, energies_ref, nbr_ref, deriv_ref, slot_ref,
    own_high_ref, own_low_ref, near_high_ref, near_low_ref,
    force_ref, sent_ref,
    cut_high_ref, cut_low_ref, gram_ref, index_ref, spread_ref,
):
    atoms = nbr_ref.shape[1]
    count = payload_ref.shape[0]
    lower = atoms // 2 - UPPER
    force_ref[...] = before_ref[...]
    sent_ref[...] = jnp.zeros_like(sent_ref)
    first = ((start_ref[0] // atoms) & 1) == parity

    @pl.when(first)
    def above():
        occup = occup_ref[...]
        weights = [occup, occup * energies_ref[...]]
        size = cut_high_ref.shape[0] // 8
        even = lower // 8 * 8
        for c in range(count):
            lanes = slice(c * LANES, (c + 1) * LANES)
            for b in range(4):
                rows = jnp.concatenate(
                    [
                        payload_ref[c, pl.ds(b, even, stride=4), :],
                        payload_ref[c, pl.ds(4 * (lower - 8) + b, 8, stride=4), :],
                    ],
                    0,
                )
                for x in range(2):
                    at = slice((x * 4 + b) * size, (x * 4 + b + 1) * size)
                    cut_high_ref[at, lanes], cut_low_ref[at, lanes] = split(rows * weights[x][:, lanes])
        gram_ref[...] = gram(
            cut_high_ref[...], cut_low_ref[...], own_high_ref[512:, :], own_low_ref[512:, :]
        )
        target = nbr_ref[:, LANES:] - (start_ref[0] + atoms)
        index_ref[...] = jnp.where(target >= even, target + (size - lower), target)
        pairs = [
            pick_pairs(
                tiles(gram_ref, 256 * h, size),
                (BLOCK, size)[h] // 8,
                block_index(index_ref, h),
                lambda *key: deriv_ref[2 + h, deriv_at(*key)],
            )
            for h in range(2)
        ]
        pair = merge(fold(pairs[0]), fold(pairs[1]))
        mine = slot_sum(pair)
        theirs = spread(lambda r: slot_ref[48 + r], pair, spread_ref, size)
        for k in range(3):
            force_ref[k : k + 1, LANES:] += -2.0 * mine[k]
            sent_ref[k : k + 1, :even] = 2.0 * theirs[k][:, :even]
            sent_ref[k : k + 1, lower - 8 : lower] += 2.0 * theirs[k][:, even:]

    @pl.when(jnp.logical_not(first))
    def below():
        for c in range(count):
            lanes = slice(c * LANES, (c + 1) * LANES)
            for a in range(4):
                at = slice(a * BLOCK, (a + 1) * BLOCK)
                cut_high_ref[at, lanes], cut_low_ref[at, lanes] = split(
                    payload_ref[c, pl.ds(a, BLOCK, stride=4), :]
                )
        gram_ref[:512, :256] = gram(
            near_high_ref[...], near_low_ref[...], cut_high_ref[:256, :], cut_low_ref[:256, :]
        )
        free = BLOCK - UPPER
        lane = lane_numbers()
        for half in range(2):
            target = jnp.zeros((8, LANES), jnp.float32)
            for piece in range(-(-UPPER // free)):
                at = plane_row(piece, count) + 8 * half
                first_lane = (piece + 1) * free
                moved = pltpu.roll(payload_ref[piece % count, at : at + 8, :], first_lane, 1)
                target = jnp.where((lane >= first_lane) & (lane < first_lane + free), moved, target)
            target = side_by_side(target, target, 0).astype(jnp.int32)
            index_ref[8 * half : 8 * half + 8, :] = jnp.where(target >= lower, target - BLOCK, -1)
        index = [index_ref[8 * half : 8 * half + 8, :] for half in range(2)]

        def deriv(k, x, b, g, half):
            plane = x * 24 + k * 8 + g * 4 + b
            at = plane_row(plane, count) + 8 * half
            return payload_ref[plane % count, at : at + 8, :]

        pair = pick_pairs(tiles(gram_ref, 0, BLOCK), BLOCK // 8, index, deriv)
        theirs = spread(lambda r: slot_map(index_ref, 8 * r), pair, spread_ref, BLOCK)
        mine = slot_sum(fold(pair))
        for k in range(3):
            force_ref[k : k + 1, BLOCK:LANES] += 2.0 * theirs[k]
            sent_ref[k : k + 1, atoms - BLOCK :] = -2.0 * mine[k][:, BLOCK:]


def last_kernel(
    start_ref, before_ref, nbr_ref, deriv_ref, slot_ref, own_high_ref, own_low_ref, near_high_ref, near_low_ref,
    force_ref, gram_ref, index_ref, spread_ref,
):
    gram_ref[...] = gram(
        near_high_ref[...], near_low_ref[...], own_high_ref[768:, :], own_low_ref[768:, :]
    )
    index_ref[...] = nbr_ref[:, LANES:] - (start_ref[0] + LANES)
    index = [part - BLOCK for part in block_index(index_ref, 1)]
    pair = fold(
        pick_pairs(tiles(gram_ref, 0, BLOCK), BLOCK // 8, index, lambda *key: deriv_ref[3, deriv_at(*key)])
    )
    nothing = [[jnp.zeros((8, LANES), jnp.float32)] * 2] * 3
    pair = merge(nothing, pair)
    mine = slot_sum(pair)
    theirs = spread(lambda r: slot_ref[40 + r], pair, spread_ref, BLOCK)
    force_ref[...] = before_ref[...]
    for k in range(3):
        force_ref[k : k + 1, LANES:] += -2.0 * mine[k]
        force_ref[k : k + 1, LANES + BLOCK :] += 2.0 * theirs[k]


def in_hbm(value):
    return pltpu.with_memory_space_constraint(value, pltpu.HBM)


def core_swap(value):
    return lax.ppermute(value, "sub", [(0, 1), (1, 0)])


def shard_swap(value):
    count = lax.axis_size(SHARD)
    pairs = [pair for at in range(1, count - 1, 2) for pair in ((at, at + 1), (at + 1, at))]
    return lax.ppermute(value, SHARD, pairs)


def local(coeffs, occup, energies, nbr, dham, dovl):
    slots, atoms = nbr.shape
    states = coeffs.shape[1]
    start = (lax.axis_index(SHARD) * atoms).reshape(1).astype(jnp.int32)
    occup = occup.reshape(1, states)
    energies = energies.reshape(1, states)
    count = states // LANES

    vmem = pl.BlockSpec(memory_space=pltpu.VMEM)
    hbm = pl.BlockSpec(memory_space=pltpu.HBM)
    smem = pl.BlockSpec(memory_space=pltpu.SMEM)
    half = jax.ShapeDtypeStruct((512, states), jnp.bfloat16)
    whole = jax.ShapeDtypeStruct((4 * atoms, states), jnp.bfloat16)
    force = jax.ShapeDtypeStruct((8, atoms), jnp.float32)
    prepared = pltpu.VMEM((512, states), jnp.bfloat16)
    padded = -(-(atoms // 2 - UPPER) // 16) * 16
    payload = jax.ShapeDtypeStruct((count, payload_rows(atoms, states), LANES), jnp.float32)
    core_payload, far_payload = pl.pallas_call(
        pack_kernel,
        out_shape=(payload, payload),
        in_specs=[smem] + [hbm] * 4,
        out_specs=(vmem, vmem),
        scratch_shapes=[
            pltpu.VMEM((48, slots, LANES), jnp.float32),
            pltpu.VMEM((48, slots, LANES), jnp.float32),
            pltpu.VMEM((slots, LANES), jnp.int32),
            pltpu.SemaphoreType.DMA((count,)),
            pltpu.SemaphoreType.DMA((count,)),
            pltpu.SemaphoreType.DMA((3,)),
        ],
        compiler_params=pltpu.CompilerParams(vmem_limit_bytes=12 * 1024 * 1024),
        name="pack",
    )(start, *(in_hbm(value) for value in (coeffs, nbr, dham, dovl)))
    far_payload = shard_swap(far_payload)
    core_payload = core_swap(core_payload)
    own_high, own_low, near_high, near_low, last_high, last_low, inner, derivs, slot_maps = pl.pallas_call(
        inner_kernel,
        out_shape=(
            whole, whole, half, half, half, half, force,
            jax.ShapeDtypeStruct((4, 96, 8, LANES), jnp.float32),
            jax.ShapeDtypeStruct((64 - UPPER // 8, 8, LANES), jnp.int32),
        ),
        in_specs=[smem, hbm] + [vmem] * 5,
        out_specs=(vmem,) * 9,
        scratch_shapes=[prepared] * 4
        + [pltpu.VMEM((512 * n, 256), jnp.float32) for n in (3, 3, 2)]
        + [
            pltpu.VMEM((2, slots, LANES), jnp.int32),
            pltpu.VMEM((3, atoms, LANES), jnp.float32),
            pltpu.VMEM((states // LANES, 4 * atoms, LANES), jnp.float32),
            pltpu.SemaphoreType.DMA((count,)),
        ],
        compiler_params=pltpu.CompilerParams(vmem_limit_bytes=32 * 1024 * 1024),
        cost_estimate=pl.CostEstimate(
            flops=3 * 2 * 8 * 512 * 256 * states, bytes_accessed=16 * 1024 * 1024, transcendentals=0
        ),
        name="inner_pairs",
    )(start, in_hbm(coeffs), occup, energies, nbr, dham, dovl)

    def cross(parity, payload, before, name):
        cut = pltpu.VMEM((8 * padded, states), jnp.bfloat16)
        return pl.pallas_call(
            functools.partial(cross_kernel, parity),
            out_shape=(force, force),
            in_specs=[smem] + [vmem] * 11,
            out_specs=(vmem, vmem),
            scratch_shapes=[
                cut,
                cut,
                pltpu.VMEM((8 * padded, 512), jnp.float32),
                pltpu.VMEM((slots, LANES), jnp.int32),
                pltpu.VMEM((3, padded, LANES), jnp.float32),
            ],
            compiler_params=pltpu.CompilerParams(vmem_limit_bytes=20 * 1024 * 1024),
            cost_estimate=pl.CostEstimate(
                flops=3 * 2 * 2 * 512 * 256 * states, bytes_accessed=6 * 1024 * 1024, transcendentals=0
            ),
            name=name,
        )(start, payload, before, occup, energies, nbr, derivs, slot_maps, own_high, own_low, near_high, near_low)

    total, core_sent = cross(0, core_payload, inner, "core_pairs")
    core_back = core_swap(core_sent)
    total, far_sent = cross(1, far_payload, total, "far_pairs")
    far_back = shard_swap(far_sent)
    total = pl.pallas_call(
        last_kernel,
        out_shape=force,
        in_specs=[smem] + [vmem] * 8,
        out_specs=vmem,
        scratch_shapes=[
            pltpu.VMEM((512, 256), jnp.float32),
            pltpu.VMEM((slots, LANES), jnp.int32),
            pltpu.VMEM((3, BLOCK, LANES), jnp.float32),
        ],
        compiler_params=pltpu.CompilerParams(vmem_limit_bytes=12 * 1024 * 1024),
        cost_estimate=pl.CostEstimate(
            flops=3 * 2 * 512 * 256 * states, bytes_accessed=0, transcendentals=0
        ),
        name="last_pairs",
    )(start, total, nbr, derivs, slot_maps, own_high, own_low, last_high, last_low)
    total = (total + core_back + far_back)[:3]
    if lax.axis_size("states") == 2:
        return total + lax.ppermute(total, "states", [(0, 1), (1, 0)])
    return lax.psum(total, "states")


def solution(mesh):
    in_specs = (
        P(("groups", "atoms", "sub"), "states"),
        P(("groups", "states")),
        P(("groups", "states")),
        P(None, ("groups", "atoms", "sub")),
        P(None, None, ("groups", "atoms", "sub")),
        P(None, None, ("groups", "atoms", "sub")),
    )
    out_specs = P(None, ("groups", "atoms", "sub"))
    return jax.shard_map(local, mesh=mesh, in_specs=in_specs, out_specs=out_specs, check_vma=False)
```

```python
import functools

import jax
import jax.numpy as jnp
from jax import lax
from jax.experimental import pallas as pl
from jax.experimental.pallas import tpu as pltpu
from jax.sharding import PartitionSpec as P

LANES = 128
BLOCK = 64
UPPER = 52
SHARD = ("atoms", "sub")


def split(value):
    high = value.astype(jnp.bfloat16)
    return high, (value - high.astype(jnp.float32)).astype(jnp.bfloat16)


def gram(left_high, left_low, right_high, right_low):
    dot = functools.partial(
        lax.dot_general,
        dimension_numbers=(((1,), (1,)), ((), ())),
        preferred_element_type=jnp.float32,
    )
    return (
        dot(left_high, right_high) + dot(left_high, right_low) + dot(left_low, right_high)
    )


def lane_numbers():
    return lax.broadcasted_iota(jnp.int32, (8, LANES), 1)


def swap_halves(value):
    return pltpu.roll(value, BLOCK, 1)


def side_by_side(left, right, odd):
    if odd:
        return jnp.where(lane_numbers() < BLOCK, swap_halves(left), right)
    return jnp.where(lane_numbers() < BLOCK, left, swap_halves(right))


def pick_pairs(tile, steps, index, deriv):
    low = [part & 7 for part in index]
    high = [part >> 3 for part in index]
    pair = [[None, None] for k in range(3)]
    for x in range(2):
        picked = {}
        for r in range(steps):
            hit = [part == r for part in high]
            for b in range(4):
                for g in range(2):
                    rows = tile(r, x, b, g)
                    for half in range(2):
                        got = jnp.take_along_axis(rows, low[half], axis=0)
                        before = picked.get((b, g, half), 0.0)
                        picked[b, g, half] = jnp.where(hit[half], got, before)
        for (b, g, half), value in picked.items():
            for k in range(3):
                term = value * deriv(k, x, b, g, half)
                if pair[k][half] is None:
                    pair[k][half] = term
                else:
                    pair[k][half] = pair[k][half] - term if x else pair[k][half] + term
    return pair


def tiles(gram_ref, column, size):
    def tile(r, x, b, g):
        block, part = divmod(r, size // 8)
        row = ((block * 2 + x) * 4 + b) * size + part * 8
        return gram_ref[row : row + 8, column + g * LANES : column + (g + 1) * LANES]

    return tile


def fold(pair):
    return [[value + swap_halves(value) for value in parts] for parts in pair]


def merge(even, odd):
    left = lane_numbers() < BLOCK
    return [[jnp.where(left, even[k][half], odd[k][half]) for half in range(2)] for k in range(3)]


def slot_sum(pair):
    return [jnp.sum(pair[k][0] + pair[k][1], axis=0, keepdims=True) for k in range(3)]


def slot_map(index_ref, base, first=0):
    target = lax.broadcasted_iota(jnp.int32, (8, LANES), 0) + base
    slot = jnp.full((8, LANES), 16, jnp.int32)
    for n in range(16):
        hit = jnp.broadcast_to(index_ref[n : n + 1, :], (8, LANES)) == target
        slot = jnp.where(hit, n, slot)
    return jnp.where(target < first, 16, slot) if first else slot


def spread(slot, pair, spread_ref, rows):
    for r in range(rows // 8):
        slots = slot(r)
        low = slots & 7
        for k in range(3):
            first = jnp.take_along_axis(pair[k][0], low, axis=0)
            second = jnp.take_along_axis(pair[k][1], low, axis=0)
            value = jnp.where(slots < 8, first, jnp.where(slots < 16, second, 0.0))
            spread_ref[k, 8 * r : 8 * r + 8, :] = value
    ones = jnp.ones((8, LANES), jnp.float32)
    out = []
    for k in range(3):
        total = lax.dot_general(
            ones,
            spread_ref[k, :rows, :],
            (((1,), (1,)), ((), ())),
            precision=lax.Precision.HIGHEST,
            preferred_element_type=jnp.float32,
        )
        out.append(total[:1])
    return out


def deriv_at(k, x, b, g, half):
    return (((k * 2 + x) * 4 + b) * 2 + g) * 2 + half


def block_index(index_ref, odd):
    return [
        side_by_side(index_ref[8 * half : 8 * half + 8, :], index_ref[8 * half : 8 * half + 8, :], odd)
        for half in range(2)
    ]


def inner_kernel(
    start_ref, coeffs_ref, occup_ref, energies_ref, nbr_ref, dham_ref, dovl_ref,
    own_high_ref, own_low_ref, near1_high_ref, near1_low_ref, near3_high_ref, near3_low_ref,
    force_ref, deriv_ref, slot_ref,
    near0_high_ref, near0_low_ref, near2_high_ref, near2_low_ref,
    gram0_ref, gram1_ref, gram2_ref, index_ref, spread_ref, columns_ref, copy_sem,
):
    states = coeffs_ref.shape[1]
    count = states // LANES
    near = [
        (near0_high_ref, near0_low_ref),
        (near1_high_ref, near1_low_ref),
        (near2_high_ref, near2_low_ref),
        (near3_high_ref, near3_low_ref),
    ]
    grams = [gram0_ref, gram1_ref, gram2_ref]
    copies = [
        pltpu.make_async_copy(
            coeffs_ref.at[:, c * LANES : (c + 1) * LANES], columns_ref.at[c], copy_sem.at[c]
        )
        for c in range(count)
    ]
    for copy in copies:
        copy.start()
    occup = occup_ref[...]
    weights = [occup, occup * energies_ref[...]]

    for tile in range(2):
        index_ref[tile] = nbr_ref[:, tile * LANES : (tile + 1) * LANES] - (start_ref[0] + tile * LANES)
    for h in range(4):
        lanes = slice(h // 2 * LANES, (h // 2 + 1) * LANES)
        for x, ref in enumerate((dham_ref, dovl_ref)):
            for k in range(3):
                for b in range(4):
                    for g in range(2):
                        for half in range(2):
                            parts = [
                                ref[k * 16 + (2 * g + parity) * 4 + b, 8 * half : 8 * half + 8, lanes]
                                for parity in range(2)
                            ]
                            at = deriv_at(k, x, b, g, half)
                            deriv_ref[h, at] = side_by_side(parts[0], parts[1], h % 2)
    for r in range(32):
        slot_ref[r] = slot_map(index_ref.at[0], 8 * r)
    lower = LANES - UPPER
    for r in range(16 + lower // 8):
        slot_ref[32 + r] = slot_map(index_ref.at[1], 8 * r)
    slot_ref[48 + lower // 8] = slot_map(index_ref.at[1], LANES + lower - 8, LANES + lower // 8 * 8)
    for c, copy in enumerate(copies):
        copy.wait()
        lanes = slice(c * LANES, (c + 1) * LANES)
        for j in range(4):
            for a in range(4):
                rows = columns_ref[c, pl.ds(j * 256 + a, BLOCK, stride=4), :]
                own = slice(j * 256 + a * BLOCK, j * 256 + (a + 1) * BLOCK)
                own_high_ref[own, lanes], own_low_ref[own, lanes] = split(rows)
                for x in range(2):
                    at = slice(x * 256 + a * BLOCK, x * 256 + (a + 1) * BLOCK)
                    near[j][0][at, lanes], near[j][1][at, lanes] = split(rows * weights[x][:, lanes])

    def multiply(h):
        own = slice(h * 256, h * 256 + 256)
        for j in range(h, min(h + 3, 4)):
            grams[h][(j - h) * 512 : (j - h) * 512 + 512, :] = gram(
                near[j][0][...], near[j][1][...], own_high_ref[own, :], own_low_ref[own, :]
            )

    def pick(h):
        index = [part - BLOCK * (h % 2) for part in block_index(index_ref.at[h // 2], h % 2)]
        steps = (min(h + 3, 4) - h) * BLOCK // 8
        return fold(
            pick_pairs(tiles(grams[h], 0, BLOCK), steps, index, lambda *key: deriv_ref[h, deriv_at(*key)])
        )

    def finish(tile, even, odd):
        pair = merge(even, odd)
        mine = slot_sum(pair)
        theirs = spread(lambda r: slot_ref[32 * tile + r], pair, spread_ref, 256 - tile * LANES)
        return mine, theirs

    for h in (2, 1, 0):
        multiply(h)
    nothing = [[jnp.zeros((8, LANES), jnp.float32)] * 2] * 3
    mine1, theirs1 = finish(1, pick(2), nothing)
    pair1 = pick(1)
    pair0 = pick(0)
    mine0, theirs0 = finish(0, pair0, pair1)
    force_ref[...] = jnp.zeros_like(force_ref)
    for k in range(3):
        force_ref[k : k + 1, :LANES] = 2.0 * (theirs0[k][:, :LANES] - mine0[k])
        force_ref[k : k + 1, LANES:] = 2.0 * (theirs0[k][:, LANES:] + theirs1[k] - mine1[k])


def payload_rows(atoms, states):
    groups = -(-48 // (states // LANES))
    return max(4 * (atoms // 2 - UPPER), 4 * BLOCK + 16 * (groups - 3))


def plane_row(plane, count):
    group = plane // count
    return 16 * group if group < 3 else 4 * BLOCK + 16 * (group - 3)


def pack_kernel(
    start_ref, coeffs_ref, nbr_ref, dham_ref, dovl_ref, core_ref, far_ref,
    ham_ref, ovl_ref, last_ref, core_sem, far_sem, deriv_sem,
):
    atoms = nbr_ref.shape[1]
    count, rows, unused = core_ref.shape
    lower = 4 * (atoms // 2 - UPPER)
    first = ((start_ref[0] // atoms) & 1) == 0
    fetched = [
        pltpu.make_async_copy(source.at[:, :, atoms - LANES :], target, deriv_sem.at[at])
        for at, (source, target) in enumerate([(dham_ref, ham_ref), (dovl_ref, ovl_ref)])
    ]
    fetched.append(
        pltpu.make_async_copy(nbr_ref.at[:, atoms - LANES :], last_ref, deriv_sem.at[2])
    )

    def fill(up_ref, up_sem, down_ref, down_sem):
        copies = []
        skip = 4 * (BLOCK - UPPER)
        for c in range(count):
            lanes = slice(c * LANES, (c + 1) * LANES)
            up_rows = coeffs_ref.at[4 * (atoms - UPPER) :, lanes]
            copies.append(pltpu.make_async_copy(up_rows, up_ref.at[c, skip : 4 * BLOCK, :], up_sem.at[c]))
            down_rows = coeffs_ref.at[:lower, lanes]
            copies.append(pltpu.make_async_copy(down_rows, down_ref.at[c, :lower, :], down_sem.at[c]))
        for copy in fetched + copies:
            copy.start()
        if rows > lower:
            down_ref[:, lower:, :] = jnp.zeros((count, rows - lower, LANES), jnp.float32)
        for plane in range(48, -(-48 // count) * count):
            up_ref[plane % count, plane_row(plane, count) : plane_row(plane, count) + 16, :] = jnp.zeros(
                (16, LANES), jnp.float32
            )
        for copy in fetched:
            copy.wait()
        last = last_ref[...]
        target = jnp.where(last >= 0, last - (start_ref[0] + atoms), -1).astype(jnp.float32)
        free = BLOCK - UPPER
        pieces = [
            [
                pltpu.roll(target[8 * half : 8 * half + 8], LANES - BLOCK - (piece + 1) * free, 1)
                for half in range(2)
            ]
            for piece in range(-(-UPPER // free))
        ]
        for x, ref in enumerate((ham_ref, ovl_ref)):
            for k in range(3):
                for g in range(2):
                    for b in range(4):
                        plane = x * 24 + k * 8 + g * 4 + b
                        for half in range(2):
                            parts = [
                                ref[k * 16 + (2 * g + parity) * 4 + b, 8 * half : 8 * half + 8, :]
                                for parity in range(2)
                            ]
                            both = side_by_side(parts[0], parts[1], 1)
                            if plane < len(pieces):
                                both = jnp.where(lane_numbers() < free, pieces[plane][half], both)
                            at = plane_row(plane, count) + 8 * half
                            up_ref[plane % count, at : at + 8, :] = both
        for copy in copies:
            copy.wait()

    @pl.when(first)
    def even():
        fill(core_ref, core_sem, far_ref, far_sem)

    @pl.when(jnp.logical_not(first))
    def odd():
        fill(far_ref, far_sem, core_ref, core_sem)


def cross_kernel(
    parity,
    start_ref, payload_ref, before_ref, occup_ref, energies_ref, nbr_ref, deriv_ref, slot_ref,
    own_high_ref, own_low_ref, near_high_ref, near_low_ref,
    force_ref, sent_ref,
    cut_high_ref, cut_low_ref, gram_ref, index_ref, spread_ref,
):
    atoms = nbr_ref.shape[1]
    count = payload_ref.shape[0]
    lower = atoms // 2 - UPPER
    force_ref[...] = before_ref[...]
    sent_ref[...] = jnp.zeros_like(sent_ref)
    first = ((start_ref[0] // atoms) & 1) == parity

    @pl.when(first)
    def above():
        occup = occup_ref[...]
        weights = [occup, occup * energies_ref[...]]
        size = cut_high_ref.shape[0] // 8
        even = lower // 8 * 8
        for c in range(count):
            lanes = slice(c * LANES, (c + 1) * LANES)
            for b in range(4):
                rows = jnp.concatenate(
                    [
                        payload_ref[c, pl.ds(b, even, stride=4), :],
                        payload_ref[c, pl.ds(4 * (lower - 8) + b, 8, stride=4), :],
                    ],
                    0,
                )
                for x in range(2):
                    at = slice((x * 4 + b) * size, (x * 4 + b + 1) * size)
                    cut_high_ref[at, lanes], cut_low_ref[at, lanes] = split(rows * weights[x][:, lanes])
        gram_ref[...] = gram(
            cut_high_ref[...], cut_low_ref[...], own_high_ref[512:, :], own_low_ref[512:, :]
        )
        target = nbr_ref[:, LANES:] - (start_ref[0] + atoms)
        index_ref[...] = jnp.where(target >= even, target + (size - lower), target)
        pairs = [
            pick_pairs(
                tiles(gram_ref, 256 * h, size),
                (BLOCK, size)[h] // 8,
                block_index(index_ref, h),
                lambda *key: deriv_ref[2 + h, deriv_at(*key)],
            )
            for h in range(2)
        ]
        pair = merge(fold(pairs[0]), fold(pairs[1]))
        mine = slot_sum(pair)
        theirs = spread(lambda r: slot_ref[48 + r], pair, spread_ref, size)
        for k in range(3):
            force_ref[k : k + 1, LANES:] += -2.0 * mine[k]
            sent_ref[k : k + 1, :even] = 2.0 * theirs[k][:, :even]
            sent_ref[k : k + 1, lower - 8 : lower] += 2.0 * theirs[k][:, even:]

    @pl.when(jnp.logical_not(first))
    def below():
        for c in range(count):
            lanes = slice(c * LANES, (c + 1) * LANES)
            for a in range(4):
                at = slice(a * BLOCK, (a + 1) * BLOCK)
                cut_high_ref[at, lanes], cut_low_ref[at, lanes] = split(
                    payload_ref[c, pl.ds(a, BLOCK, stride=4), :]
                )
        gram_ref[:512, :256] = gram(
            near_high_ref[...], near_low_ref[...], cut_high_ref[:256, :], cut_low_ref[:256, :]
        )
        free = BLOCK - UPPER
        lane = lane_numbers()
        for half in range(2):
            target = jnp.zeros((8, LANES), jnp.float32)
            for piece in range(-(-UPPER // free)):
                at = plane_row(piece, count) + 8 * half
                first_lane = (piece + 1) * free
                moved = pltpu.roll(payload_ref[piece % count, at : at + 8, :], first_lane, 1)
                target = jnp.where((lane >= first_lane) & (lane < first_lane + free), moved, target)
            target = side_by_side(target, target, 0).astype(jnp.int32)
            index_ref[8 * half : 8 * half + 8, :] = jnp.where(target >= lower, target - BLOCK, -1)
        index = [index_ref[8 * half : 8 * half + 8, :] for half in range(2)]

        def deriv(k, x, b, g, half):
            plane = x * 24 + k * 8 + g * 4 + b
            at = plane_row(plane, count) + 8 * half
            return payload_ref[plane % count, at : at + 8, :]

        pair = pick_pairs(tiles(gram_ref, 0, BLOCK), BLOCK // 8, index, deriv)
        theirs = spread(lambda r: slot_map(index_ref, 8 * r), pair, spread_ref, BLOCK)
        mine = slot_sum(fold(pair))
        for k in range(3):
            force_ref[k : k + 1, BLOCK:LANES] += 2.0 * theirs[k]
            sent_ref[k : k + 1, atoms - BLOCK :] = -2.0 * mine[k][:, BLOCK:]


def last_kernel(
    start_ref, before_ref, back_ref, nbr_ref, deriv_ref, slot_ref,
    own_high_ref, own_low_ref, near_high_ref, near_low_ref,
    force_ref, gram_ref, index_ref, spread_ref,
):
    gram_ref[...] = gram(
        near_high_ref[...], near_low_ref[...], own_high_ref[768:, :], own_low_ref[768:, :]
    )
    index_ref[...] = nbr_ref[:, LANES:] - (start_ref[0] + LANES)
    index = [part - BLOCK for part in block_index(index_ref, 1)]
    pair = fold(
        pick_pairs(tiles(gram_ref, 0, BLOCK), BLOCK // 8, index, lambda *key: deriv_ref[3, deriv_at(*key)])
    )
    nothing = [[jnp.zeros((8, LANES), jnp.float32)] * 2] * 3
    pair = merge(nothing, pair)
    mine = slot_sum(pair)
    theirs = spread(lambda r: slot_ref[40 + r], pair, spread_ref, BLOCK)
    force_ref[...] = before_ref[...] + back_ref[...]
    for k in range(3):
        force_ref[k : k + 1, LANES:] += -2.0 * mine[k]
        force_ref[k : k + 1, LANES + BLOCK :] += 2.0 * theirs[k]


def in_hbm(value):
    return pltpu.with_memory_space_constraint(value, pltpu.HBM)


def core_swap(value):
    return lax.ppermute(value, "sub", [(0, 1), (1, 0)])


def shard_swap(value):
    count = lax.axis_size(SHARD)
    pairs = [pair for at in range(1, count - 1, 2) for pair in ((at, at + 1), (at + 1, at))]
    return lax.ppermute(value, SHARD, pairs)


def local(coeffs, occup, energies, nbr, dham, dovl):
    slots, atoms = nbr.shape
    states = coeffs.shape[1]
    start = (lax.axis_index(SHARD) * atoms).reshape(1).astype(jnp.int32)
    occup = occup.reshape(1, states)
    energies = energies.reshape(1, states)
    count = states // LANES

    vmem = pl.BlockSpec(memory_space=pltpu.VMEM)
    hbm = pl.BlockSpec(memory_space=pltpu.HBM)
    smem = pl.BlockSpec(memory_space=pltpu.SMEM)
    half = jax.ShapeDtypeStruct((512, states), jnp.bfloat16)
    whole = jax.ShapeDtypeStruct((4 * atoms, states), jnp.bfloat16)
    force = jax.ShapeDtypeStruct((8, atoms), jnp.float32)
    prepared = pltpu.VMEM((512, states), jnp.bfloat16)
    padded = -(-(atoms // 2 - UPPER) // 16) * 16
    payload = jax.ShapeDtypeStruct((count, payload_rows(atoms, states), LANES), jnp.float32)
    core_payload, far_payload = pl.pallas_call(
        pack_kernel,
        out_shape=(payload, payload),
        in_specs=[smem] + [hbm] * 4,
        out_specs=(vmem, vmem),
        scratch_shapes=[
            pltpu.VMEM((48, slots, LANES), jnp.float32),
            pltpu.VMEM((48, slots, LANES), jnp.float32),
            pltpu.VMEM((slots, LANES), jnp.int32),
            pltpu.SemaphoreType.DMA((count,)),
            pltpu.SemaphoreType.DMA((count,)),
            pltpu.SemaphoreType.DMA((3,)),
        ],
        compiler_params=pltpu.CompilerParams(vmem_limit_bytes=12 * 1024 * 1024),
        name="pack",
    )(start, *(in_hbm(value) for value in (coeffs, nbr, dham, dovl)))
    far_payload = shard_swap(far_payload)
    core_payload = core_swap(core_payload)
    own_high, own_low, near_high, near_low, last_high, last_low, inner, derivs, slot_maps = pl.pallas_call(
        inner_kernel,
        out_shape=(
            whole, whole, half, half, half, half, force,
            jax.ShapeDtypeStruct((4, 96, 8, LANES), jnp.float32),
            jax.ShapeDtypeStruct((64 - UPPER // 8, 8, LANES), jnp.int32),
        ),
        in_specs=[smem, hbm] + [vmem] * 5,
        out_specs=(vmem,) * 9,
        scratch_shapes=[prepared] * 4
        + [pltpu.VMEM((512 * n, 256), jnp.float32) for n in (3, 3, 2)]
        + [
            pltpu.VMEM((2, slots, LANES), jnp.int32),
            pltpu.VMEM((3, atoms, LANES), jnp.float32),
            pltpu.VMEM((states // LANES, 4 * atoms, LANES), jnp.float32),
            pltpu.SemaphoreType.DMA((count,)),
        ],
        compiler_params=pltpu.CompilerParams(vmem_limit_bytes=32 * 1024 * 1024),
        cost_estimate=pl.CostEstimate(
            flops=3 * 2 * 8 * 512 * 256 * states, bytes_accessed=16 * 1024 * 1024, transcendentals=0
        ),
        name="inner_pairs",
    )(start, in_hbm(coeffs), occup, energies, nbr, dham, dovl)

    def cross(parity, payload, before, name):
        cut = pltpu.VMEM((8 * padded, states), jnp.bfloat16)
        return pl.pallas_call(
            functools.partial(cross_kernel, parity),
            out_shape=(force, force),
            in_specs=[smem] + [vmem] * 11,
            out_specs=(vmem, vmem),
            scratch_shapes=[
                cut,
                cut,
                pltpu.VMEM((8 * padded, 512), jnp.float32),
                pltpu.VMEM((slots, LANES), jnp.int32),
                pltpu.VMEM((3, padded, LANES), jnp.float32),
            ],
            compiler_params=pltpu.CompilerParams(vmem_limit_bytes=20 * 1024 * 1024),
            cost_estimate=pl.CostEstimate(
                flops=3 * 2 * 2 * 512 * 256 * states, bytes_accessed=6 * 1024 * 1024, transcendentals=0
            ),
            name=name,
        )(start, payload, before, occup, energies, nbr, derivs, slot_maps, own_high, own_low, near_high, near_low)

    total, core_sent = cross(0, core_payload, inner, "core_pairs")
    core_back = core_swap(core_sent)
    total, far_sent = cross(1, far_payload, total, "far_pairs")
    far_back = shard_swap(far_sent)
    total = pl.pallas_call(
        last_kernel,
        out_shape=force,
        in_specs=[smem] + [vmem] * 9,
        out_specs=vmem,
        scratch_shapes=[
            pltpu.VMEM((512, 256), jnp.float32),
            pltpu.VMEM((slots, LANES), jnp.int32),
            pltpu.VMEM((3, BLOCK, LANES), jnp.float32),
        ],
        compiler_params=pltpu.CompilerParams(vmem_limit_bytes=12 * 1024 * 1024),
        cost_estimate=pl.CostEstimate(
            flops=3 * 2 * 512 * 256 * states, bytes_accessed=0, transcendentals=0
        ),
        name="last_pairs",
    )(start, total, core_back, nbr, derivs, slot_maps, own_high, own_low, last_high, last_low)
    total = (total + far_back)[:3]
    if lax.axis_size("states") == 2:
        return total + lax.ppermute(total, "states", [(0, 1), (1, 0)])
    return lax.psum(total, "states")


def solution(mesh):
    in_specs = (
        P(("groups", "atoms", "sub"), "states"),
        P(("groups", "states")),
        P(("groups", "states")),
        P(None, ("groups", "atoms", "sub")),
        P(None, None, ("groups", "atoms", "sub")),
        P(None, None, ("groups", "atoms", "sub")),
    )
    out_specs = P(None, ("groups", "atoms", "sub"))
    return jax.shard_map(local, mesh=mesh, in_specs=in_specs, out_specs=out_specs, check_vma=False)
```

```python
import functools

import jax
import jax.numpy as jnp
from jax import lax
from jax.experimental import pallas as pl
from jax.experimental.pallas import tpu as pltpu
from jax.sharding import PartitionSpec as P

LANES = 128
BLOCK = 64
UPPER = 52
SHARD = ("atoms", "sub")


def split(value):
    high = value.astype(jnp.bfloat16)
    return high, (value - high.astype(jnp.float32)).astype(jnp.bfloat16)


def gram(left_high, left_low, right_high, right_low):
    dot = functools.partial(
        lax.dot_general,
        dimension_numbers=(((1,), (1,)), ((), ())),
        preferred_element_type=jnp.float32,
    )
    return (
        dot(left_high, right_high) + dot(left_high, right_low) + dot(left_low, right_high)
    )


def lane_numbers():
    return lax.broadcasted_iota(jnp.int32, (8, LANES), 1)


def swap_halves(value):
    return pltpu.roll(value, BLOCK, 1)


def side_by_side(left, right, odd):
    if odd:
        return jnp.where(lane_numbers() < BLOCK, swap_halves(left), right)
    return jnp.where(lane_numbers() < BLOCK, left, swap_halves(right))


def pick_pairs(tile, steps, index, deriv):
    low = [part & 7 for part in index]
    high = [part >> 3 for part in index]
    pair = [[None, None] for k in range(3)]
    for x in range(2):
        picked = {}
        for r in range(steps):
            hit = [part == r for part in high]
            for b in range(4):
                for g in range(2):
                    rows = tile(r, x, b, g)
                    for half in range(2):
                        got = jnp.take_along_axis(rows, low[half], axis=0)
                        before = picked.get((b, g, half), 0.0)
                        picked[b, g, half] = jnp.where(hit[half], got, before)
        for (b, g, half), value in picked.items():
            for k in range(3):
                term = value * deriv(k, x, b, g, half)
                if pair[k][half] is None:
                    pair[k][half] = term
                else:
                    pair[k][half] = pair[k][half] - term if x else pair[k][half] + term
    return pair


def tiles(gram_ref, column, size):
    def tile(r, x, b, g):
        block, part = divmod(r, size // 8)
        row = ((block * 2 + x) * 4 + b) * size + part * 8
        return gram_ref[row : row + 8, column + g * LANES : column + (g + 1) * LANES]

    return tile


def fold(pair):
    return [[value + swap_halves(value) for value in parts] for parts in pair]


def merge(even, odd):
    left = lane_numbers() < BLOCK
    return [[jnp.where(left, even[k][half], odd[k][half]) for half in range(2)] for k in range(3)]


def slot_sum(pair):
    return [jnp.sum(pair[k][0] + pair[k][1], axis=0, keepdims=True) for k in range(3)]


def slot_map(index_ref, base, first=0):
    target = lax.broadcasted_iota(jnp.int32, (8, LANES), 0) + base
    slot = jnp.full((8, LANES), 16, jnp.int32)
    for n in range(16):
        hit = jnp.broadcast_to(index_ref[n : n + 1, :], (8, LANES)) == target
        slot = jnp.where(hit, n, slot)
    return jnp.where(target < first, 16, slot) if first else slot


def spread(slot, pair, spread_ref, rows):
    for r in range(rows // 8):
        slots = slot(r)
        low = slots & 7
        for k in range(3):
            first = jnp.take_along_axis(pair[k][0], low, axis=0)
            second = jnp.take_along_axis(pair[k][1], low, axis=0)
            value = jnp.where(slots < 8, first, jnp.where(slots < 16, second, 0.0))
            spread_ref[k, 8 * r : 8 * r + 8, :] = value
    ones = jnp.ones((8, LANES), jnp.float32)
    out = []
    for k in range(3):
        total = lax.dot_general(
            ones,
            spread_ref[k, :rows, :],
            (((1,), (1,)), ((), ())),
            precision=lax.Precision.HIGHEST,
            preferred_element_type=jnp.float32,
        )
        out.append(total[:1])
    return out


def deriv_at(k, x, b, g, half):
    return (((k * 2 + x) * 4 + b) * 2 + g) * 2 + half


def block_index(index_ref, odd):
    return [
        side_by_side(index_ref[8 * half : 8 * half + 8, :], index_ref[8 * half : 8 * half + 8, :], odd)
        for half in range(2)
    ]


def inner_kernel(
    start_ref, coeffs_ref, occup_ref, energies_ref, nbr_ref, dham_ref, dovl_ref,
    own_high_ref, own_low_ref, near1_high_ref, near1_low_ref, near3_high_ref, near3_low_ref,
    force_ref, deriv_ref, slot_ref,
    near0_high_ref, near0_low_ref, near2_high_ref, near2_low_ref,
    gram0_ref, gram1_ref, gram2_ref, index_ref, spread_ref, columns_ref, copy_sem,
):
    states = coeffs_ref.shape[1]
    count = states // LANES
    near = [
        (near0_high_ref, near0_low_ref),
        (near1_high_ref, near1_low_ref),
        (near2_high_ref, near2_low_ref),
        (near3_high_ref, near3_low_ref),
    ]
    grams = [gram0_ref, gram1_ref, gram2_ref]
    copies = [
        pltpu.make_async_copy(
            coeffs_ref.at[:, c * LANES : (c + 1) * LANES], columns_ref.at[c], copy_sem.at[c]
        )
        for c in range(count)
    ]
    for copy in copies:
        copy.start()
    occup = occup_ref[...]
    weights = [occup, occup * energies_ref[...]]

    for tile in range(2):
        index_ref[tile] = nbr_ref[:, tile * LANES : (tile + 1) * LANES] - (start_ref[0] + tile * LANES)
    for h in range(4):
        lanes = slice(h // 2 * LANES, (h // 2 + 1) * LANES)
        for x, ref in enumerate((dham_ref, dovl_ref)):
            for k in range(3):
                for b in range(4):
                    for g in range(2):
                        for half in range(2):
                            parts = [
                                ref[k * 16 + (2 * g + parity) * 4 + b, 8 * half : 8 * half + 8, lanes]
                                for parity in range(2)
                            ]
                            at = deriv_at(k, x, b, g, half)
                            deriv_ref[h, at] = side_by_side(parts[0], parts[1], h % 2)
    for r in range(32):
        slot_ref[r] = slot_map(index_ref.at[0], 8 * r)
    lower = LANES - UPPER
    for r in range(16 + lower // 8):
        slot_ref[32 + r] = slot_map(index_ref.at[1], 8 * r)
    slot_ref[48 + lower // 8] = slot_map(index_ref.at[1], LANES + lower - 8, LANES + lower // 8 * 8)
    for c, copy in enumerate(copies):
        copy.wait()
        lanes = slice(c * LANES, (c + 1) * LANES)
        for j in range(4):
            for a in range(4):
                rows = columns_ref[c, pl.ds(j * 256 + a, BLOCK, stride=4), :]
                own = slice(j * 256 + a * BLOCK, j * 256 + (a + 1) * BLOCK)
                own_high_ref[own, lanes], own_low_ref[own, lanes] = split(rows)
                for x in range(2):
                    at = slice(x * 256 + a * BLOCK, x * 256 + (a + 1) * BLOCK)
                    near[j][0][at, lanes], near[j][1][at, lanes] = split(rows * weights[x][:, lanes])

    def multiply(h):
        own = slice(h * 256, h * 256 + 256)
        for j in range(h, min(h + 3, 4)):
            grams[h][(j - h) * 512 : (j - h) * 512 + 512, :] = gram(
                near[j][0][...], near[j][1][...], own_high_ref[own, :], own_low_ref[own, :]
            )

    def pick(h):
        index = [part - BLOCK * (h % 2) for part in block_index(index_ref.at[h // 2], h % 2)]
        steps = (min(h + 3, 4) - h) * BLOCK // 8
        return fold(
            pick_pairs(tiles(grams[h], 0, BLOCK), steps, index, lambda *key: deriv_ref[h, deriv_at(*key)])
        )

    def finish(tile, even, odd):
        pair = merge(even, odd)
        mine = slot_sum(pair)
        theirs = spread(lambda r: slot_ref[32 * tile + r], pair, spread_ref, 256 - tile * LANES)
        return mine, theirs

    for h in (2, 1, 0):
        multiply(h)
    nothing = [[jnp.zeros((8, LANES), jnp.float32)] * 2] * 3
    mine1, theirs1 = finish(1, pick(2), nothing)
    pair1 = pick(1)
    pair0 = pick(0)
    mine0, theirs0 = finish(0, pair0, pair1)
    force_ref[...] = jnp.zeros_like(force_ref)
    for k in range(3):
        force_ref[k : k + 1, :LANES] = 2.0 * (theirs0[k][:, :LANES] - mine0[k])
        force_ref[k : k + 1, LANES:] = 2.0 * (theirs0[k][:, LANES:] + theirs1[k] - mine1[k])


def payload_rows(atoms, states):
    groups = -(-48 // (states // LANES))
    return max(4 * (atoms // 2 - UPPER), 4 * BLOCK + 16 * (groups - 3))


def plane_row(plane, count):
    group = plane // count
    return 16 * group if group < 3 else 4 * BLOCK + 16 * (group - 3)


def pack_kernel(
    start_ref, coeffs_ref, nbr_ref, dham_ref, dovl_ref, core_ref, far_ref,
    ham_ref, ovl_ref, last_ref, core_sem, far_sem, deriv_sem,
):
    atoms = nbr_ref.shape[1]
    count, rows, unused = core_ref.shape
    lower = 4 * (atoms // 2 - UPPER)
    first = ((start_ref[0] // atoms) & 1) == 0
    fetched = [
        pltpu.make_async_copy(source.at[:, :, atoms - LANES :], target, deriv_sem.at[at])
        for at, (source, target) in enumerate([(dham_ref, ham_ref), (dovl_ref, ovl_ref)])
    ]
    fetched.append(
        pltpu.make_async_copy(nbr_ref.at[:, atoms - LANES :], last_ref, deriv_sem.at[2])
    )

    def fill(up_ref, up_sem, down_ref, down_sem):
        copies = []
        skip = 4 * (BLOCK - UPPER)
        for c in range(count):
            lanes = slice(c * LANES, (c + 1) * LANES)
            up_rows = coeffs_ref.at[4 * (atoms - UPPER) :, lanes]
            copies.append(pltpu.make_async_copy(up_rows, up_ref.at[c, skip : 4 * BLOCK, :], up_sem.at[c]))
            down_rows = coeffs_ref.at[:lower, lanes]
            copies.append(pltpu.make_async_copy(down_rows, down_ref.at[c, :lower, :], down_sem.at[c]))
        for copy in fetched + copies:
            copy.start()
        if rows > lower:
            down_ref[:, lower:, :] = jnp.zeros((count, rows - lower, LANES), jnp.float32)
        for plane in range(48, -(-48 // count) * count):
            up_ref[plane % count, plane_row(plane, count) : plane_row(plane, count) + 16, :] = jnp.zeros(
                (16, LANES), jnp.float32
            )
        for copy in fetched:
            copy.wait()
        last = last_ref[...]
        target = jnp.where(last >= 0, last - (start_ref[0] + atoms), -1).astype(jnp.float32)
        free = BLOCK - UPPER
        pieces = [
            [
                pltpu.roll(target[8 * half : 8 * half + 8], LANES - BLOCK - (piece + 1) * free, 1)
                for half in range(2)
            ]
            for piece in range(-(-UPPER // free))
        ]
        for x, ref in enumerate((ham_ref, ovl_ref)):
            for k in range(3):
                for g in range(2):
                    for b in range(4):
                        plane = x * 24 + k * 8 + g * 4 + b
                        for half in range(2):
                            parts = [
                                ref[k * 16 + (2 * g + parity) * 4 + b, 8 * half : 8 * half + 8, :]
                                for parity in range(2)
                            ]
                            both = side_by_side(parts[0], parts[1], 1)
                            if plane < len(pieces):
                                both = jnp.where(lane_numbers() < free, pieces[plane][half], both)
                            at = plane_row(plane, count) + 8 * half
                            up_ref[plane % count, at : at + 8, :] = both
        for copy in copies:
            copy.wait()

    @pl.when(first)
    def even():
        fill(core_ref, core_sem, far_ref, far_sem)

    @pl.when(jnp.logical_not(first))
    def odd():
        fill(far_ref, far_sem, core_ref, core_sem)


def cross_kernel(
    parity,
    start_ref, payload_ref, before_ref, occup_ref, energies_ref, nbr_ref, deriv_ref, slot_ref,
    own_high_ref, own_low_ref, near_high_ref, near_low_ref,
    force_ref, sent_ref,
    cut_high_ref, cut_low_ref, gram_ref, index_ref, spread_ref,
):
    atoms = nbr_ref.shape[1]
    count = payload_ref.shape[0]
    lower = atoms // 2 - UPPER
    force_ref[...] = before_ref[...]
    sent_ref[...] = jnp.zeros_like(sent_ref)
    first = ((start_ref[0] // atoms) & 1) == parity

    @pl.when(first)
    def above():
        occup = occup_ref[...]
        weights = [occup, occup * energies_ref[...]]
        size = cut_high_ref.shape[0] // 8
        extra = size - BLOCK
        even = lower // 8 * 8
        for c in range(count):
            lanes = slice(c * LANES, (c + 1) * LANES)
            for b in range(4):
                rows = jnp.concatenate(
                    [
                        payload_ref[c, pl.ds(b, even, stride=4), :],
                        payload_ref[c, pl.ds(4 * (lower - 8) + b, 8, stride=4), :],
                    ],
                    0,
                )
                for x in range(2):
                    high, low = split(rows * weights[x][:, lanes])
                    at = slice((x * 4 + b) * BLOCK, (x * 4 + b + 1) * BLOCK)
                    cut_high_ref[at, lanes], cut_low_ref[at, lanes] = high[:BLOCK], low[:BLOCK]
                    at = slice(512 + (x * 4 + b) * extra, 512 + (x * 4 + b + 1) * extra)
                    cut_high_ref[at, lanes], cut_low_ref[at, lanes] = high[BLOCK:], low[BLOCK:]
        gram_ref[:, 256:] = gram(
            cut_high_ref[...], cut_low_ref[...], own_high_ref[768:, :], own_low_ref[768:, :]
        )
        gram_ref[:512, :256] = gram(
            cut_high_ref[:512, :], cut_low_ref[:512, :], own_high_ref[512:768, :], own_low_ref[512:768, :]
        )
        first_tile = tiles(gram_ref, 256, BLOCK)
        extra_tile = tiles(gram_ref.at[512:, :], 256, extra)

        def odd_tile(r, *key):
            return first_tile(r, *key) if r < BLOCK // 8 else extra_tile(r - BLOCK // 8, *key)

        target = nbr_ref[:, LANES:] - (start_ref[0] + atoms)
        index_ref[...] = jnp.where(target >= even, target + (size - lower), target)
        pairs = [
            pick_pairs(
                (tiles(gram_ref, 0, BLOCK), odd_tile)[h],
                (BLOCK, size)[h] // 8,
                block_index(index_ref, h),
                lambda *key: deriv_ref[2 + h, deriv_at(*key)],
            )
            for h in range(2)
        ]
        pair = merge(fold(pairs[0]), fold(pairs[1]))
        mine = slot_sum(pair)
        theirs = spread(lambda r: slot_ref[48 + r], pair, spread_ref, size)
        for k in range(3):
            force_ref[k : k + 1, LANES:] += -2.0 * mine[k]
            sent_ref[k : k + 1, :even] = 2.0 * theirs[k][:, :even]
            sent_ref[k : k + 1, lower - 8 : lower] += 2.0 * theirs[k][:, even:]

    @pl.when(jnp.logical_not(first))
    def below():
        for c in range(count):
            lanes = slice(c * LANES, (c + 1) * LANES)
            for a in range(4):
                at = slice(a * BLOCK, (a + 1) * BLOCK)
                cut_high_ref[at, lanes], cut_low_ref[at, lanes] = split(
                    payload_ref[c, pl.ds(a, BLOCK, stride=4), :]
                )
        gram_ref[:512, :256] = gram(
            near_high_ref[...], near_low_ref[...], cut_high_ref[:256, :], cut_low_ref[:256, :]
        )
        free = BLOCK - UPPER
        lane = lane_numbers()
        for half in range(2):
            target = jnp.zeros((8, LANES), jnp.float32)
            for piece in range(-(-UPPER // free)):
                at = plane_row(piece, count) + 8 * half
                first_lane = (piece + 1) * free
                moved = pltpu.roll(payload_ref[piece % count, at : at + 8, :], first_lane, 1)
                target = jnp.where((lane >= first_lane) & (lane < first_lane + free), moved, target)
            target = side_by_side(target, target, 0).astype(jnp.int32)
            index_ref[8 * half : 8 * half + 8, :] = jnp.where(target >= lower, target - BLOCK, -1)
        index = [index_ref[8 * half : 8 * half + 8, :] for half in range(2)]

        def deriv(k, x, b, g, half):
            plane = x * 24 + k * 8 + g * 4 + b
            at = plane_row(plane, count) + 8 * half
            return payload_ref[plane % count, at : at + 8, :]

        pair = pick_pairs(tiles(gram_ref, 0, BLOCK), BLOCK // 8, index, deriv)
        theirs = spread(lambda r: slot_map(index_ref, 8 * r), pair, spread_ref, BLOCK)
        mine = slot_sum(fold(pair))
        for k in range(3):
            force_ref[k : k + 1, BLOCK:LANES] += 2.0 * theirs[k]
            sent_ref[k : k + 1, atoms - BLOCK :] = -2.0 * mine[k][:, BLOCK:]


def last_kernel(
    start_ref, before_ref, back_ref, nbr_ref, deriv_ref, slot_ref,
    own_high_ref, own_low_ref, near_high_ref, near_low_ref,
    force_ref, gram_ref, index_ref, spread_ref,
):
    gram_ref[...] = gram(
        near_high_ref[...], near_low_ref[...], own_high_ref[768:, :], own_low_ref[768:, :]
    )
    index_ref[...] = nbr_ref[:, LANES:] - (start_ref[0] + LANES)
    index = [part - BLOCK for part in block_index(index_ref, 1)]
    pair = fold(
        pick_pairs(tiles(gram_ref, 0, BLOCK), BLOCK // 8, index, lambda *key: deriv_ref[3, deriv_at(*key)])
    )
    nothing = [[jnp.zeros((8, LANES), jnp.float32)] * 2] * 3
    pair = merge(nothing, pair)
    mine = slot_sum(pair)
    theirs = spread(lambda r: slot_ref[40 + r], pair, spread_ref, BLOCK)
    force_ref[...] = before_ref[...] + back_ref[...]
    for k in range(3):
        force_ref[k : k + 1, LANES:] += -2.0 * mine[k]
        force_ref[k : k + 1, LANES + BLOCK :] += 2.0 * theirs[k]


def in_hbm(value):
    return pltpu.with_memory_space_constraint(value, pltpu.HBM)


def core_swap(value):
    return lax.ppermute(value, "sub", [(0, 1), (1, 0)])


def shard_swap(value):
    count = lax.axis_size(SHARD)
    pairs = [pair for at in range(1, count - 1, 2) for pair in ((at, at + 1), (at + 1, at))]
    return lax.ppermute(value, SHARD, pairs)


def local(coeffs, occup, energies, nbr, dham, dovl):
    slots, atoms = nbr.shape
    states = coeffs.shape[1]
    start = (lax.axis_index(SHARD) * atoms).reshape(1).astype(jnp.int32)
    occup = occup.reshape(1, states)
    energies = energies.reshape(1, states)
    count = states // LANES

    vmem = pl.BlockSpec(memory_space=pltpu.VMEM)
    hbm = pl.BlockSpec(memory_space=pltpu.HBM)
    smem = pl.BlockSpec(memory_space=pltpu.SMEM)
    half = jax.ShapeDtypeStruct((512, states), jnp.bfloat16)
    whole = jax.ShapeDtypeStruct((4 * atoms, states), jnp.bfloat16)
    force = jax.ShapeDtypeStruct((8, atoms), jnp.float32)
    prepared = pltpu.VMEM((512, states), jnp.bfloat16)
    padded = -(-(atoms // 2 - UPPER) // 16) * 16
    payload = jax.ShapeDtypeStruct((count, payload_rows(atoms, states), LANES), jnp.float32)
    core_payload, far_payload = pl.pallas_call(
        pack_kernel,
        out_shape=(payload, payload),
        in_specs=[smem] + [hbm] * 4,
        out_specs=(vmem, vmem),
        scratch_shapes=[
            pltpu.VMEM((48, slots, LANES), jnp.float32),
            pltpu.VMEM((48, slots, LANES), jnp.float32),
            pltpu.VMEM((slots, LANES), jnp.int32),
            pltpu.SemaphoreType.DMA((count,)),
            pltpu.SemaphoreType.DMA((count,)),
            pltpu.SemaphoreType.DMA((3,)),
        ],
        compiler_params=pltpu.CompilerParams(vmem_limit_bytes=12 * 1024 * 1024),
        name="pack",
    )(start, *(in_hbm(value) for value in (coeffs, nbr, dham, dovl)))
    far_payload = shard_swap(far_payload)
    core_payload = core_swap(core_payload)
    own_high, own_low, near_high, near_low, last_high, last_low, inner, derivs, slot_maps = pl.pallas_call(
        inner_kernel,
        out_shape=(
            whole, whole, half, half, half, half, force,
            jax.ShapeDtypeStruct((4, 96, 8, LANES), jnp.float32),
            jax.ShapeDtypeStruct((64 - UPPER // 8, 8, LANES), jnp.int32),
        ),
        in_specs=[smem, hbm] + [vmem] * 5,
        out_specs=(vmem,) * 9,
        scratch_shapes=[prepared] * 4
        + [pltpu.VMEM((512 * n, 256), jnp.float32) for n in (3, 3, 2)]
        + [
            pltpu.VMEM((2, slots, LANES), jnp.int32),
            pltpu.VMEM((3, atoms, LANES), jnp.float32),
            pltpu.VMEM((states // LANES, 4 * atoms, LANES), jnp.float32),
            pltpu.SemaphoreType.DMA((count,)),
        ],
        compiler_params=pltpu.CompilerParams(vmem_limit_bytes=32 * 1024 * 1024),
        cost_estimate=pl.CostEstimate(
            flops=3 * 2 * 8 * 512 * 256 * states, bytes_accessed=16 * 1024 * 1024, transcendentals=0
        ),
        name="inner_pairs",
    )(start, in_hbm(coeffs), occup, energies, nbr, dham, dovl)

    def cross(parity, payload, before, name):
        cut = pltpu.VMEM((8 * padded, states), jnp.bfloat16)
        return pl.pallas_call(
            functools.partial(cross_kernel, parity),
            out_shape=(force, force),
            in_specs=[smem] + [vmem] * 11,
            out_specs=(vmem, vmem),
            scratch_shapes=[
                cut,
                cut,
                pltpu.VMEM((8 * padded, 512), jnp.float32),
                pltpu.VMEM((slots, LANES), jnp.int32),
                pltpu.VMEM((3, padded, LANES), jnp.float32),
            ],
            compiler_params=pltpu.CompilerParams(vmem_limit_bytes=20 * 1024 * 1024),
            cost_estimate=pl.CostEstimate(
                flops=3 * 2 * 2 * 512 * 256 * states, bytes_accessed=6 * 1024 * 1024, transcendentals=0
            ),
            name=name,
        )(start, payload, before, occup, energies, nbr, derivs, slot_maps, own_high, own_low, near_high, near_low)

    total, core_sent = cross(0, core_payload, inner, "core_pairs")
    core_back = core_swap(core_sent)
    total, far_sent = cross(1, far_payload, total, "far_pairs")
    far_back = shard_swap(far_sent)
    total = pl.pallas_call(
        last_kernel,
        out_shape=force,
        in_specs=[smem] + [vmem] * 9,
        out_specs=vmem,
        scratch_shapes=[
            pltpu.VMEM((512, 256), jnp.float32),
            pltpu.VMEM((slots, LANES), jnp.int32),
            pltpu.VMEM((3, BLOCK, LANES), jnp.float32),
        ],
        compiler_params=pltpu.CompilerParams(vmem_limit_bytes=12 * 1024 * 1024),
        cost_estimate=pl.CostEstimate(
            flops=3 * 2 * 512 * 256 * states, bytes_accessed=0, transcendentals=0
        ),
        name="last_pairs",
    )(start, total, core_back, nbr, derivs, slot_maps, own_high, own_low, last_high, last_low)
    total = (total + far_back)[:3]
    if lax.axis_size("states") == 2:
        return total + lax.ppermute(total, "states", [(0, 1), (1, 0)])
    return lax.psum(total, "states")


def solution(mesh):
    in_specs = (
        P(("groups", "atoms", "sub"), "states"),
        P(("groups", "states")),
        P(("groups", "states")),
        P(None, ("groups", "atoms", "sub")),
        P(None, None, ("groups", "atoms", "sub")),
        P(None, None, ("groups", "atoms", "sub")),
    )
    out_specs = P(None, ("groups", "atoms", "sub"))
    return jax.shard_map(local, mesh=mesh, in_specs=in_specs, out_specs=out_specs, check_vma=False)
```
